32 devices in a mesh: dp: 4 (over x, core), mp: 8 (over z, y).
Axes of the slice: x: 2, y: 2, z: 4, core: 2. Of those that a mesh axis runs over, the one named last changes fastest.
Arguments:
- block_input: bfloat16 [8, 64, 50176], P(None, 'dp', 'mp'), may hold values from -40 to 40
- norm1_gain: bfloat16 [8, 64], P(None, 'dp'), may hold values from 0.5 to 2
- norm1_bias: bfloat16 [8, 64], P(None, 'dp'), may hold values from -3 to 3
- input_weight: bfloat16 [512, 16, 64], P(None, None, 'dp'), may hold values from -0.25 to 0.25
- input_bias: bfloat16 [16, 64], P(None, 'dp'), may hold values from -3 to 3
- conv_weight: bfloat16 [49, 15, 64], P(None, None, 'dp'), may hold values from -2.5 to 2.5
- conv_bias: bfloat16 [15, 64], P(None, 'dp'), may hold values from -3 to 3
- gate_weight1: bfloat16 [64, 2, 64], P(None, None, 'dp'), may hold values from -0.75 to 0.75
- gate_bias1: bfloat16 [2, 64], P(None, 'dp'), may hold values from -3 to 3
- gate_weight2: bfloat16 [128, 4, 64], P(None, None, 'dp'), may hold values from -0.5 to 0.5
- gate_bias2: bfloat16 [4, 64], P(None, 'dp'), may hold values from -3 to 3
- gate_weight3: bfloat16 [256, 8, 64], P(None, None, 'dp'), may hold values from -0.375 to 0.375
- gate_bias3: bfloat16 [8, 64], P(None, 'dp'), may hold values from -3 to 3
- output_weight: bfloat16 [512, 8, 64], P(None, None, 'dp'), may hold values from -0.25 to 0.25
- output_bias: bfloat16 [8, 64], P(None, 'dp'), may hold values from -3 to 3
- layer_scale1: bfloat16 [8, 64], P(None, 'dp'), may hold values from 0.5 to 2
- norm2_gain: bfloat16 [8, 64], P(None, 'dp'), may hold values from 0.5 to 2
- norm2_bias: bfloat16 [8, 64], P(None, 'dp'), may hold values from -3 to 3
- expand_weight: bfloat16 [512, 32, 64], P(None, None, 'dp'), may hold values from -0.25 to 0.25
- expand_bias: bfloat16 [32, 64], P(None, 'dp'), may hold values from -3 to 3
- reduce_weight: bfloat16 [32, 64, 512], P(None, 'dp'), may hold values from -0.125 to 0.125
- reduce_bias: bfloat16 [8, 64], P(None, 'dp'), may hold values from -3 to 3
- layer_scale2: bfloat16 [8, 64], P(None, 'dp'), may hold values from 0.5 to 2
- cotangent: bfloat16 [8, 64, 50176], P(None, 'dp', 'mp'), may hold values from -6 to 6
Outputs:
- block_output: bfloat16 [8, 64, 50176], P(None, 'dp', 'mp')
- input_grad: bfloat16 [8, 64, 50176], P(None, 'dp', 'mp')
- grad_norm1_gain: float32 [8, 64], P(None, 'dp')
- grad_norm1_bias: float32 [8, 64], P(None, 'dp')
- grad_input_weight: float32 [512, 16, 64], P(None, None, 'dp')
- grad_input_bias: float32 [16, 64], P(None, 'dp')
- grad_conv_weight: float32 [49, 15, 64], P(None, None, 'dp')
- grad_conv_bias: float32 [15, 64], P(None, 'dp')
- grad_gate_weight1: float32 [64, 2, 64], P(None, None, 'dp')
- grad_gate_bias1: float32 [2, 64], P(None, 'dp')
- grad_gate_weight2: float32 [128, 4, 64], P(None, None, 'dp')
- grad_gate_bias2: float32 [4, 64], P(None, 'dp')
- grad_gate_weight3: float32 [256, 8, 64], P(None, None, 'dp')
- grad_gate_bias3: float32 [8, 64], P(None, 'dp')
- grad_output_weight: float32 [512, 8, 64], P(None, None, 'dp')
- grad_output_bias: float32 [8, 64], P(None, 'dp')
- grad_layer_scale1: float32 [8, 64], P(None, 'dp')
- grad_norm2_gain: float32 [8, 64], P(None, 'dp')
- grad_norm2_bias: float32 [8, 64], P(None, 'dp')
- grad_expand_weight: float32 [512, 32, 64], P(None, None, 'dp')
- grad_expand_bias: float32 [32, 64], P(None, 'dp')
- grad_reduce_weight: float32 [32, 64, 512], P(None, 'dp')
- grad_reduce_bias: float32 [8, 64], P(None, 'dp')
- grad_layer_scale2: float32 [8, 64], P(None, 'dp')
The draws below stay inside these ranges and needn't reach their ends.
All inputs are finite; a program needn't handle non-finite values.
Results may differ from the reference program's by a relative error of at most 0.014.
Values may be sent and summed in bfloat16 or wider, within the bound.
No kernel may reach another device: no remote copies, remote signals or barrier semaphores. Data moves between devices by JAX's collectives and lax.ppermute only.
A program may use at most 576 MiB of HBM per device.

```python
import math
import jax
import jax.numpy as jnp
from jax import lax

WIDTH = 512
FFN = 2048
ORDER0 = 64
KERNEL = 7
CROP = 14
PIX = 50176


def draw_block_input(key, part):
    key = jax.random.fold_in(key, 7)
    subkeys = jax.random.split(key, 5)
    full_shape = (WIDTH // ORDER0, ORDER0, PIX)
    channel_ramp = 1.0 + 2.0 * jnp.arange(ORDER0, dtype=jnp.float32) / (ORDER0 - 1)
    channel_scale = jnp.exp(jax.random.uniform(subkeys[0], (WIDTH // ORDER0, ORDER0, 1), minval=-1.15, maxval=1.15)) * channel_ramp[None, :, None]
    pixel_scale = jnp.exp(jax.random.uniform(subkeys[1], (1, 1, PIX), minval=-1.15, maxval=1.15))
    offset = jnp.clip(0.5 * jax.random.normal(subkeys[2], (WIDTH // ORDER0, ORDER0, 1)), -1.5, 1.5)
    fluctuation = jnp.clip(jax.random.normal(subkeys[4], full_shape), -4.0, 4.0)
    return (0.3 * (fluctuation * channel_scale + offset) * pixel_scale).astype(jnp.bfloat16)


def block_scale(key, extent, pieces, least, high):
    loudness = 1.0
    for dim, shards_of in pieces:
        heights = jax.random.uniform(jax.random.fold_in(jax.random.fold_in(key, 6), dim), (shards_of,), jnp.float32, least / len(pieces), high / len(pieces))
        loudness = loudness * jnp.repeat(jnp.exp(heights), extent[dim] // shards_of).reshape((-1,) + (1,) * (len(extent) - 1 - dim))
    return loudness


def gaussian(stream_key, extent, scale, reach, cuts=(), kind=jnp.bfloat16):
    drawn = jax.random.normal(stream_key, extent, jnp.float32) * scale
    if len(cuts) > 0:
        drawn = block_scale(stream_key, extent, cuts, -0.22, 0.18) * drawn
    return jnp.clip(drawn, min=-reach, max=reach).astype(kind)


def setup_inputs(seed: int = 0) -> dict:
    arg_keys = jax.random.split(jax.random.key(seed), 25)
    block_input = draw_block_input(jax.random.fold_in(arg_keys[24], 71), 0)
    norm1_gain = jnp.clip(jnp.exp(math.log(2.0) - 1.3862944 * jax.random.uniform(arg_keys[1], (WIDTH // ORDER0, ORDER0), jnp.float32) ** block_scale(arg_keys[1], (WIDTH // ORDER0, ORDER0), ((1, 4),), -0.2, 0.2)), 0.5, 2.0).astype(jnp.bfloat16)
    norm1_bias = gaussian(arg_keys[2], (WIDTH // ORDER0, ORDER0), 0.5, 3.0, ((1, 4),))
    input_weight = gaussian(arg_keys[3], (WIDTH, 2 * WIDTH // ORDER0, ORDER0), WIDTH ** -0.5, 0.25, ((2, 4),))
    input_bias = gaussian(arg_keys[4], (2 * WIDTH // ORDER0, ORDER0), 0.5, 3.0, ((1, 4),))
    conv_weight = gaussian(arg_keys[5], (KERNEL * KERNEL, 2 * WIDTH // ORDER0 - 1, ORDER0), 5 ** -0.5, 2.5, ((2, 4),))
    conv_bias = gaussian(arg_keys[6], (2 * WIDTH // ORDER0 - 1, ORDER0), 0.5, 3.0, ((1, 4),))
    gate_weight1 = gaussian(arg_keys[7], (ORDER0, 2, ORDER0), ORDER0 ** -0.5, 0.75, ((2, 4),))
    gate_bias1 = gaussian(arg_keys[8], (2, ORDER0), 0.5, 3.0, ((1, 4),))
    gate_weight2 = gaussian(arg_keys[9], (2 * ORDER0, 4, ORDER0), (2 * ORDER0) ** -0.5, 0.5, ((2, 4),))
    gate_bias2 = gaussian(arg_keys[10], (4, ORDER0), 0.5, 3.0, ((1, 4),))
    gate_weight3 = gaussian(arg_keys[11], (4 * ORDER0, 8, ORDER0), (4 * ORDER0) ** -0.5, 0.375, ((2, 4),))
    gate_bias3 = gaussian(arg_keys[12], (8, ORDER0), 0.5, 3.0, ((1, 4),))
    output_weight = gaussian(arg_keys[13], (WIDTH, WIDTH // ORDER0, ORDER0), WIDTH ** -0.5, 0.25, ((2, 4),))
    output_bias = gaussian(arg_keys[14], (WIDTH // ORDER0, ORDER0), 0.5, 3.0, ((1, 4),))
    layer_scale1 = jnp.clip(jnp.exp(math.log(2.0) - 1.3862944 * jax.random.uniform(arg_keys[15], (WIDTH // ORDER0, ORDER0), jnp.float32) ** block_scale(arg_keys[15], (WIDTH // ORDER0, ORDER0), ((1, 4),), -0.2, 0.2)), 0.5, 2.0).astype(jnp.bfloat16)
    norm2_gain = jnp.clip(jnp.exp(math.log(2.0) - 1.3862944 * jax.random.uniform(arg_keys[16], (WIDTH // ORDER0, ORDER0), jnp.float32) ** block_scale(arg_keys[16], (WIDTH // ORDER0, ORDER0), ((1, 4),), -0.2, 0.2)), 0.5, 2.0).astype(jnp.bfloat16)
    norm2_bias = gaussian(arg_keys[17], (WIDTH // ORDER0, ORDER0), 0.5, 3.0, ((1, 4),))
    expand_weight = gaussian(arg_keys[18], (WIDTH, FFN // ORDER0, ORDER0), WIDTH ** -0.5, 0.25, ((2, 4),))
    expand_bias = gaussian(arg_keys[19], (FFN // ORDER0, ORDER0), 0.5, 3.0, ((1, 4),))
    reduce_weight = gaussian(arg_keys[20], (FFN // ORDER0, ORDER0, WIDTH), FFN ** -0.5, 0.125, ((1, 4),))
    reduce_bias = gaussian(arg_keys[21], (WIDTH // ORDER0, ORDER0), 0.5, 3.0, ((1, 4),))
    layer_scale2 = jnp.clip(jnp.exp(math.log(2.0) - 1.3862944 * jax.random.uniform(arg_keys[22], (WIDTH // ORDER0, ORDER0), jnp.float32) ** block_scale(arg_keys[22], (WIDTH // ORDER0, ORDER0), ((1, 4),), -0.2, 0.2)), 0.5, 2.0).astype(jnp.bfloat16)
    cotangent = gaussian(arg_keys[23], (WIDTH // ORDER0, ORDER0, PIX), 1.0, 6.0, ((1, 4), (2, 8)))
    return {"block_input": block_input, "norm1_gain": norm1_gain, "norm1_bias": norm1_bias, "input_weight": input_weight, "input_bias": input_bias, "conv_weight": conv_weight, "conv_bias": conv_bias, "gate_weight1": gate_weight1, "gate_bias1": gate_bias1, "gate_weight2": gate_weight2, "gate_bias2": gate_bias2, "gate_weight3": gate_weight3, "gate_bias3": gate_bias3, "output_weight": output_weight, "output_bias": output_bias, "layer_scale1": layer_scale1, "norm2_gain": norm2_gain, "norm2_bias": norm2_bias, "expand_weight": expand_weight, "expand_bias": expand_bias, "reduce_weight": reduce_weight, "reduce_bias": reduce_bias, "layer_scale2": layer_scale2, "cotangent": cotangent}


@jax.custom_vjp
def low(v):
    return lax.optimization_barrier(v.astype(jnp.bfloat16)).astype(jnp.float32)

@jax.custom_vjp
def low_back(v):
    return v

def low_keep(v):
    return (low(v), None)

def low_pass(kept, grad):
    return (grad,)

def back_keep(v):
    return (v, None)

def back_low(kept, grad):
    return (low(grad),)
low.defvjp(low_keep, low_pass)
low_back.defvjp(back_keep, back_low)
epsilon = 1e-06
highest = lax.Precision.HIGHEST

def layer_norm(values, norm_gain, norm_bias):
    center = lax.optimization_barrier(jnp.mean(values, axis=0))
    spread = lax.optimization_barrier(jnp.mean(jnp.square(values - center), axis=0))
    return (values - center) * lax.rsqrt(spread + epsilon) * norm_gain[:, None] + norm_bias[:, None]

def apply_weight(weight, values):
    return jnp.dot(weight.T, values, precision=highest)

def depthwise(values, weight):
    channels = values.shape[0]
    half_span = KERNEL // 2
    crop_grid = values.reshape(channels, -1, CROP, CROP)
    padded = jnp.pad(crop_grid, ((0, 0), (0, 0), (half_span, half_span), (half_span, half_span)))
    result = jnp.zeros(crop_grid.shape, jnp.float32)
    for tap_row in range(KERNEL):
        for tap_col in range(KERNEL):
            window = padded[:, :, tap_row:tap_row + CROP, tap_col:tap_col + CROP]
            result = result + weight[tap_row * KERNEL + tap_col][:, None, None, None] * window
    return result.reshape(channels, -1)

def forward(params, values):
    norm1_gain, norm1_bias, input_weight, input_bias, conv_weight, conv_bias, gate_weight1, gate_bias1, gate_weight2, gate_bias2, gate_weight3, gate_bias3, output_weight, output_bias, layer_scale1, norm2_gain, norm2_bias, expand_weight, expand_bias, reduce_weight, reduce_bias, layer_scale2 = params
    normed1 = low(layer_norm(values, norm1_gain, norm1_bias))
    projected = low_back(apply_weight(input_weight, normed1) + input_bias[:, None])
    gate_in = projected[:ORDER0]
    conv_out = (depthwise(projected[ORDER0:], conv_weight) + conv_bias[:, None]) / 3.0
    order_now = low(gate_in * conv_out[:ORDER0])
    first_row = ORDER0
    for gate_weight, gate_bias in ((gate_weight1, gate_bias1), (gate_weight2, gate_bias2), (gate_weight3, gate_bias3)):
        width_next = gate_weight.shape[1]
        pre_gate = low_back(apply_weight(gate_weight, order_now) + gate_bias[:, None])
        order_now = low(pre_gate * conv_out[first_row:first_row + width_next])
        first_row = first_row + width_next
    branch = low_back(apply_weight(output_weight, order_now) + output_bias[:, None])
    middle = values + layer_scale1[:, None] * branch
    normed2 = low(layer_norm(middle, norm2_gain, norm2_bias))
    hidden_pre = low_back(apply_weight(expand_weight, normed2) + expand_bias[:, None])
    hidden = low(jax.nn.gelu(hidden_pre, approximate=False))
    mlp_out = low_back(apply_weight(reduce_weight, hidden))
    return middle + layer_scale2[:, None] * (mlp_out + reduce_bias[:, None])

def as_matrix(tensor):
    floats = tensor.astype(jnp.float32)
    if floats.ndim == 2:
        return floats.reshape(-1)
    return floats.reshape(floats.shape[0], -1)

def reference(block_input, norm1_gain, norm1_bias, input_weight, input_bias, conv_weight, conv_bias, gate_weight1, gate_bias1, gate_weight2, gate_bias2, gate_weight3, gate_bias3, output_weight, output_bias, layer_scale1, norm2_gain, norm2_bias, expand_weight, expand_bias, reduce_weight, reduce_bias, layer_scale2, cotangent):
    weights = (norm1_gain, norm1_bias, input_weight, input_bias, conv_weight, conv_bias, gate_weight1, gate_bias1, gate_weight2, gate_bias2, gate_weight3, gate_bias3, output_weight, output_bias, layer_scale1, norm2_gain, norm2_bias, expand_weight, expand_bias, reduce_weight, reduce_bias, layer_scale2)
    params = tuple((as_matrix(tensor) for tensor in weights[:19]))
    params = params + (reduce_weight.astype(jnp.float32).reshape(-1, WIDTH),)
    params = params + tuple((as_matrix(tensor) for tensor in weights[20:]))
    crop_group = 16 * CROP * CROP
    group_count = PIX // crop_group
    stacked_input = block_input.astype(jnp.float32).reshape(WIDTH, group_count, crop_group).transpose(1, 0, 2)
    stacked_cot = cotangent.astype(jnp.float32).reshape(WIDTH, group_count, crop_group).transpose(1, 0, 2)

    def block_step(totals, block_pair):
        values, grad_out = block_pair
        result, pullback = jax.vjp(forward, params, values)
        grad_params, grad_values = pullback(grad_out)
        return (jax.tree.map(jnp.add, totals, grad_params), (result, grad_values))
    zero_grads = jax.tree.map(jnp.zeros_like, params)
    totals, (results, grad_inputs) = lax.scan(block_step, zero_grads, (stacked_input, stacked_cot))
    block_output = results.transpose(1, 0, 2).reshape(block_input.shape).astype(jnp.bfloat16)
    input_grad = grad_inputs.transpose(1, 0, 2).reshape(block_input.shape).astype(jnp.bfloat16)
    shaped = tuple((summed.reshape(tensor.shape) for summed, tensor in zip(totals, weights)))
    return (block_output, input_grad, shaped[0], shaped[1], shaped[2], shaped[3], shaped[4], shaped[5], shaped[6], shaped[7], shaped[8], shaped[9], shaped[10], shaped[11], shaped[12], shaped[13], shaped[14], shaped[15], shaped[16], shaped[17], shaped[18], shaped[19], shaped[20], shaped[21])
```

```python
from functools import partial

import jax
import jax.numpy as jnp
from jax import lax
from jax.experimental import pallas as pl
from jax.experimental.pallas import tpu as pltpu
from jax.sharding import PartitionSpec as P

WIDTH = 512
GROUP = 64
SIDE = 14
CROP = SIDE * SIDE
CROPS = 8
TOKENS = CROP * CROPS
SHARD = 128
TAPS = 49
EPSILON = 1e-06
LOW = jnp.bfloat16
FULL = jnp.float32
VMEM = 58 * 1024 * 1024

NN = (((1,), (0,)), ((), ()))
NT = (((1,), (1,)), ((), ()))
TN = (((0,), (0,)), ((), ()))

CORE_SWAP = [(0, 1), (1, 0), (2, 3), (3, 2)]
CHIP_SWAP = [(0, 2), (2, 0), (1, 3), (3, 1)]
BOTH_SWAP = [(0, 3), (3, 0), (1, 2), (2, 1)]

S_GATE3, S_GATE2, S_GATE1, S_CONV, S_VEC, S_EXPAND, S_ROWS = 0, 256, 320, 352, 592, 800, 832
(V_N1G, V_N1B, V_INB, V_CB, V_GB1, V_GB2, V_GB3, V_OB, V_LS1, V_N2G, V_N2B, V_RB, V_LS2) = range(13)
VECTORS = 13
E_OUT, E_VEC, E_EXPAND, E_ROWS = 0, 352 + 512, 496 + 512, 576 + 512
E_GATE = 512


def mm(left, right, dims=NN):
    return lax.dot_general(left, right, dims, preferred_element_type=FULL)


def call(body, out, weight=1.0, **kwargs):
    flops, moved = int(weight * 1.15e9 / 4), 1 << 10
    return pl.pallas_call(
        body,
        out_shape=out,
        compiler_params=pltpu.CompilerParams(vmem_limit_bytes=VMEM),
        cost_estimate=pl.CostEstimate(flops=flops, bytes_accessed=moved, transcendentals=0),
        **kwargs,
    )


def struct(shape, dtype):
    return jax.ShapeDtypeStruct(shape, dtype)


SMEM_SPEC = pl.BlockSpec(memory_space=pltpu.SMEM)


def whole(shape):
    return pl.BlockSpec(shape, lambda i: (0,) * len(shape))


def turn_blocks(me, x_ref, outs, wide, blocks):
    lanes = x_ref.shape[1]
    for dest in range(4):
        for crop in range(CROPS):
            start = CROP * (CROPS * dest + crop)
            base = start // 128 * 128
            window = x_ref[:, base : base + min(lanes - base, 384)].astype(FULL)
            wide[pl.ds(crop, CROP, stride=CROPS), :] = window[:, start - base : start - base + CROP].T
        blocks[dest ^ me] = wide[...].astype(LOW)
    for k in range(4):
        outs[k][...] = blocks[k]


PIXEL_SCRATCH = [pltpu.VMEM((TOKENS, SHARD), FULL), pltpu.VMEM((4, TOKENS, SHARD), LOW)]


def to_pixels_body(me_ref, x_ref, *refs):
    turn_blocks(me_ref[0], x_ref, refs[:4], refs[4], refs[5])


def to_pixels(me, x):
    return call(
        to_pixels_body,
        (struct((TOKENS, SHARD), LOW),) * 4,
        weight=4.0,
        in_specs=[SMEM_SPEC, pl.BlockSpec(memory_space=pltpu.VMEM)],
        scratch_shapes=PIXEL_SCRATCH,
    )(me, x)


def first_body(me_ref, x_ref, *refs):
    pack_body(*refs[:18], refs[18], refs[23])
    turn_blocks(me_ref[0], x_ref, refs[19:23], refs[24], refs[25])


def first_kernel(me, x, small):
    return call(
        first_body,
        (struct((S_ROWS, 128), LOW),) + (struct((TOKENS, SHARD), LOW),) * 4,
        in_specs=[SMEM_SPEC] + [pl.BlockSpec(memory_space=pltpu.VMEM)] * 19,
        scratch_shapes=[pltpu.VMEM((S_ROWS, 128), FULL)] + PIXEL_SCRATCH,
    )(me, x, *small)


def from_pixels_body(me_ref, *refs):
    ins, out_ref, wide, blocks = refs[:4], refs[4], refs[5], refs[6]
    me = me_ref[0]
    for k in range(4):
        blocks[k ^ me] = ins[k][...]
    for source in range(4):
        wide[...] = blocks[source].astype(FULL)
        for crop in range(CROPS):
            start = CROP * (CROPS * source + crop)
            part = wide[pl.ds(crop, CROP, stride=CROPS), :].T
            out_ref[:, start : start + CROP] = part.astype(LOW)


def from_pixels(me, blocks):
    return call(
        from_pixels_body,
        struct((SHARD, 4 * TOKENS), LOW),
        weight=4.0,
        in_specs=[SMEM_SPEC] + [pl.BlockSpec(memory_space=pltpu.VMEM)] * 4,
        scratch_shapes=[pltpu.VMEM((TOKENS, SHARD), FULL), pltpu.VMEM((4, TOKENS, SHARD), LOW)],
    )(me, *blocks)


def pack_body(g3, g2, g1, conv, *refs):
    vectors, expand, out_ref, slab = refs[:VECTORS], refs[VECTORS], refs[VECTORS + 1], refs[VECTORS + 2]
    slab[...] = jnp.zeros_like(slab)
    slab[S_GATE3 : S_GATE3 + 128, :] = g3[:, :128].astype(FULL)
    slab[S_GATE3 + 128 : S_GATE3 + 256, :] = g3[:, 128:].astype(FULL)
    slab[S_GATE2 : S_GATE2 + 64, :] = g2[...].astype(FULL)
    slab[S_GATE1 : S_GATE1 + 32, :GROUP] = g1[...].astype(FULL)
    slab[S_CONV : S_CONV + 240, :TAPS] = conv[...].astype(FULL)
    for number, ref in enumerate(vectors):
        first = S_VEC + 16 * number + (1 if number == V_CB else 0)
        slab[first : first + ref.shape[0], :16] = ref[...].astype(FULL)
    slab[S_EXPAND : S_EXPAND + 32, :16] = expand[...].astype(FULL)
    out_ref[...] = slab[...].astype(LOW)


def iota(shape, dim):
    return lax.broadcasted_iota(jnp.int32, shape, dim)


def spread(lanes):
    return jnp.where(iota((128, lanes), 1) % 16 == iota((128, lanes), 0), 1.0, 0.0).astype(LOW)


def prepare_body(me_ref, *refs):
    slabs, ins = refs[0:4], refs[4:8]
    vec, expand, w1, w1_back, w2, w3, w_in, taps, perm, channels = refs[8:]
    me = me_ref[0]
    totals = jnp.zeros((VECTORS, 1024), FULL)
    spread_wide = spread(1024)
    row = iota((VECTORS * 16, 1024), 0) % 16
    lane = iota((VECTORS * 16, 1024), 1)
    in_row = row == lane // 64
    spread_expand = spread(512)
    expand_rows = iota((32, 512), 0) == iota((32, 512), 1) // 16
    w1[...] = jnp.zeros_like(w1)
    channels[0:GROUP, :] = jnp.where(iota((GROUP, 128), 1) == TAPS // 2, 3.0, 0.0)
    for k in range(4):
        source = me ^ k
        slab = slabs[k]
        values = mm(slab[S_VEC : S_VEC + VECTORS * 16, :], spread_wide)
        values = jnp.where(in_row & (lane // 16 % 4 == source), values, 0.0)
        totals = totals + jnp.sum(values.reshape(VECTORS, 16, 1024), axis=1)
        values = mm(slab[S_EXPAND : S_EXPAND + 32, :], spread_expand)
        values = jnp.sum(jnp.where(expand_rows, values, 0.0), axis=0, keepdims=True)
        expand[8 * k : 8 * k + 8, :] = jnp.broadcast_to(values, (8, 512))
        for a in range(16):
            place = pl.ds(pl.multiple_of(a * 64 + source * 16, 16), 16)
            rows = slice(a * 16, a * 16 + 16)
            w_in[place, :] = ins[k][rows, :]
            if a < 15:
                later = pl.ds(pl.multiple_of((a + 1) * 64 + source * 16, 16), 16)
                channels[later, :] = slab[S_CONV + a * 16 : S_CONV + a * 16 + 16, :].astype(FULL)
            if a < 8:
                w3[place, 0:128] = slab[S_GATE3 + a * 16 : S_GATE3 + a * 16 + 16, :]
                w3[place, 128:256] = slab[S_GATE3 + 128 + a * 16 : S_GATE3 + 128 + a * 16 + 16, :]
            if a < 4:
                w2[place, :] = slab[S_GATE2 + a * 16 : S_GATE2 + a * 16 + 16, :]
            if a < 2:
                w1[place, :] = slab[S_GATE1 + a * 16 : S_GATE1 + a * 16 + 16, :]
        column = iota((SHARD, WIDTH), 0)
        target = column // 16 * 64 + source * 16 + column % 16
        perm[k * SHARD : (k + 1) * SHARD, :] = jnp.where(iota((SHARD, WIDTH), 1) == target, 1.0, 0.0).astype(LOW)
    vec[0:VECTORS, :] = totals
    vec[VECTORS:16, :] = jnp.zeros((16 - VECTORS, 1024), FULL)
    single = w1[...].astype(FULL)
    w1_back[...] = (single + pltpu.roll(single, GROUP, 1)).astype(LOW)
    taps[...] = channels[...].T[0:64, :]


def prepare(me, slabs, ins):
    return call(
        prepare_body,
        (
            struct((16, 1024), FULL),
            struct((32, 512), FULL),
            struct((128, 128), LOW),
            struct((128, 128), LOW),
            struct((256, 128), LOW),
            struct((512, 256), LOW),
            struct((1024, 512), LOW),
            struct((64, 1024), FULL),
            struct((512, 512), LOW),
        ),
        weight=4.0,
        in_specs=[SMEM_SPEC] + [pl.BlockSpec(memory_space=pltpu.VMEM)] * 8,
        scratch_shapes=[pltpu.VMEM((1024, 128), FULL)],
    )(me, *slabs, *ins)


def join_output_body(me_ref, r0, r1, r2, r3, out):
    me = me_ref[0]
    for k, ref in enumerate((r0, r1, r2, r3)):
        for a in range(8):
            place = pl.ds(pl.multiple_of(a * 64 + (me ^ k) * 16, 16), 16)
            out[place, :] = ref[a * 16 : a * 16 + 16, :]


def join_output(me, shards):
    return call(
        join_output_body,
        struct((512, 512), LOW),
        in_specs=[SMEM_SPEC] + [pl.BlockSpec(memory_space=pltpu.VMEM)] * 4,
    )(me, *shards)


def normed(values):
    center = jnp.sum(values, axis=1, keepdims=True) * (1.0 / WIDTH)
    away = values - center
    spread_sq = jnp.sum(away * away, axis=1, keepdims=True) * (1.0 / WIDTH)
    inverse = lax.rsqrt(spread_sq + EPSILON)
    return away * inverse, inverse


def norm_back(grad, unit, inverse, gain):
    grad_unit = grad * gain
    first = jnp.sum(grad_unit, axis=1, keepdims=True) * (1.0 / WIDTH)
    second = jnp.sum(grad_unit * unit, axis=1, keepdims=True) * (1.0 / WIDTH)
    return inverse * (grad_unit - first - unit * second)


def total(values):
    return jnp.sum(values, axis=0, keepdims=True)


def row(vec, number, lanes=WIDTH):
    return vec[number : number + 1, 0:lanes]


def rows_spec(tile, lanes):
    return pl.BlockSpec((tile, lanes), lambda i: (i, 0))


def chunks(count, size, body):
    def step(i, carry):
        body(pl.ds(pl.multiple_of(i * size, size), size))
        return carry

    lax.fori_loop(0, count // size, step, 0)


NORM_ROWS = 224
HALVES = (slice(0, TOKENS // 2), slice(TOKENS // 2, TOKENS))


def join(blocks, perm, rows):
    return mm(jnp.concatenate([r[rows, :] for r in blocks], axis=1), perm[...])


def conv_rows(source, weights, emit, flip):
    def one_row(i, carry):
        def one_tap_row(r, sums):
            base = (i + r - 3) * SIDE
            values = [source[base + c] for c in range(SIDE)]
            first = (6 - r) * 7 if flip else r * 7
            taps = [weights[first + (6 - s if flip else s)] for s in range(7)]
            sums = list(sums)
            for s in range(7):
                for c in range(SIDE):
                    if 0 <= c + s - 3 < SIDE:
                        sums[c] = sums[c] + taps[s] * values[c + s - 3]
            return tuple(sums)

        zero = jnp.zeros((CROPS, 128), FULL)
        sums = lax.fori_loop(
            jnp.maximum(0, 3 - i), jnp.minimum(7, 17 - i), one_tap_row, (zero,) * SIDE
        )
        emit(i, sums)
        return carry

    lax.fori_loop(0, SIDE, one_row, 0)


def wide_taps(taps, weights):
    for tap in range(TAPS):
        weights[tap] = jnp.broadcast_to(taps[tap : tap + 1, :], (CROPS, 128))


PIXEL_BLOCK = pl.BlockSpec((CROP, CROPS, 128), lambda i: (0, 0, i))


def lane_block(rows):
    return pl.BlockSpec((rows, 128), lambda i: (0, i))


def front_body(r0, r1, r2, r3, perm, vec, w_in, taps, vec_part, x, z, u, dwv, weights):
    @pl.when(pl.program_id(0) == 0)
    def _():
        for rows in HALVES:
            x[rows, :] = join((r0, r1, r2, r3), perm, rows).astype(LOW)

        def norm_rows(rows):
            unit, _ = normed(x[rows, :].astype(FULL))
            z[rows, :] = (unit * row(vec, V_N1G) + row(vec, V_N1B)).astype(LOW)

        chunks(TOKENS, NORM_ROWS, norm_rows)

    wide_taps(taps, weights)
    values = mm(z[...], w_in[...], NT) + vec_part[V_INB : V_INB + 1, :]
    u[...] = values.reshape(CROP, CROPS, 128)
    bias = jnp.broadcast_to(vec_part[V_CB : V_CB + 1, :], (CROPS, 128))

    def emit(i, sums):
        for c in range(SIDE):
            dwv[i * SIDE + c] = (sums[c] + bias) * (1.0 / 3.0)

    conv_rows(u, weights, emit, False)


def front(blocks, perm, vec, w_in, taps):
    pixels = struct((CROP, CROPS, 1024), FULL)
    rows = struct((TOKENS, WIDTH), LOW)
    x, z, u, dwv = call(
        front_body,
        (rows, rows, pixels, pixels),
        weight=28.0,
        grid=(8,),
        in_specs=[whole((TOKENS, SHARD))] * 4
        + [
            whole((512, 512)),
            whole((16, 1024)),
            pl.BlockSpec((128, 512), lambda i: (i, 0)),
            lane_block(64),
            lane_block(16),
        ],
        out_specs=(whole((TOKENS, WIDTH)), whole((TOKENS, WIDTH)), PIXEL_BLOCK, PIXEL_BLOCK),
        scratch_shapes=[pltpu.VMEM((TAPS, CROPS, 128), FULL)],
    )(*blocks, perm, vec, w_in, taps, vec)
    return x, z, u, dwv.reshape(TOKENS, 1024)


def gate_chain(dwv, vec, w1, w2, w3):
    first = dwv[:, 0:128]
    turned = pltpu.roll(first, GROUP, 1)
    q0 = (first * turned).astype(LOW)
    t1 = mm(q0, w1[...], NT) + row(vec, V_GB1, 128)
    q1 = (t1 * dwv[:, 128:256]).astype(LOW)
    t2 = mm(q1, w2[...], NT) + row(vec, V_GB2, 256)
    q2 = (t2 * dwv[:, 256:512]).astype(LOW)
    t3 = mm(q2, w3[...], NT) + row(vec, V_GB3, 512)
    q3 = (t3 * dwv[:, 512:1024]).astype(LOW)
    return turned, (q0, q1, q2, q3), (t1, t2, t3)


def branch_body(dwv, x, vec, w1, w2, w3, w_out, z_out):
    _, orders, _ = gate_chain(dwv[...], vec, w1, w2, w3)
    branch = mm(orders[3], w_out[...], NT) + row(vec, V_OB)
    middle = x[...].astype(FULL) + row(vec, V_LS1) * branch
    unit, _ = normed(middle)
    z_out[...] = (unit * row(vec, V_N2G) + row(vec, V_N2B)).astype(LOW)


def branch_forward(dwv, x, vec, w1, w2, w3, w_out, tile=784):
    return call(
        branch_body,
        struct((TOKENS, WIDTH), LOW),
        weight=7.0,
        grid=(TOKENS // tile,),
        in_specs=[
            rows_spec(tile, 1024),
            rows_spec(tile, WIDTH),
            whole((16, 1024)),
            whole((128, 128)),
            whole((256, 128)),
            whole((512, 256)),
            whole((512, 512)),
        ],
        out_specs=rows_spec(tile, WIDTH),
    )(dwv, x, vec, w1, w2, w3, w_out)


def gelu_parts(s):
    bell = jnp.exp2((-0.5 * 1.4426950408889634) * (s * s))
    size = jnp.abs(s)
    t = pltpu.reciprocal(1.0 + (0.3275911 * 0.7071067811865476) * size, approx=True)
    poly = 0.5 * 1.061405429
    for coefficient in (-1.453152027, 1.421413741, -0.284496736, 0.254829592):
        poly = poly * t + 0.5 * coefficient
    tail = poly * t * bell
    cdf = jnp.where(s >= 0.0, 1.0 - tail, tail)
    return s * cdf, cdf + s * (bell * 0.3989422804014327)


PIECE = 16


def mlp_body(z, r0, r1, r2, r3, perm, vec, expand, *refs):
    e_in, r_in = refs[0:4], refs[4:8]
    dy, f, dz, se, sr, ke, kr, gb = refs[8:16]
    we, wr, df, s0, s1, g0, g1, h0, h1, d0, d1, acc_e, acc_r, sums, sem_e, sem_r = refs[16:]
    pre, grad_h, hid, grad_s = (s0, s1), (g0, g1), (h0, h1), (d0, d1)
    half = TOKENS // 2
    for slot in range(4):
        pltpu.make_async_copy(e_in[slot], we.at[slot], sem_e.at[slot]).start()
        pltpu.make_async_copy(r_in[slot], wr.at[slot], sem_r.at[slot]).start()

    def arrived(slot):
        pltpu.make_async_copy(we.at[slot], we.at[slot], sem_e.at[slot]).wait()
        pltpu.make_async_copy(wr.at[slot], wr.at[slot], sem_r.at[slot]).wait()

    for rows in HALVES:
        dy[rows, :] = join((r0, r1, r2, r3), perm, rows).astype(LOW)

    def scaled(rows):
        df[rows, :] = (dy[rows, :].astype(FULL) * row(vec, V_LS2)).astype(LOW)
        f[rows, :] = jnp.zeros((112, WIDTH), FULL)
        dz[rows, :] = jnp.zeros((112, WIDTH), FULL)

    chunks(TOKENS, 112, scaled)
    acc_e[...] = jnp.zeros_like(acc_e)
    acc_r[...] = jnp.zeros_like(acc_r)
    sums[...] = jnp.zeros_like(sums)
    h1[...] = jnp.zeros_like(h1)
    d1[...] = jnp.zeros_like(d1)
    arrived(0)
    s0[...] = mm(z[HALVES[0], :], we[0], NT)
    g0[...] = mm(df[HALVES[0], :], wr[0], NT)
    pieces = half // PIECE

    def unit(here, tile, before, after):
        there = 1 - here
        rows = HALVES[there]
        bias = expand[pl.ds(pl.multiple_of(tile * 8, 8), 1), :]
        done = [0]
        column = [jnp.zeros((8, 512), FULL)]

        def some(part):
            while done[0] < pieces * part // 6:
                piece = slice(done[0] * PIECE, (done[0] + 1) * PIECE)
                act, slope = gelu_parts(pre[here][piece, :] + bias)
                hid[here][piece, :] = act.astype(LOW)
                grad = (grad_h[here][piece, :] * slope).astype(LOW)
                grad_s[here][piece, :] = grad
                grad = grad.astype(FULL)
                column[0] = column[0] + (grad[0:8] + grad[8:16])
                done[0] += 1

        f[rows, :] += mm(hid[there][...], wr[before])
        some(1)
        dz[rows, :] += mm(grad_s[there][...], we[before])
        some(2)
        acc_e[before] += mm(grad_s[there][...], z[rows, :], TN)
        some(3)
        acc_r[before] += mm(hid[there][...], df[rows, :], TN)
        some(4)
        pre[there][...] = mm(z[rows, :], we[after], NT)
        some(5)
        grad_h[there][...] = mm(df[rows, :], wr[after], NT)
        some(6)
        sums[tile] += column[0]

    def one_tile(tile, carry):
        unit(0, tile, jnp.maximum(tile - 1, 0), tile)

        @pl.when(tile < 3)
        def _():
            arrived(tile + 1)

        unit(1, tile, tile, jnp.minimum(tile + 1, 3))
        return carry

    lax.fori_loop(0, 4, one_tile, 0)
    rows = HALVES[1]
    f[rows, :] += mm(h1[...], wr[3])
    dz[rows, :] += mm(d1[...], we[3])
    acc_e[3] += mm(d1[...], z[rows, :], TN)
    acc_r[3] += mm(h1[...], df[rows, :], TN)
    for pair, (e_out, r_out) in enumerate(((se, sr), (ke, kr))):
        for number in range(2):
            e_out[number] = acc_e[2 * pair + number].astype(LOW)
            r_out[number] = acc_r[2 * pair + number].astype(LOW)
    for tile in range(4):
        gb[8 * tile : 8 * tile + 8, :] = sums[tile]


def feed_forward(z, blocks, perm, vec, expand, expand_shards, reduce_shards):
    vmem = pl.BlockSpec(memory_space=pltpu.VMEM)
    anywhere = pl.BlockSpec(memory_space=pl.ANY)
    half = TOKENS // 2
    pair = struct((2, 512, 512), LOW)
    rows = struct((TOKENS, WIDTH), FULL)
    return call(
        mlp_body,
        (struct((TOKENS, WIDTH), LOW), rows, rows, pair, pair, pair, pair, struct((32, 512), FULL)),
        weight=40.0,
        in_specs=[vmem] * 8 + [anywhere] * 8,
        scratch_shapes=[pltpu.VMEM((4, 512, 512), LOW)] * 2
        + [pltpu.VMEM((TOKENS, WIDTH), LOW)]
        + [pltpu.VMEM((half, 512), FULL)] * 4
        + [pltpu.VMEM((half, 512), LOW)] * 4
        + [pltpu.VMEM((4, 512, 512), FULL)] * 2
        + [pltpu.VMEM((4, 8, 512), FULL)]
        + [pltpu.SemaphoreType.DMA((4,))] * 2,
    )(z, *blocks, perm, vec, expand, *expand_shards, *reduce_shards)


def pack_vectors(values, count, source):
    lane = iota((count * 16, 1024), 1)
    keep = (iota((count * 16, 1024), 0) % 16 == lane // 64) & (lane // 16 % 4 == source)
    tall = jnp.broadcast_to(values[:, None, :], (count, 16, 1024)).reshape(count * 16, 1024)
    gather = jnp.where(iota((1024, 128), 0) % 16 == iota((1024, 128), 1), 1.0, 0.0).astype(LOW)
    return mm(jnp.where(keep, tall, 0.0).astype(LOW), gather)


def part_pair(parts, sibling, keep):
    sibling[0] = parts[1]
    sibling[1] = parts[3]
    keep[0] = parts[0]
    keep[1] = parts[2]


def branch_back_body(steps, me_ref, dwv, x, dy, f, dz, vec, w1, w1_back, w2, w3, w_out, perm, gb, *refs):
    (o0, o1, o2, o3, g_out, dx_out, sibling, keep) = refs[0:8]
    acc_o, acc_3, acc_2, acc_1, sums, parts = refs[8:]
    step = pl.program_id(0)
    values = dwv[...]
    turned, orders, gates = gate_chain(values, vec, w1, w2, w3)
    branch = mm(orders[3], w_out[...], NT) + row(vec, V_OB)
    middle = x[...].astype(FULL) + row(vec, V_LS1) * branch
    unit, inverse = normed(middle)
    top = dy[...].astype(FULL)
    mlp = f[...] + row(vec, V_RB)
    output = (middle + row(vec, V_LS2) * mlp).astype(LOW)
    blocks = mm(output, perm[...], NT).astype(LOW)
    for k, ref in enumerate((o0, o1, o2, o3)):
        ref[...] = blocks[:, k * SHARD : (k + 1) * SHARD]
    grad = dz[...]
    middle_grad = top + norm_back(grad, unit, inverse, row(vec, V_N2G))
    dx_out[...] = middle_grad
    grad_branch = (middle_grad * row(vec, V_LS1)).astype(LOW)
    grad_o = mm(grad_branch, orders[3], TN)
    back = mm(grad_branch, w_out[...])
    gt3 = (back * values[:, 512:1024]).astype(LOW)
    g_out[:, 512:1024] = back * gates[2] * (1.0 / 3.0)
    grad_3 = mm(gt3, orders[2], TN)
    back = mm(gt3, w3[...])
    gt2 = (back * values[:, 256:512]).astype(LOW)
    g_out[:, 256:512] = back * gates[1] * (1.0 / 3.0)
    grad_2 = mm(gt2, orders[1], TN)
    back = mm(gt2, w2[...])
    gt1 = (back * values[:, 128:256]).astype(LOW)
    g_out[:, 128:256] = back * gates[0] * (1.0 / 3.0)
    grad_1 = mm(gt1, orders[0], TN)
    back = mm(gt1, w1_back[...])
    g_out[:, 0:128] = back * turned * (1.0 / 3.0)

    @pl.when(step == 0)
    def _():
        acc_o[...] = jnp.zeros_like(acc_o)
        acc_3[...] = jnp.zeros_like(acc_3)
        acc_2[...] = jnp.zeros_like(acc_2)
        acc_1[...] = jnp.zeros_like(acc_1)
        sums[...] = jnp.zeros_like(sums)

    acc_o[...] += grad_o
    acc_3[...] += grad_3
    acc_2[...] += grad_2
    acc_1[...] += grad_1
    sums[0:1, 0:128] += total(gt1.astype(FULL))
    sums[1:2, 0:256] += total(gt2.astype(FULL))
    sums[2:3, 0:512] += total(gt3.astype(FULL))
    sums[3:4, 0:512] += total(grad_branch.astype(FULL))
    sums[4:5, 0:512] += total(middle_grad * branch)
    sums[5:6, 0:512] += total(grad * unit)
    sums[6:7, 0:512] += total(grad)
    sums[7:8, 0:512] += total(top) * row(vec, V_LS2)
    sums[8:9, 0:512] += total(top * mlp)

    @pl.when(step == steps - 1)
    def _():
        me = me_ref[0]
        vectors = sums[0:9, :]
        expand_rows = iota((32, 512), 0) == iota((32, 512), 1) // 16
        gather = jnp.where(iota((512, 128), 0) % 16 == iota((512, 128), 1), 1.0, 0.0).astype(LOW)
        for source in range(4):
            k = source ^ me
            for a in range(8):
                rows = slice(a * 64 + source * 16, a * 64 + source * 16 + 16)
                for part in range(4):
                    first = part * 128 + a * 16
                    parts[k, first : first + 16, :] = acc_o[rows, part * 128 : part * 128 + 128].astype(LOW)
                first = E_GATE + a * 16
                parts[k, first : first + 16, :] = acc_3[rows, 0:128].astype(LOW)
                parts[k, first + 128 : first + 144, :] = acc_3[rows, 128:256].astype(LOW)
                if a < 4:
                    parts[k, first + 256 : first + 272, :] = acc_2[rows, :].astype(LOW)
                if a < 2:
                    parts[k, first + 320 : first + 336, :] = acc_1[rows, :].astype(LOW)
            parts[k, E_VEC : E_VEC + 144, :] = pack_vectors(vectors, 9, source).astype(LOW)
        for k in range(4):
            slot = (2, 0, 3, 1)[k]
            line = total(gb[8 * slot : 8 * slot + 8, :])
            tall = jnp.where(expand_rows, jnp.broadcast_to(line, (32, 512)), 0.0)
            parts[k, E_EXPAND : E_EXPAND + 32, :] = mm(tall.astype(LOW), gather).astype(LOW)
            parts[k, E_EXPAND + 32 : E_ROWS, :] = jnp.zeros((E_ROWS - E_EXPAND - 32, 128), LOW)
        part_pair(parts, sibling, keep)


def branch_backward(me, dwv, x, dy, f, dz, vec, w1, w1_back, w2, w3, w_out, perm, biases, tile=224):
    steps = TOKENS // tile
    wide = rows_spec(tile, WIDTH)
    block = rows_spec(tile, SHARD)
    pair = (2, E_ROWS, 128)
    return call(
        partial(branch_back_body, steps),
        (struct((TOKENS, SHARD), LOW),) * 4
        + (
            struct((TOKENS, 1024), FULL),
            struct((TOKENS, WIDTH), FULL),
            struct(pair, LOW),
            struct(pair, LOW),
        ),
        weight=20.0,
        grid=(steps,),
        in_specs=[
            SMEM_SPEC,
            rows_spec(tile, 1024),
            wide,
            wide,
            wide,
            wide,
            whole((16, 1024)),
            whole((128, 128)),
            whole((128, 128)),
            whole((256, 128)),
            whole((512, 256)),
            whole((512, 512)),
            whole((512, 512)),
        ]
        + [whole((32, 512))],
        out_specs=(block,) * 4
        + (rows_spec(tile, 1024), wide, whole(pair), whole(pair)),
        scratch_shapes=[
            pltpu.VMEM((512, 512), FULL),
            pltpu.VMEM((512, 256), FULL),
            pltpu.VMEM((256, 128), FULL),
            pltpu.VMEM((128, 128), FULL),
            pltpu.VMEM((16, 1024), FULL),
            pltpu.VMEM((4, E_ROWS, 128), LOW),
        ],
    )(me, dwv, x, dy, f, dz, vec, w1, w1_back, w2, w3, w_out, perm, biases)


def conv_back_body(me_ref, g, u, taps, z, du, sibling, keep, weights, grad_taps, parts):
    step, steps = pl.program_id(0), pl.num_programs(0)
    me = me_ref[0]
    wide_taps(taps, weights)
    zero = jnp.zeros((CROPS, 128), FULL)

    def emit(i, sums):
        stacked = jnp.concatenate(list(sums), axis=0).astype(LOW)
        du[pl.ds(pl.multiple_of(i * SIDE * CROPS, 16), SIDE * CROPS), :] = stacked

    conv_rows(g, weights, emit, True)

    for r in range(7):

        def one_row(i, sums):
            grads = [g[i * SIDE + c] for c in range(SIDE)]
            values = [u[(i + r - 3) * SIDE + c] for c in range(SIDE)]
            sums = list(sums)
            for c in range(SIDE):
                for s in range(7):
                    if 0 <= c + s - 3 < SIDE:
                        sums[s] = sums[s] + grads[c] * values[c + s - 3]
            return tuple(sums)

        sums = lax.fori_loop(max(0, 3 - r), min(SIDE, SIDE + 3 - r), one_row, (zero,) * 7)
        for s in range(7):
            grad_taps[r * 7 + s : r * 7 + s + 1, :] = total(sums[s])
    grad_taps[49:50, :] = total(jnp.sum(g[...], axis=0))
    grad_taps[50:51, :] = total(du[...].astype(FULL))
    grad_taps[51:128, :] = jnp.zeros((77, 128), FULL)
    grad_w = mm(du[...], z[...], TN)
    tall = grad_taps[...].T.astype(LOW)
    for a in range(2):
        for source in range(4):
            k = source ^ me
            rows = slice(a * 64 + source * 16, a * 64 + source * 16 + 16)
            for part in range(4):
                place = pl.ds(pl.multiple_of(part * 128 + step * 32 + a * 16, 16), 16)
                parts[k, place, :] = grad_w[rows, part * 128 : part * 128 + 128].astype(LOW)
            place = pl.ds(pl.multiple_of(512 + step * 32 + a * 16, 16), 16)
            parts[k, place, :] = tall[rows, :]

    @pl.when(step == steps - 1)
    def _():
        part_pair(parts, sibling, keep)


C_ROWS = 640


def conv_backward(me, g, u, taps, z, base):
    pixels = pl.BlockSpec((CROP, CROPS, 128), lambda i: (0, 0, i + base))
    pair = (2, C_ROWS, 128)
    return call(
        conv_back_body,
        (struct((TOKENS, 512), LOW), struct(pair, LOW), struct(pair, LOW)),
        weight=24.0,
        grid=(4,),
        in_specs=[
            SMEM_SPEC,
            pixels,
            pixels,
            pl.BlockSpec((64, 128), lambda i: (0, i + base)),
            whole((TOKENS, WIDTH)),
        ],
        out_specs=(lane_block(TOKENS), whole(pair), whole(pair)),
        scratch_shapes=[
            pltpu.VMEM((TAPS, CROPS, 128), FULL),
            pltpu.VMEM((128, 128), FULL),
            pltpu.VMEM((4, C_ROWS, 128), LOW),
        ],
    )(me, g.reshape(CROP, CROPS, 1024), u, taps, z)


def input_back_body(steps, me_ref, du_low, du_high, x, dx, vec, w_in, perm, *refs):
    (o0, o1, o2, o3, sibling, keep, sums, parts) = refs
    step = pl.program_id(0)
    unit, inverse = normed(x[...].astype(FULL))
    grad = mm(du_low[...], w_in[0:512, :]) + mm(du_high[...], w_in[512:1024, :])
    grad_x = (dx[...] + norm_back(grad, unit, inverse, row(vec, V_N1G))).astype(LOW)
    blocks = mm(grad_x, perm[...], NT).astype(LOW)
    for k, ref in enumerate((o0, o1, o2, o3)):
        ref[...] = blocks[:, k * SHARD : (k + 1) * SHARD]

    @pl.when(step == 0)
    def _():
        sums[...] = jnp.zeros_like(sums)

    sums[0:1, 0:512] += total(grad * unit)
    sums[1:2, 0:512] += total(grad)

    @pl.when(step == steps - 1)
    def _():
        me = me_ref[0]
        vectors = sums[0:2, :]
        for source in range(4):
            parts[source ^ me, 0:32, :] = pack_vectors(vectors, 2, source).astype(LOW)
            parts[source ^ me, 32:64, :] = jnp.zeros((32, 128), LOW)
        part_pair(parts, sibling, keep)


def input_backward(me, du_low, du_high, x, dx, vec, w_in, perm, tile=224):
    steps = TOKENS // tile
    wide = rows_spec(tile, WIDTH)
    pair = (2, 64, 128)
    return call(
        partial(input_back_body, steps),
        (struct((TOKENS, SHARD), LOW),) * 4 + (struct(pair, LOW), struct(pair, LOW)),
        weight=8.0,
        grid=(steps,),
        in_specs=[
            SMEM_SPEC,
            wide,
            wide,
            wide,
            wide,
            whole((16, 1024)),
            whole((1024, 512)),
            whole((512, 512)),
        ],
        out_specs=(rows_spec(tile, SHARD),) * 4 + (whole(pair), whole(pair)),
        scratch_shapes=[pltpu.VMEM((16, 1024), FULL), pltpu.VMEM((4, 64, 128), LOW)],
    )(me, du_low, du_high, x, dx, vec, w_in, perm)


def unpack_body(late, high, low, last, g1, g2, g3, conv, w_out, w_in, *refs):
    late_refs, expand, (in_bias, conv_bias, gain, bias) = refs[0:9], refs[9], refs[10:14]
    gates = late[E_GATE:E_VEC, :].astype(FULL)
    g3[:, 0:128] = gates[0:128]
    g3[:, 128:256] = gates[128:256]
    g2[...] = gates[256:320]
    g1[...] = gates[320:352, 0:GROUP]
    for part in range(4):
        lanes = slice(part * 128, part * 128 + 128)
        w_out[:, lanes] = late[lanes, :].astype(FULL)
        w_in[0:128, lanes] = low[lanes, :].astype(FULL)
        w_in[128:256, lanes] = high[lanes, :].astype(FULL)
    taps = jnp.concatenate([low[512:640, :], high[512:640, :]], axis=0).astype(FULL)
    conv[...] = taps[16:256, 0:TAPS]
    vectors = late[E_VEC : E_VEC + 144, :].astype(FULL)
    for number, ref in enumerate(late_refs):
        ref[...] = vectors[16 * number : 16 * number + ref.shape[0], 0:16]
    expand[...] = late[E_EXPAND : E_EXPAND + 32, 0:16].astype(FULL)
    gain[...] = last[0:8, 0:16].astype(FULL)
    bias[...] = last[16:24, 0:16].astype(FULL)
    own = jnp.where(iota((256, 16), 0) % 16 == iota((256, 16), 1), 1.0, 0.0)
    rows = jnp.where(iota((16, 256), 0) == iota((16, 256), 1) // 16, 1.0, 0.0).astype(LOW)
    conv_bias[...] = mm(rows, (taps[:, 49:50] * own).astype(LOW))[1:16, :]
    in_bias[...] = mm(rows, (taps[:, 50:51] * own).astype(LOW))


def unpack_small(late, high, low, last):
    vector = lambda rows: struct((rows, 16), FULL)
    return call(
        unpack_body,
        (struct((32, 64), FULL), struct((64, 128), FULL), struct((128, 256), FULL), struct((240, 49), FULL))
        + (struct((128, 512), FULL), struct((256, 512), FULL))
        + (vector(2), vector(4))
        + (vector(8),) * 7
        + (vector(32), vector(16), vector(15), vector(8), vector(8)),
    )(late, high, low, last)


def swap(values, pairs):
    return lax.ppermute(values, "dp", pairs)


def exchange(blocks):
    return (
        blocks[0],
        swap(blocks[1], CORE_SWAP),
        swap(blocks[2], CHIP_SWAP),
        swap(blocks[3], BOTH_SWAP),
    )


def gather(values):
    across = swap(values, CHIP_SWAP)
    return (values, swap(values, CORE_SWAP), across, swap(across, CORE_SWAP))


def hold(*values):
    return lax.optimization_barrier(values)


def onward(keep, got):
    return (keep[1].astype(FULL) + got[1].astype(FULL)).astype(LOW)


def own_sum(keep, got, other, count):
    values = (keep[0].astype(FULL) + got[0].astype(FULL) + other.astype(FULL)).astype(LOW)
    return values.reshape(count, values.shape[0] // count, values.shape[1])


def trade(parts):
    return lax.all_to_all(parts, "mp", split_axis=0, concat_axis=0, tiled=True)


def spread_sum(parts):
    mine = jnp.sum(parts.astype(FULL), axis=0).astype(LOW)
    return jnp.broadcast_to(mine[None], parts.shape)


def flat(parts):
    return parts.reshape(-1, parts.shape[2])


def per_device(
    mp_count,
    block_input,
    norm1_gain,
    norm1_bias,
    input_weight,
    input_bias,
    conv_weight,
    conv_bias,
    gate_weight1,
    gate_bias1,
    gate_weight2,
    gate_bias2,
    gate_weight3,
    gate_bias3,
    output_weight,
    output_bias,
    layer_scale1,
    norm2_gain,
    norm2_bias,
    expand_weight,
    expand_bias,
    reduce_weight,
    reduce_bias,
    layer_scale2,
    cotangent,
):
    me = lax.axis_index("dp").astype(jnp.int32).reshape(1)

    def turned(weight):
        return jnp.transpose(weight, (1, 2, 0)).reshape(-1, weight.shape[0])

    small, *x_blocks = first_kernel(
        me,
        block_input.reshape(SHARD, -1),
        (
            turned(gate_weight3),
            turned(gate_weight2),
            turned(gate_weight1),
            turned(conv_weight),
            norm1_gain,
            norm1_bias,
            input_bias,
            conv_bias,
            gate_bias1,
            gate_bias2,
            gate_bias3,
            output_bias,
            layer_scale1,
            norm2_gain,
            norm2_bias,
            reduce_bias,
            layer_scale2,
            expand_bias,
        ),
    )
    in_shards = gather(turned(input_weight))
    slabs = gather(small)
    x_blocks = exchange(x_blocks)
    dy_blocks = to_pixels(me, cotangent.reshape(SHARD, -1))
    x_blocks, dy_blocks, late_weights = hold(
        x_blocks,
        dy_blocks,
        (turned(output_weight), turned(expand_weight), reduce_weight.reshape(-1, WIDTH)),
    )
    out_shards = gather(late_weights[0])
    dy_blocks = exchange(dy_blocks)
    expand_shards = gather(late_weights[1])
    reduce_shards = gather(late_weights[2])

    vec, expand, w1, w1_back, w2, w3, w_in, taps, perm = prepare(me, slabs, in_shards)
    x, z1, u, dwv = front(x_blocks, perm, vec, w_in, taps)
    w_out = join_output(me, out_shards)
    z2 = branch_forward(dwv, x, vec, w1, w2, w3, w_out)
    order = (1, 3, 0, 2)
    expand_tiles = jnp.concatenate([expand[8 * k : 8 * k + 8] for k in order], axis=0)
    dy, f, dz, se, sr, ke, kr, bias_grads = feed_forward(
        z2, dy_blocks, perm, vec, expand_tiles, [expand_shards[k] for k in order], [reduce_shards[k] for k in order]
    )

    got_e, got_r = swap(se, CORE_SWAP), swap(sr, CORE_SWAP)
    on_e, on_r = onward(ke, got_e), onward(kr, got_r)
    dz, on_e, on_r = hold(dz, on_e, on_r)
    other_e, other_r = swap(on_e, CHIP_SWAP), swap(on_r, CHIP_SWAP)
    *outs, g, dx1, sib, keep_late = branch_backward(
        me, dwv, x, dy, f, dz, vec, w1, w1_back, w2, w3, w_out, perm, bias_grads
    )
    got_late = swap(sib, CORE_SWAP)
    g, other_e, got_late = hold(g, other_e, got_late)
    trade_e = own_sum(ke, got_e, other_e, mp_count)
    on_late = onward(keep_late, got_late)
    g, trade_e, on_late = hold(g, trade_e, on_late)
    trade_e = trade(trade_e)
    other_late = swap(on_late, CHIP_SWAP)
    outs = exchange(outs)
    du_high, sib, keep_high = conv_backward(me, g, u, taps, z1, 4)
    got_high = swap(sib, CORE_SWAP)
    du_high, other_r, trade_e, other_late, got_high = hold(du_high, other_r, trade_e, other_late, got_high)
    trade_r = own_sum(kr, got_r, other_r, mp_count)
    trade_late = own_sum(keep_late, got_late, other_late, mp_count)
    on_high = onward(keep_high, got_high)
    spread_e = spread_sum(trade_e)
    g, trade_r, trade_late, on_high, spread_e = hold(g, trade_r, trade_late, on_high, spread_e)
    trade_r, trade_late, spread_e = trade(trade_r), trade(trade_late), trade(spread_e)
    other_high = swap(on_high, CHIP_SWAP)
    du_low, sib, keep_low = conv_backward(me, g, u, taps, z1, 0)
    got_low = swap(sib, CORE_SWAP)
    du_low, trade_r, trade_late, other_high, got_low = hold(du_low, trade_r, trade_late, other_high, got_low)
    trade_high = own_sum(keep_high, got_high, other_high, mp_count)
    on_low = onward(keep_low, got_low)
    spread_r, spread_late = spread_sum(trade_r), spread_sum(trade_late)
    du_low, trade_high, on_low, spread_r, spread_late = hold(du_low, trade_high, on_low, spread_r, spread_late)
    trade_high, spread_r, spread_late = trade(trade_high), trade(spread_r), trade(spread_late)
    other_low = swap(on_low, CHIP_SWAP)
    *ins, sib, keep_last = input_backward(me, du_low, du_high, x, dx1, vec, w_in, perm)
    got_last = swap(sib, CORE_SWAP)
    other_last = swap(onward(keep_last, got_last), CHIP_SWAP)
    ins = exchange(ins)
    trade_low = trade(own_sum(keep_low, got_low, other_low, mp_count))
    trade_last = trade(own_sum(keep_last, got_last, other_last, mp_count))
    spread_high, spread_low, spread_last = (
        trade(spread_sum(trade_high)),
        trade(spread_sum(trade_low)),
        trade(spread_sum(trade_last)),
    )

    def back(values, blocks):
        return jnp.transpose(values.reshape(blocks, 16, values.shape[1]), (2, 0, 1))

    (
        g1, g2, g3, gconv, gout, gin, gb1, gb2, gb3, gob, gls1, gn2g, gn2b, grb, gls2, geb, ginb, gcb, gn1g, gn1b,
    ) = unpack_small(flat(spread_late), flat(spread_high), flat(spread_low), flat(spread_last))
    block_output = from_pixels(me, outs).reshape(block_input.shape)
    input_grad = from_pixels(me, ins).reshape(block_input.shape)
    return (
        block_output,
        input_grad,
        gn1g,
        gn1b,
        back(gin, 16),
        ginb,
        back(gconv, 15),
        gcb,
        back(g1, 2),
        gb1,
        back(g2, 4),
        gb2,
        back(g3, 8),
        gb3,
        back(gout, 8),
        gob,
        gls1,
        gn2g,
        gn2b,
        back(flat(spread_e).astype(FULL), 32),
        geb,
        flat(spread_r).astype(FULL).reshape(32, 16, WIDTH),
        grb,
        gls2,
    )


def solution(mesh):
    pixels = P(None, "dp", "mp")
    vector = P(None, "dp")
    matrix = P(None, None, "dp")
    params = (
        vector, vector, matrix, vector, matrix, vector, matrix, vector, matrix, vector, matrix, vector,
        matrix, vector, vector, vector, vector, matrix, vector, P(None, "dp", None), vector, vector,
    )
    return jax.shard_map(
        partial(per_device, mesh.shape["mp"]),
        mesh=mesh,
        in_specs=(pixels,) + params + (pixels,),
        out_specs=(pixels, pixels) + params,
        check_vma=False,
    )
```

```python
from functools import partial

import jax
import jax.numpy as jnp
from jax import lax
from jax.experimental import pallas as pl
from jax.experimental.pallas import tpu as pltpu
from jax.sharding import PartitionSpec as P

WIDTH = 512
GROUP = 64
SIDE = 14
CROP = SIDE * SIDE
CROPS = 8
TOKENS = CROP * CROPS
SHARD = 128
TAPS = 49
EPSILON = 1e-06
LOW = jnp.bfloat16
FULL = jnp.float32
VMEM = 58 * 1024 * 1024

NN = (((1,), (0,)), ((), ()))
NT = (((1,), (1,)), ((), ()))
TN = (((0,), (0,)), ((), ()))

CORE_SWAP = [(0, 1), (1, 0), (2, 3), (3, 2)]
CHIP_SWAP = [(0, 2), (2, 0), (1, 3), (3, 1)]
BOTH_SWAP = [(0, 3), (3, 0), (1, 2), (2, 1)]

S_GATE3, S_GATE2, S_GATE1, S_CONV, S_EXPAND, S_ROWS = 0, 256, 320, 352, 560, 592
S_LANE = 64
(V_N1G, V_N1B, V_INB, V_CB, V_GB1, V_GB2, V_GB3, V_OB, V_LS1, V_N2G, V_N2B, V_RB, V_LS2) = range(13)
VECTORS = 13
E_OUT, E_VEC, E_EXPAND, E_ROWS = 0, 352 + 512, 496 + 512, 640 + 512
E_GATE = 512


def mm(left, right, dims=NN):
    return lax.dot_general(left, right, dims, preferred_element_type=FULL)


def call(body, out, weight=1.0, **kwargs):
    flops, moved = int(weight * 1.15e9 / 4), 1 << 10
    return pl.pallas_call(
        body,
        out_shape=out,
        compiler_params=pltpu.CompilerParams(vmem_limit_bytes=VMEM),
        cost_estimate=pl.CostEstimate(flops=flops, bytes_accessed=moved, transcendentals=0),
        **kwargs,
    )


def struct(shape, dtype):
    return jax.ShapeDtypeStruct(shape, dtype)


SMEM_SPEC = pl.BlockSpec(memory_space=pltpu.SMEM)


def whole(shape):
    return pl.BlockSpec(shape, lambda i: (0,) * len(shape))


def turn_blocks(me, x_ref, outs, wide, blocks):
    lanes = x_ref.shape[1]
    for dest in range(4):
        for crop in range(CROPS):
            start = CROP * (CROPS * dest + crop)
            base = start // 128 * 128
            window = x_ref[:, base : base + min(lanes - base, 384)].astype(FULL)
            wide[pl.ds(crop, CROP, stride=CROPS), :] = window[:, start - base : start - base + CROP].T
        blocks[dest ^ me] = wide[...].astype(LOW)
    for k in range(4):
        outs[k][...] = blocks[k]


PIXEL_SCRATCH = [pltpu.VMEM((TOKENS, SHARD), FULL), pltpu.VMEM((4, TOKENS, SHARD), LOW)]


def second_body(me_ref, x_ref, w_out, expand, reduce, *refs):
    weights = refs[4]
    weights[0:128, :] = w_out[...]
    weights[128:640, :] = expand[...]
    weights[640:1152, :] = reduce[...]
    turn_blocks(me_ref[0], x_ref, refs[:4], refs[5], refs[6])


def second_kernel(me, x, w_out, expand, reduce):
    *blocks, weights = call(
        second_body,
        (struct((TOKENS, SHARD), LOW),) * 4 + (struct((1152, 512), LOW),),
        weight=5.0,
        in_specs=[SMEM_SPEC] + [pl.BlockSpec(memory_space=pltpu.VMEM)] * 4,
        scratch_shapes=PIXEL_SCRATCH,
    )(me, x, w_out, expand, reduce)
    return blocks, weights


def first_body(me_ref, x_ref, *refs):
    pack_body(*refs[:18], refs[18], refs[23])
    turn_blocks(me_ref[0], x_ref, refs[19:23], refs[24], refs[25])


def first_kernel(me, x, small):
    return call(
        first_body,
        (struct((S_ROWS, 128), LOW),) + (struct((TOKENS, SHARD), LOW),) * 4,
        in_specs=[SMEM_SPEC] + [pl.BlockSpec(memory_space=pltpu.VMEM)] * 19,
        scratch_shapes=[pltpu.VMEM((S_ROWS, 128), FULL)] + PIXEL_SCRATCH,
    )(me, x, *small)


def from_pixels_body(me_ref, *refs):
    ins, out_ref, wide, blocks = refs[:4], refs[4], refs[5], refs[6]
    me = me_ref[0]
    for k in range(4):
        blocks[k ^ me] = ins[k][...]
    for source in range(4):
        wide[...] = blocks[source].astype(FULL)
        for crop in range(CROPS):
            start = CROP * (CROPS * source + crop)
            part = wide[pl.ds(crop, CROP, stride=CROPS), :].T
            out_ref[:, start : start + CROP] = part.astype(LOW)


def from_pixels(me, blocks):
    return call(
        from_pixels_body,
        struct((SHARD, 4 * TOKENS), LOW),
        weight=4.0,
        in_specs=[SMEM_SPEC] + [pl.BlockSpec(memory_space=pltpu.VMEM)] * 4,
        scratch_shapes=[pltpu.VMEM((TOKENS, SHARD), FULL), pltpu.VMEM((4, TOKENS, SHARD), LOW)],
    )(me, *blocks)


def pack_body(g3, g2, g1, conv, *refs):
    vectors, expand, out_ref, slab = refs[:VECTORS], refs[VECTORS], refs[VECTORS + 1], refs[VECTORS + 2]
    slab[...] = jnp.zeros_like(slab)
    slab[S_GATE3 : S_GATE3 + 128, :] = g3[:, :128].astype(FULL)
    slab[S_GATE3 + 128 : S_GATE3 + 256, :] = g3[:, 128:].astype(FULL)
    slab[S_GATE2 : S_GATE2 + 64, :] = g2[...].astype(FULL)
    slab[S_GATE1 : S_GATE1 + 32, :GROUP] = g1[...].astype(FULL)
    slab[S_CONV : S_CONV + 240, :TAPS] = conv[...].astype(FULL)
    for number, ref in enumerate(vectors):
        first = S_CONV + 16 * number + (1 if number == V_CB else 0)
        slab[first : first + ref.shape[0], S_LANE : S_LANE + 16] = ref[...].astype(FULL)
    slab[S_EXPAND : S_EXPAND + 32, S_LANE : S_LANE + 16] = expand[...].astype(FULL).T
    out_ref[...] = slab[...].astype(LOW)


def iota(shape, dim):
    return lax.broadcasted_iota(jnp.int32, shape, dim)


def spread(lanes):
    return jnp.where(iota((128, lanes), 1) % 16 + S_LANE == iota((128, lanes), 0), 1.0, 0.0).astype(LOW)


def prepare_body(me_ref, *refs):
    slabs, ins = refs[0:4], refs[4:8]
    vec, expand, w1, w1_back, w2, w3, w_in, taps, perm, channels = refs[8:]
    me = me_ref[0]
    totals = jnp.zeros((VECTORS, 1024), FULL)
    spread_wide = spread(1024)
    row = iota((VECTORS * 16, 1024), 0) % 16
    lane = iota((VECTORS * 16, 1024), 1)
    in_row = row == lane // 64
    spread_expand = spread(512)
    expand_rows = iota((32, 512), 0) == iota((32, 512), 1) // 16
    w1[...] = jnp.zeros_like(w1)
    channels[0:GROUP, :] = jnp.where(iota((GROUP, 128), 1) == TAPS // 2, 3.0, 0.0)
    for k in range(4):
        source = me ^ k
        slab = slabs[k]
        values = mm(slab[S_CONV : S_CONV + VECTORS * 16, :], spread_wide)
        values = jnp.where(in_row & (lane // 16 % 4 == source), values, 0.0)
        totals = totals + jnp.sum(values.reshape(VECTORS, 16, 1024), axis=1)
        values = mm(slab[S_EXPAND : S_EXPAND + 32, :], spread_expand)
        values = jnp.sum(jnp.where(expand_rows, values, 0.0), axis=0, keepdims=True)
        expand[8 * k : 8 * k + 8, :] = jnp.broadcast_to(values, (8, 512))
        for a in range(16):
            place = pl.ds(pl.multiple_of(a * 64 + source * 16, 16), 16)
            rows = slice(a * 16, a * 16 + 16)
            w_in[place, :] = ins[k][rows, :]
            if a < 15:
                later = pl.ds(pl.multiple_of((a + 1) * 64 + source * 16, 16), 16)
                channels[later, :] = slab[S_CONV + a * 16 : S_CONV + a * 16 + 16, :].astype(FULL)
            if a < 8:
                w3[place, 0:128] = slab[S_GATE3 + a * 16 : S_GATE3 + a * 16 + 16, :]
                w3[place, 128:256] = slab[S_GATE3 + 128 + a * 16 : S_GATE3 + 128 + a * 16 + 16, :]
            if a < 4:
                w2[place, :] = slab[S_GATE2 + a * 16 : S_GATE2 + a * 16 + 16, :]
            if a < 2:
                w1[place, :] = slab[S_GATE1 + a * 16 : S_GATE1 + a * 16 + 16, :]
        column = iota((SHARD, WIDTH), 0)
        target = column // 16 * 64 + source * 16 + column % 16
        perm[k * SHARD : (k + 1) * SHARD, :] = jnp.where(iota((SHARD, WIDTH), 1) == target, 1.0, 0.0).astype(LOW)
    vec[0:VECTORS, :] = totals
    vec[VECTORS:16, :] = jnp.zeros((16 - VECTORS, 1024), FULL)
    single = w1[...].astype(FULL)
    w1_back[...] = (single + pltpu.roll(single, GROUP, 1)).astype(LOW)
    taps[...] = channels[...].T[0:64, :]


def prepare(me, slabs, ins):
    return call(
        prepare_body,
        (
            struct((16, 1024), FULL),
            struct((32, 512), FULL),
            struct((128, 128), LOW),
            struct((128, 128), LOW),
            struct((256, 128), LOW),
            struct((512, 256), LOW),
            struct((1024, 512), LOW),
            struct((64, 1024), FULL),
            struct((512, 512), LOW),
        ),
        weight=4.0,
        in_specs=[SMEM_SPEC] + [pl.BlockSpec(memory_space=pltpu.VMEM)] * 8,
        scratch_shapes=[pltpu.VMEM((1024, 128), FULL)],
    )(me, *slabs, *ins)


def join_output_body(me_ref, r0, r1, r2, r3, out):
    me = me_ref[0]
    for k, ref in enumerate((r0, r1, r2, r3)):
        for a in range(8):
            place = pl.ds(pl.multiple_of(a * 64 + (me ^ k) * 16, 16), 16)
            out[place, :] = ref[a * 16 : a * 16 + 16, :]


def join_output(me, shards):
    return call(
        join_output_body,
        struct((512, 512), LOW),
        grid=(1,),
        in_specs=[SMEM_SPEC] + [pl.BlockSpec((128, 512), lambda i: (0, 0))] * 4,
        out_specs=whole((512, 512)),
    )(me, *shards)


def normed(values):
    center = jnp.sum(values, axis=1, keepdims=True) * (1.0 / WIDTH)
    away = values - center
    spread_sq = jnp.sum(away * away, axis=1, keepdims=True) * (1.0 / WIDTH)
    inverse = lax.rsqrt(spread_sq + EPSILON)
    return away * inverse, inverse


def norm_back(grad, unit, inverse, gain):
    grad_unit = grad * gain
    first = jnp.sum(grad_unit, axis=1, keepdims=True) * (1.0 / WIDTH)
    second = jnp.sum(grad_unit * unit, axis=1, keepdims=True) * (1.0 / WIDTH)
    return inverse * (grad_unit - first - unit * second)


def total(values):
    return jnp.sum(values, axis=0, keepdims=True)


def row(vec, number, lanes=WIDTH):
    return vec[number : number + 1, 0:lanes]


def rows_spec(tile, lanes):
    return pl.BlockSpec((tile, lanes), lambda i: (i, 0))


def chunks(count, size, body):
    def step(i, carry):
        body(pl.ds(pl.multiple_of(i * size, size), size))
        return carry

    lax.fori_loop(0, count // size, step, 0)


NORM_ROWS = 224
HALVES = (slice(0, TOKENS // 2), slice(TOKENS // 2, TOKENS))


def join(blocks, perm, rows):
    return mm(jnp.concatenate([r[rows, :] for r in blocks], axis=1), perm[...])


def conv_rows(source, weights, emit, flip):
    def one_row(i, carry):
        def one_tap_row(r, sums):
            base = (i + r - 3) * SIDE
            values = [source[base + c] for c in range(SIDE)]
            first = (6 - r) * 7 if flip else r * 7
            taps = [weights[first + (6 - s if flip else s)] for s in range(7)]
            sums = list(sums)
            for s in range(7):
                for c in range(SIDE):
                    if 0 <= c + s - 3 < SIDE:
                        sums[c] = sums[c] + taps[s] * values[c + s - 3]
            return tuple(sums)

        zero = jnp.zeros((CROPS, 128), FULL)
        sums = lax.fori_loop(
            jnp.maximum(0, 3 - i), jnp.minimum(7, 17 - i), one_tap_row, (zero,) * SIDE
        )
        emit(i, sums)
        return carry

    lax.fori_loop(0, SIDE, one_row, 0)


def wide_taps(taps, weights):
    for tap in range(TAPS):
        weights[tap] = jnp.broadcast_to(taps[tap : tap + 1, :], (CROPS, 128))


PIXEL_BLOCK = pl.BlockSpec((CROP, CROPS, 128), lambda i: (0, 0, i))


def lane_block(rows):
    return pl.BlockSpec((rows, 128), lambda i: (0, i))


def front_body(r0, r1, r2, r3, perm, vec, w_in, taps, vec_part, x, z, u, dwv, weights):
    @pl.when(pl.program_id(0) == 0)
    def _():
        for rows in HALVES:
            x[rows, :] = join((r0, r1, r2, r3), perm, rows).astype(LOW)

        def norm_rows(rows):
            unit, _ = normed(x[rows, :].astype(FULL))
            z[rows, :] = (unit * row(vec, V_N1G) + row(vec, V_N1B)).astype(LOW)

        chunks(TOKENS, NORM_ROWS, norm_rows)

    wide_taps(taps, weights)
    values = mm(z[...], w_in[...], NT) + vec_part[V_INB : V_INB + 1, :]
    u[...] = values.reshape(CROP, CROPS, 128)
    bias = jnp.broadcast_to(vec_part[V_CB : V_CB + 1, :], (CROPS, 128))

    def emit(i, sums):
        for c in range(SIDE):
            dwv[i * SIDE + c] = (sums[c] + bias) * (1.0 / 3.0)

    conv_rows(u, weights, emit, False)


def front(blocks, perm, vec, w_in, taps):
    pixels = struct((CROP, CROPS, 1024), FULL)
    rows = struct((TOKENS, WIDTH), LOW)
    x, z, u, dwv = call(
        front_body,
        (rows, rows, pixels, pixels),
        weight=28.0,
        grid=(8,),
        in_specs=[whole((TOKENS, SHARD))] * 4
        + [
            whole((512, 512)),
            whole((16, 1024)),
            pl.BlockSpec((128, 512), lambda i: (i, 0)),
            lane_block(64),
            lane_block(16),
        ],
        out_specs=(whole((TOKENS, WIDTH)), whole((TOKENS, WIDTH)), PIXEL_BLOCK, PIXEL_BLOCK),
        scratch_shapes=[pltpu.VMEM((TAPS, CROPS, 128), FULL)],
    )(*blocks, perm, vec, w_in, taps, vec)
    return x, z, u, dwv.reshape(TOKENS, 1024)


def gate_chain(dwv, vec, w1, w2, w3):
    first = dwv[:, 0:128]
    turned = pltpu.roll(first, GROUP, 1)
    q0 = (first * turned).astype(LOW)
    t1 = mm(q0, w1[...], NT) + row(vec, V_GB1, 128)
    q1 = (t1 * dwv[:, 128:256]).astype(LOW)
    t2 = mm(q1, w2[...], NT) + row(vec, V_GB2, 256)
    q2 = (t2 * dwv[:, 256:512]).astype(LOW)
    t3 = mm(q2, w3[...], NT) + row(vec, V_GB3, 512)
    q3 = (t3 * dwv[:, 512:1024]).astype(LOW)
    return turned, (q0, q1, q2, q3), (t1, t2, t3)


def branch_body(dwv, x, vec, w1, w2, w3, w_out, z_out):
    _, orders, _ = gate_chain(dwv[...], vec, w1, w2, w3)
    branch = mm(orders[3], w_out[...], NT) + row(vec, V_OB)
    middle = x[...].astype(FULL) + row(vec, V_LS1) * branch
    unit, _ = normed(middle)
    z_out[...] = (unit * row(vec, V_N2G) + row(vec, V_N2B)).astype(LOW)


def branch_forward(dwv, x, vec, w1, w2, w3, w_out, tile=784):
    return call(
        branch_body,
        struct((TOKENS, WIDTH), LOW),
        weight=7.0,
        grid=(TOKENS // tile,),
        in_specs=[
            rows_spec(tile, 1024),
            rows_spec(tile, WIDTH),
            whole((16, 1024)),
            whole((128, 128)),
            whole((256, 128)),
            whole((512, 256)),
            whole((512, 512)),
        ],
        out_specs=rows_spec(tile, WIDTH),
    )(dwv, x, vec, w1, w2, w3, w_out)


def gelu_parts(s):
    bell = jnp.exp2((-0.5 * 1.4426950408889634) * (s * s))
    size = jnp.abs(s)
    t = pltpu.reciprocal(1.0 + (0.3275911 * 0.7071067811865476) * size, approx=True)
    poly = 0.5 * 1.061405429
    for coefficient in (-1.453152027, 1.421413741, -0.284496736, 0.254829592):
        poly = poly * t + 0.5 * coefficient
    tail = poly * t * bell
    cdf = jnp.where(s >= 0.0, 1.0 - tail, tail)
    return s * cdf, cdf + s * (bell * 0.3989422804014327)


PIECE = 16


def mlp_body(z, r0, r1, r2, r3, perm, vec, expand, *refs):
    shards = refs[0:4]
    dy, f, dz, sibling, keep, gb = refs[4:10]
    we, wr, df, s0, s1, g0, g1, h0, h1, d0, d1, acc_e, acc_r, sums, sem_e, sem_r = refs[10:]
    pre, grad_h, hid, grad_s = (s0, s1), (g0, g1), (h0, h1), (d0, d1)
    half = TOKENS // 2
    for slot in range(4):
        pltpu.make_async_copy(shards[slot].at[pl.ds(128, 512)], we.at[slot], sem_e.at[slot]).start()
        pltpu.make_async_copy(shards[slot].at[pl.ds(640, 512)], wr.at[slot], sem_r.at[slot]).start()

    def arrived(slot):
        pltpu.make_async_copy(we.at[slot], we.at[slot], sem_e.at[slot]).wait()
        pltpu.make_async_copy(wr.at[slot], wr.at[slot], sem_r.at[slot]).wait()

    for rows in HALVES:
        dy[rows, :] = join((r0, r1, r2, r3), perm, rows).astype(LOW)

    def scaled(rows):
        df[rows, :] = (dy[rows, :].astype(FULL) * row(vec, V_LS2)).astype(LOW)
        f[rows, :] = jnp.zeros((112, WIDTH), FULL)
        dz[rows, :] = jnp.zeros((112, WIDTH), FULL)

    chunks(TOKENS, 112, scaled)
    acc_e[...] = jnp.zeros_like(acc_e)
    acc_r[...] = jnp.zeros_like(acc_r)
    sums[...] = jnp.zeros_like(sums)
    h1[...] = jnp.zeros_like(h1)
    d1[...] = jnp.zeros_like(d1)
    arrived(0)
    s0[...] = mm(z[HALVES[0], :], we[0], NT)
    g0[...] = mm(df[HALVES[0], :], wr[0], NT)
    pieces = half // PIECE

    def unit(here, tile, before, after):
        there = 1 - here
        rows = HALVES[there]
        bias = expand[pl.ds(pl.multiple_of(tile * 8, 8), 1), :]
        done = [0]
        column = [jnp.zeros((8, 512), FULL)]

        def some(part):
            while done[0] < pieces * part // 6:
                piece = slice(done[0] * PIECE, (done[0] + 1) * PIECE)
                act, slope = gelu_parts(pre[here][piece, :] + bias)
                hid[here][piece, :] = act.astype(LOW)
                grad = (grad_h[here][piece, :] * slope).astype(LOW)
                grad_s[here][piece, :] = grad
                grad = grad.astype(FULL)
                column[0] = column[0] + (grad[0:8] + grad[8:16])
                done[0] += 1

        f[rows, :] += mm(hid[there][...], wr[before])
        some(1)
        dz[rows, :] += mm(grad_s[there][...], we[before])
        some(2)
        acc_e[before] += mm(grad_s[there][...], z[rows, :], TN)
        some(3)
        acc_r[before] += mm(hid[there][...], df[rows, :], TN)
        some(4)
        pre[there][...] = mm(z[rows, :], we[after], NT)
        some(5)
        grad_h[there][...] = mm(df[rows, :], wr[after], NT)
        some(6)
        sums[tile] += column[0]

    def one_tile(tile, carry):
        unit(0, tile, jnp.maximum(tile - 1, 0), tile)

        @pl.when(tile < 3)
        def _():
            arrived(tile + 1)

        unit(1, tile, tile, jnp.minimum(tile + 1, 3))
        return carry

    lax.fori_loop(0, 4, one_tile, 0)
    rows = HALVES[1]
    f[rows, :] += mm(h1[...], wr[3])
    dz[rows, :] += mm(d1[...], we[3])
    acc_e[3] += mm(d1[...], z[rows, :], TN)
    acc_r[3] += mm(h1[...], df[rows, :], TN)
    for pair, out in enumerate((sibling, keep)):
        for number in range(2):
            out[number, 0:512, :] = acc_e[2 * pair + number].astype(LOW)
            out[number, 512:1024, :] = acc_r[2 * pair + number].astype(LOW)
    for tile in range(4):
        gb[8 * tile : 8 * tile + 8, :] = sums[tile]


def feed_forward(z, blocks, perm, vec, expand, shards):
    vmem = pl.BlockSpec(memory_space=pltpu.VMEM)
    anywhere = pl.BlockSpec(memory_space=pl.ANY)
    half = TOKENS // 2
    pair = struct((2, 1024, 512), LOW)
    rows = struct((TOKENS, WIDTH), FULL)
    return call(
        mlp_body,
        (struct((TOKENS, WIDTH), LOW), rows, rows, pair, pair, struct((32, 512), FULL)),
        weight=40.0,
        in_specs=[vmem] * 8 + [anywhere] * 4,
        scratch_shapes=[pltpu.VMEM((4, 512, 512), LOW)] * 2
        + [pltpu.VMEM((TOKENS, WIDTH), LOW)]
        + [pltpu.VMEM((half, 512), FULL)] * 4
        + [pltpu.VMEM((half, 512), LOW)] * 4
        + [pltpu.VMEM((4, 512, 512), FULL)] * 2
        + [pltpu.VMEM((4, 8, 512), FULL)]
        + [pltpu.SemaphoreType.DMA((4,))] * 2,
    )(z, *blocks, perm, vec, expand, *shards)


def pack_vectors(values, count, source):
    lane = iota((count * 16, 1024), 1)
    keep = (iota((count * 16, 1024), 0) % 16 == lane // 64) & (lane // 16 % 4 == source)
    tall = jnp.broadcast_to(values[:, None, :], (count, 16, 1024)).reshape(count * 16, 1024)
    gather = jnp.where(iota((1024, 128), 0) % 16 == iota((1024, 128), 1), 1.0, 0.0).astype(LOW)
    return mm(jnp.where(keep, tall, 0.0).astype(LOW), gather)


def part_pair(parts, sibling, keep):
    sibling[0] = parts[1]
    sibling[1] = parts[3]
    keep[0] = parts[0]
    keep[1] = parts[2]


def branch_back_body(steps, me_ref, dwv, x, dy, f, dz, vec, w1, w1_back, w2, w3, w_out, perm, gb, *refs):
    (o0, o1, o2, o3, g_out, dx_out, sibling, keep) = refs[0:8]
    acc_o, acc_3, acc_2, acc_1, sums, parts = refs[8:]
    step = pl.program_id(0)
    values = dwv[...]
    turned, orders, gates = gate_chain(values, vec, w1, w2, w3)
    branch = mm(orders[3], w_out[...], NT) + row(vec, V_OB)
    middle = x[...].astype(FULL) + row(vec, V_LS1) * branch
    unit, inverse = normed(middle)
    top = dy[...].astype(FULL)
    mlp = f[...] + row(vec, V_RB)
    output = (middle + row(vec, V_LS2) * mlp).astype(LOW)
    blocks = mm(output, perm[...], NT).astype(LOW)
    for k, ref in enumerate((o0, o1, o2, o3)):
        ref[...] = blocks[:, k * SHARD : (k + 1) * SHARD]
    grad = dz[...]
    middle_grad = top + norm_back(grad, unit, inverse, row(vec, V_N2G))
    dx_out[...] = middle_grad
    grad_branch = (middle_grad * row(vec, V_LS1)).astype(LOW)
    grad_o = mm(grad_branch, orders[3], TN)
    back = mm(grad_branch, w_out[...])
    gt3 = (back * values[:, 512:1024]).astype(LOW)
    g_out[:, 512:1024] = back * gates[2] * (1.0 / 3.0)
    grad_3 = mm(gt3, orders[2], TN)
    back = mm(gt3, w3[...])
    gt2 = (back * values[:, 256:512]).astype(LOW)
    g_out[:, 256:512] = back * gates[1] * (1.0 / 3.0)
    grad_2 = mm(gt2, orders[1], TN)
    back = mm(gt2, w2[...])
    gt1 = (back * values[:, 128:256]).astype(LOW)
    g_out[:, 128:256] = back * gates[0] * (1.0 / 3.0)
    grad_1 = mm(gt1, orders[0], TN)
    back = mm(gt1, w1_back[...])
    g_out[:, 0:128] = back * turned * (1.0 / 3.0)

    @pl.when(step == 0)
    def _():
        acc_o[...] = jnp.zeros_like(acc_o)
        acc_3[...] = jnp.zeros_like(acc_3)
        acc_2[...] = jnp.zeros_like(acc_2)
        acc_1[...] = jnp.zeros_like(acc_1)
        sums[...] = jnp.zeros_like(sums)

    acc_o[...] += grad_o
    acc_3[...] += grad_3
    acc_2[...] += grad_2
    acc_1[...] += grad_1
    sums[0:1, 0:128] += total(gt1.astype(FULL))
    sums[1:2, 0:256] += total(gt2.astype(FULL))
    sums[2:3, 0:512] += total(gt3.astype(FULL))
    sums[3:4, 0:512] += total(grad_branch.astype(FULL))
    sums[4:5, 0:512] += total(middle_grad * branch)
    sums[5:6, 0:512] += total(grad * unit)
    sums[6:7, 0:512] += total(grad)
    sums[7:8, 0:512] += total(top) * row(vec, V_LS2)
    sums[8:9, 0:512] += total(top * mlp)

    @pl.when(step == steps - 1)
    def _():
        me = me_ref[0]
        vectors = sums[0:9, :]
        expand_rows = iota((32, 512), 0) == iota((32, 512), 1) // 16
        gather = jnp.where(iota((512, 128), 0) % 16 == iota((512, 128), 1), 1.0, 0.0).astype(LOW)
        for source in range(4):
            k = source ^ me
            for a in range(8):
                rows = slice(a * 64 + source * 16, a * 64 + source * 16 + 16)
                for part in range(4):
                    first = part * 128 + a * 16
                    parts[k, first : first + 16, :] = acc_o[rows, part * 128 : part * 128 + 128].astype(LOW)
                first = E_GATE + a * 16
                parts[k, first : first + 16, :] = acc_3[rows, 0:128].astype(LOW)
                parts[k, first + 128 : first + 144, :] = acc_3[rows, 128:256].astype(LOW)
                if a < 4:
                    parts[k, first + 256 : first + 272, :] = acc_2[rows, :].astype(LOW)
                if a < 2:
                    parts[k, first + 320 : first + 336, :] = acc_1[rows, :].astype(LOW)
            parts[k, E_VEC : E_VEC + 144, :] = pack_vectors(vectors, 9, source).astype(LOW)
        for k in range(4):
            slot = (2, 0, 3, 1)[k]
            line = total(gb[8 * slot : 8 * slot + 8, :])
            tall = jnp.where(expand_rows, jnp.broadcast_to(line, (32, 512)), 0.0)
            parts[k, E_EXPAND : E_EXPAND + 32, :] = mm(tall.astype(LOW), gather).astype(LOW)
            parts[k, E_EXPAND + 32 : E_ROWS, :] = jnp.zeros((E_ROWS - E_EXPAND - 32, 128), LOW)
        part_pair(parts, sibling, keep)


def branch_backward(me, dwv, x, dy, f, dz, vec, w1, w1_back, w2, w3, w_out, perm, biases, tile=224):
    steps = TOKENS // tile
    wide = rows_spec(tile, WIDTH)
    block = rows_spec(tile, SHARD)
    pair = (2, E_ROWS, 128)
    return call(
        partial(branch_back_body, steps),
        (struct((TOKENS, SHARD), LOW),) * 4
        + (
            struct((TOKENS, 1024), FULL),
            struct((TOKENS, WIDTH), FULL),
            struct(pair, LOW),
            struct(pair, LOW),
        ),
        weight=20.0,
        grid=(steps,),
        in_specs=[
            SMEM_SPEC,
            rows_spec(tile, 1024),
            wide,
            wide,
            wide,
            wide,
            whole((16, 1024)),
            whole((128, 128)),
            whole((128, 128)),
            whole((256, 128)),
            whole((512, 256)),
            whole((512, 512)),
            whole((512, 512)),
        ]
        + [whole((32, 512))],
        out_specs=(block,) * 4
        + (rows_spec(tile, 1024), wide, whole(pair), whole(pair)),
        scratch_shapes=[
            pltpu.VMEM((512, 512), FULL),
            pltpu.VMEM((512, 256), FULL),
            pltpu.VMEM((256, 128), FULL),
            pltpu.VMEM((128, 128), FULL),
            pltpu.VMEM((16, 1024), FULL),
            pltpu.VMEM((4, E_ROWS, 128), LOW),
        ],
    )(me, dwv, x, dy, f, dz, vec, w1, w1_back, w2, w3, w_out, perm, biases)


def conv_back_body(me_ref, g, u, taps, z, du, sibling, keep, weights, grad_taps, parts):
    step, steps = pl.program_id(0), pl.num_programs(0)
    me = me_ref[0]
    wide_taps(taps, weights)
    zero = jnp.zeros((CROPS, 128), FULL)

    def emit(i, sums):
        stacked = jnp.concatenate(list(sums), axis=0).astype(LOW)
        du[pl.ds(pl.multiple_of(i * SIDE * CROPS, 16), SIDE * CROPS), :] = stacked

    conv_rows(g, weights, emit, True)

    for r in range(7):

        def one_row(i, sums):
            grads = [g[i * SIDE + c] for c in range(SIDE)]
            values = [u[(i + r - 3) * SIDE + c] for c in range(SIDE)]
            sums = list(sums)
            for c in range(SIDE):
                for s in range(7):
                    if 0 <= c + s - 3 < SIDE:
                        sums[s] = sums[s] + grads[c] * values[c + s - 3]
            return tuple(sums)

        sums = lax.fori_loop(max(0, 3 - r), min(SIDE, SIDE + 3 - r), one_row, (zero,) * 7)
        for s in range(7):
            grad_taps[r * 7 + s : r * 7 + s + 1, :] = total(sums[s])
    grad_taps[49:50, :] = total(jnp.sum(g[...], axis=0))
    grad_taps[50:51, :] = total(du[...].astype(FULL))
    grad_taps[51:128, :] = jnp.zeros((77, 128), FULL)
    grad_w = mm(du[...], z[...], TN)
    tall = grad_taps[...].T.astype(LOW)
    for a in range(2):
        for source in range(4):
            k = source ^ me
            rows = slice(a * 64 + source * 16, a * 64 + source * 16 + 16)
            for part in range(4):
                place = pl.ds(pl.multiple_of(part * 64 + step * 32 + a * 16, 16), 16)
                parts[k, place, :] = grad_w[rows, part * 128 : part * 128 + 128].astype(LOW)
            place = pl.ds(pl.multiple_of(256 + step * 32 + a * 16, 16), 16)
            parts[k, place, :] = tall[rows, :]

    @pl.when(step == steps - 1)
    def _():
        part_pair(parts, sibling, keep)


C_ROWS = 320


def conv_backward(me, g, u, taps, z, base):
    pixels = pl.BlockSpec((CROP, CROPS, 128), lambda i: (0, 0, i + base))
    pair = (2, C_ROWS, 128)
    return call(
        conv_back_body,
        (struct((TOKENS, 256), LOW), struct(pair, LOW), struct(pair, LOW)),
        weight=12.0,
        grid=(2,),
        in_specs=[
            SMEM_SPEC,
            pixels,
            pixels,
            pl.BlockSpec((64, 128), lambda i: (0, i + base)),
            whole((TOKENS, WIDTH)),
        ],
        out_specs=(lane_block(TOKENS), whole(pair), whole(pair)),
        scratch_shapes=[
            pltpu.VMEM((TAPS, CROPS, 128), FULL),
            pltpu.VMEM((128, 128), FULL),
            pltpu.VMEM((4, C_ROWS, 128), LOW),
        ],
    )(me, g.reshape(CROP, CROPS, 1024), u, taps, z)


def input_back_body(steps, me_ref, du0, du1, du2, du3, x, dx, vec, w_in, perm, *refs):
    (o0, o1, o2, o3, e0, e1, e2, e3, sums, parts) = refs
    step = pl.program_id(0)
    unit, inverse = normed(x[...].astype(FULL))
    grad = mm(jnp.concatenate([du0[...], du1[...], du2[...], du3[...]], axis=1), w_in[...])
    grad_x = (dx[...] + norm_back(grad, unit, inverse, row(vec, V_N1G))).astype(LOW)
    blocks = mm(grad_x, perm[...], NT).astype(LOW)
    for k, ref in enumerate((o0, o1, o2, o3)):
        ref[...] = blocks[:, k * SHARD : (k + 1) * SHARD]

    @pl.when(step == 0)
    def _():
        sums[...] = jnp.zeros_like(sums)

    sums[0:1, 0:512] += total(grad * unit)
    sums[1:2, 0:512] += total(grad)

    @pl.when(step == steps - 1)
    def _():
        me = me_ref[0]
        vectors = sums[0:2, :]
        for source in range(4):
            parts[source ^ me, :, :] = pack_vectors(vectors, 2, source).astype(LOW)
        for k, ref in enumerate((e0, e1, e2, e3)):
            ref[...] = parts[k]


def input_backward(me, dus, x, dx, vec, w_in, perm, tile=224):
    steps = TOKENS // tile
    wide = rows_spec(tile, WIDTH)
    end = (32, 128)
    return call(
        partial(input_back_body, steps),
        (struct((TOKENS, SHARD), LOW),) * 4 + (struct(end, LOW),) * 4,
        weight=8.0,
        grid=(steps,),
        in_specs=[
            SMEM_SPEC,
            *[rows_spec(tile, 256)] * 4,
            wide,
            wide,
            whole((16, 1024)),
            whole((1024, 512)),
            whole((512, 512)),
        ],
        out_specs=(rows_spec(tile, SHARD),) * 4 + (whole(end),) * 4,
        scratch_shapes=[pltpu.VMEM((16, 1024), FULL), pltpu.VMEM((4, 32, 128), LOW)],
    )(me, *dus, x, dx, vec, w_in, perm)


def unpack_body(full, final, *refs):
    (g1, g2, g3, conv, w_out, w_in), late_refs, expand = refs[0:6], refs[6:15], refs[15]
    (in_bias, conv_bias, gain, bias), low = refs[16:20], refs[20]
    size = final.shape[1] - 32
    last = jnp.zeros((32, 128), FULL)
    for piece in range(final.shape[0]):
        low[piece * size : (piece + 1) * size, :] = final[piece, 0:size, :]
        last = last + final[piece, size : size + 32, :].astype(FULL)
    gates = full[E_GATE:E_VEC, :].astype(FULL)
    g3[:, 0:128] = gates[0:128]
    g3[:, 128:256] = gates[128:256]
    g2[...] = gates[256:320]
    g1[...] = gates[320:352, 0:GROUP]
    calls = (
        (low, 0),
        (low, C_ROWS),
        (full, E_ROWS),
        (full, E_ROWS + C_ROWS),
    )
    taps = []
    for j, (source, first) in enumerate(calls):
        for part in range(4):
            rows = slice(first + part * 64, first + part * 64 + 64)
            w_in[j * 64 : j * 64 + 64, part * 128 : part * 128 + 128] = source[rows, :].astype(FULL)
        taps.append(source[first + 256 : first + 320, :])
    for part in range(4):
        lanes = slice(part * 128, part * 128 + 128)
        w_out[:, lanes] = full[lanes, :].astype(FULL)
    taps = jnp.concatenate(taps, axis=0).astype(FULL)
    conv[...] = taps[16:256, 0:TAPS]
    vectors = full[E_VEC : E_VEC + 144, :].astype(FULL)
    for number, ref in enumerate(late_refs):
        ref[...] = vectors[16 * number : 16 * number + ref.shape[0], 0:16]
    expand[...] = full[E_EXPAND : E_EXPAND + 32, 0:16].astype(FULL).T
    gain[...] = last[0:8, 0:16]
    bias[...] = last[16:24, 0:16]
    own = jnp.where(iota((256, 16), 0) % 16 == iota((256, 16), 1), 1.0, 0.0)
    rows = jnp.where(iota((16, 256), 0) == iota((16, 256), 1) // 16, 1.0, 0.0).astype(LOW)
    conv_bias[...] = mm(rows, (taps[:, 49:50] * own).astype(LOW))[1:16, :]
    in_bias[...] = mm(rows, (taps[:, 50:51] * own).astype(LOW))


VMEM_SPEC = pl.BlockSpec(memory_space=pltpu.VMEM)


def unpack_small(full, final):
    vector = lambda rows: struct((rows, 16), FULL)
    return call(
        unpack_body,
        (struct((32, 64), FULL), struct((64, 128), FULL), struct((128, 256), FULL), struct((240, 49), FULL))
        + (struct((128, 512), FULL), struct((256, 512), FULL))
        + (vector(2), vector(4))
        + (vector(8),) * 7
        + (struct((16, 32), FULL), vector(16), vector(15), vector(8), vector(8)),
        in_specs=[VMEM_SPEC] * 2,
        scratch_shapes=[pltpu.VMEM((2 * C_ROWS, 128), LOW)],
    )(full, final)


def widen_body(values, out_e, out_r):
    out_e[...] = values[0:512, :].astype(FULL)
    out_r[...] = values[512:1024, :].astype(FULL)


def widen(values):
    return call(widen_body, (struct((512, 512), FULL),) * 2)(values)


class Slot:
    def __init__(self, where):
        self.where, self.jobs, self.args, self.specs, self.outs, self.scratch = where, [], [], [], [], []

    def add(self, body, args, specs, outs, scratch=()):
        first = (len(self.args), len(self.outs), len(self.scratch))
        self.jobs.append((body, first, (len(args), len(outs), len(scratch))))
        self.args += args
        self.specs += specs
        self.outs += outs
        self.scratch += scratch
        return slice(first[1], first[1] + len(outs))

    def onward(self, keeps, gots):
        def body(where, ins, outs, _):
            row = 0
            for keep, got in zip(ins[0::2], ins[1::2]):
                outs[0][row : row + keep.shape[1], :] = (keep[0].astype(FULL) + got[0].astype(FULL)).astype(LOW)
                row += keep.shape[1]

        args, specs = self.pairs(keeps, gots, 1)
        rows = sum(k.shape[1] for k in keeps)
        return self.add(body, args, specs, [struct((rows, keeps[0].shape[2]), LOW)])

    def pairs(self, keeps, gots, index):
        args, specs = [], []
        for keep, got in zip(keeps, gots):
            args += [keep, got]
            specs += [pl.BlockSpec((1,) + keep.shape[1:], lambda i: (index, 0, 0))] * 2
        return args, specs

    def own(self, keeps, gots, other):
        def body(where, ins, outs, _):
            row = 0
            for keep, got in zip(ins[0:-1:2], ins[1:-1:2]):
                rows = slice(row, row + keep.shape[1])
                value = keep[0].astype(FULL) + got[0].astype(FULL) + ins[-1][rows, :].astype(FULL)
                outs[0][rows, :] = value.astype(LOW)
                row += keep.shape[1]

        args, specs = self.pairs(keeps, gots, 0)
        return self.add(body, args + [other], specs + [VMEM_SPEC], [struct(other.shape, LOW)])

    def halves(self, keeps, gots, other):
        def body(where, ins, outs, scratch):
            row = 0
            for keep, got in zip(ins[0:-1:2], ins[1:-1:2]):
                rows = slice(row, row + keep.shape[1])
                value = keep[0].astype(FULL) + got[0].astype(FULL) + ins[-1][rows, :].astype(FULL)
                scratch[0][rows, :] = value.astype(LOW)
                row += keep.shape[1]
            size = row // 2
            bit = where[0] & 1
            outs[0][...] = scratch[0][pl.ds(pl.multiple_of((1 - bit) * size, 16), size), :]
            outs[1][...] = scratch[0][pl.ds(pl.multiple_of(bit * size, 16), size), :]

        args, specs = self.pairs(keeps, gots, 0)
        rows, lanes = other.shape
        half = struct((rows // 2, lanes), LOW)
        return self.add(body, args + [other], specs + [VMEM_SPEC], [half, half], [pltpu.VMEM((rows, lanes), LOW)])

    def both(self, stay, got):
        def body(where, ins, outs, _):
            outs[0][...] = (ins[0][...].astype(FULL) + ins[1][...].astype(FULL)).astype(LOW)

        return self.add(body, [stay, got], [VMEM_SPEC] * 2, [struct(stay.shape, LOW)])

    def spread(self, parts, ends=()):
        count, rows, lanes = parts.shape
        tail = ends[0].shape[0] if ends else 0

        def body(where, ins, outs, _):
            value = ins[0][0].astype(FULL)
            for number in range(1, count):
                value = value + ins[0][number].astype(FULL)
            value = value.astype(LOW)
            for number in range(count):
                outs[0][number, 0:rows, :] = value
            if ends:
                value = ins[1][...].astype(FULL)
                for end in ins[2:]:
                    value = value + end[...].astype(FULL)
                value = value.astype(LOW)
                for number in range(count):
                    outs[0][number, rows : rows + tail, :] = value

        out = struct((count, rows + tail, lanes), LOW)
        return self.add(body, [parts, *ends], [VMEM_SPEC] * (1 + len(ends)), [out])

    def run(self):
        counts = len(self.args), len(self.outs)

        def body(where, *refs):
            ins, outs, scratch = refs[: counts[0]], refs[counts[0] : sum(counts)], refs[sum(counts) :]
            for job, first, size in self.jobs:
                cut = [slice(f, f + n) for f, n in zip(first, size)]
                job(where, ins[cut[0]], outs[cut[1]], scratch[cut[2]])

        return call(
            body,
            tuple(self.outs),
            grid=(1,),
            in_specs=[SMEM_SPEC] + self.specs,
            out_specs=tuple([VMEM_SPEC] * len(self.outs)),
            scratch_shapes=self.scratch,
        )(self.where, *self.args)


def swap(values, pairs):
    return lax.ppermute(values, "dp", pairs)


def exchange(blocks):
    return (
        blocks[0],
        swap(blocks[1], CORE_SWAP),
        swap(blocks[2], CHIP_SWAP),
        swap(blocks[3], BOTH_SWAP),
    )


def gather(values):
    across = swap(values, CHIP_SWAP)
    return (values, swap(values, CORE_SWAP), across, swap(across, CORE_SWAP))


def hold(*values):
    return lax.optimization_barrier(values)


def trade(values, count, stride=1):
    parts = values.reshape(count // stride, -1, values.shape[-1])
    groups = [list(range(first, count, stride)) for first in range(stride)] if stride > 1 else None
    return lax.all_to_all(parts, "mp", split_axis=0, concat_axis=0, axis_index_groups=groups, tiled=True)


def flat(parts):
    return parts.reshape(-1, parts.shape[2])


def per_device(
    mp_count,
    block_input,
    norm1_gain,
    norm1_bias,
    input_weight,
    input_bias,
    conv_weight,
    conv_bias,
    gate_weight1,
    gate_bias1,
    gate_weight2,
    gate_bias2,
    gate_weight3,
    gate_bias3,
    output_weight,
    output_bias,
    layer_scale1,
    norm2_gain,
    norm2_bias,
    expand_weight,
    expand_bias,
    reduce_weight,
    reduce_bias,
    layer_scale2,
    cotangent,
):
    me = lax.axis_index("dp").astype(jnp.int32).reshape(1)

    def turned(weight):
        return jnp.transpose(weight, (1, 2, 0)).reshape(-1, weight.shape[0])

    small, *x_blocks = first_kernel(
        me,
        block_input.reshape(SHARD, -1),
        (
            turned(gate_weight3),
            turned(gate_weight2),
            turned(gate_weight1),
            turned(conv_weight),
            norm1_gain,
            norm1_bias,
            input_bias,
            conv_bias,
            gate_bias1,
            gate_bias2,
            gate_bias3,
            output_bias,
            layer_scale1,
            norm2_gain,
            norm2_bias,
            reduce_bias,
            layer_scale2,
            expand_bias.T,
        ),
    )
    in_shards = gather(turned(input_weight))
    slabs = gather(small)
    dy_blocks, late_weights = second_kernel(
        me,
        cotangent.reshape(SHARD, -1),
        turned(output_weight),
        turned(expand_weight),
        reduce_weight.reshape(-1, WIDTH),
    )
    x_blocks, _, _ = hold(x_blocks, in_shards[2], slabs[2])
    x_blocks = exchange(x_blocks)
    vec, expand, w1, w1_back, w2, w3, w_in, taps, perm = prepare(me, slabs, in_shards)
    x_blocks, dy_blocks, late_weights, vec = hold(x_blocks, dy_blocks, late_weights, vec)
    dy_blocks = exchange(dy_blocks)
    late_core, late_across = swap(late_weights, CORE_SWAP), swap(late_weights, CHIP_SWAP)
    x, z1, u, dwv = front(x_blocks, perm, vec, w_in, taps)
    z1, dwv, late_across, dy_blocks = hold(z1, dwv, late_across, dy_blocks)
    shards = (late_weights, late_core, late_across, swap(late_across, CORE_SWAP))
    w_out = join_output(me, shards)
    z2 = branch_forward(dwv, x, vec, w1, w2, w3, w_out)
    order = (1, 3, 0, 2)
    expand_tiles = jnp.concatenate([expand[8 * k : 8 * k + 8] for k in order], axis=0)
    dy, f, dz, sib_g, keep_g, bias_grads = feed_forward(
        z2, dy_blocks, perm, vec, expand_tiles, [shards[k] for k in order]
    )

    where = lax.axis_index("mp").astype(jnp.int32).reshape(1)
    neighbours = [(i, i ^ 1) for i in range(mp_count)]

    def slot(*requests):
        work = Slot(where)
        found = [getattr(work, name)(*args) for name, *args in requests]
        results = work.run()
        return [results[one] if one.stop - one.start > 1 else results[one.start] for one in found]

    got_g = swap(sib_g, CORE_SWAP)
    (on_g,) = slot(("onward", [keep_g], [got_g]))
    dz, on_g = hold(dz, on_g)
    other_g = swap(on_g, CHIP_SWAP)
    *outs, g, dx1, sib, keep_late = branch_backward(
        me, dwv, x, dy, f, dz, vec, w1, w1_back, w2, w3, w_out, perm, bias_grads
    )
    got_late = swap(sib, CORE_SWAP)
    g, other_g, outs = hold(g, other_g, outs)
    ((go_g, stay_g),) = slot(("halves", [keep_g], [got_g], other_g))
    g, go_g = hold(g, go_g)
    near_g = lax.ppermute(go_g, "mp", neighbours)
    outs = exchange(outs)

    du3, sib, keep3 = conv_backward(me, g, u, taps, z1, 6)
    got3 = swap(sib, CORE_SWAP)
    du3, near_g = hold(du3, near_g)
    (part_g,) = slot(("both", stay_g, near_g))
    g, part_g = hold(g, part_g)
    part_g = trade(part_g, mp_count, 2)

    du2, sib, keep2 = conv_backward(me, g, u, taps, z1, 4)
    got2 = swap(sib, CORE_SWAP)
    du2, part_g, got_late, got3, got2 = hold(du2, part_g, got_late, got3, got2)
    high = [keep_late, keep2, keep3], [got_late, got2, got3]
    full_g, on_h = slot(("spread", part_g), ("onward", *high))
    g, full_g, on_h = hold(g, full_g, on_h)
    full_g = trade(full_g, mp_count, 2)
    other_h = swap(on_h, CHIP_SWAP)

    du1, sib, keep1 = conv_backward(me, g, u, taps, z1, 2)
    got1 = swap(sib, CORE_SWAP)
    du1, full_g, other_h = hold(du1, full_g, other_h)
    (part_h,) = slot(("own", *high, other_h))
    g, part_h, full_g = hold(g, part_h, full_g)
    far_g = lax.ppermute(full_g, "mp", neighbours)
    part_h = trade(part_h, mp_count)

    du0, sib, keep0 = conv_backward(me, g, u, taps, z1, 0)
    got0 = swap(sib, CORE_SWAP)
    du0, part_h, got0, got1, outs = hold(du0, part_h, got0, got1, outs)
    low = [keep0, keep1], [got0, got1]
    full_h, on_l = slot(("spread", part_h), ("onward", *low))
    du0, full_h, on_l = hold(du0, full_h, on_l)
    full_h = trade(full_h, mp_count)
    other_l = swap(on_l, CHIP_SWAP)

    *ins, e0, e1, e2, e3 = input_backward(me, (du0, du1, du2, du3), x, dx1, vec, w_in, perm)
    ins = exchange(ins)
    ends = exchange((e0, e1, e2, e3))
    e0, other_l, full_h, far_g = hold(e0, other_l, full_h, far_g)
    (part_l,) = slot(("own", *low, other_l))
    part_l = trade(part_l, mp_count)
    part_l, ins = hold(part_l, ins)
    (full_l,) = slot(("spread", part_l, ends))
    full_l = trade(full_l, mp_count)
    upper = (where[0] & 1) != 0
    full_g, far_g = flat(full_g), flat(far_g)
    sum_g = jnp.concatenate([jnp.where(upper, far_g, full_g), jnp.where(upper, full_g, far_g)], axis=0)

    def back(values, blocks):
        return jnp.transpose(values.reshape(blocks, 16, values.shape[1]), (2, 0, 1))

    sum_e, sum_r = widen(sum_g)
    (
        g1, g2, g3, gconv, gout, gin, gb1, gb2, gb3, gob, gls1, gn2g, gn2b, grb, gls2, geb, ginb, gcb, gn1g, gn1b,
    ) = unpack_small(flat(full_h), full_l)
    block_output = from_pixels(me, outs).reshape(block_input.shape)
    input_grad = from_pixels(me, ins).reshape(block_input.shape)
    return (
        block_output,
        input_grad,
        gn1g,
        gn1b,
        back(gin, 16),
        ginb,
        back(gconv, 15),
        gcb,
        back(g1, 2),
        gb1,
        back(g2, 4),
        gb2,
        back(g3, 8),
        gb3,
        back(gout, 8),
        gob,
        gls1,
        gn2g,
        gn2b,
        back(sum_e, 32),
        geb.T,
        sum_r.reshape(32, 16, WIDTH),
        grb,
        gls2,
    )


def solution(mesh):
    pixels = P(None, "dp", "mp")
    vector = P(None, "dp")
    matrix = P(None, None, "dp")
    params = (
        vector, vector, matrix, vector, matrix, vector, matrix, vector, matrix, vector, matrix, vector,
        matrix, vector, vector, vector, vector, matrix, vector, P(None, "dp", None), vector, vector,
    )
    return jax.shard_map(
        partial(per_device, mesh.shape["mp"]),
        mesh=mesh,
        in_specs=(pixels,) + params + (pixels,),
        out_specs=(pixels, pixels) + params,
        check_vma=False,
    )
```

```python
from functools import partial

import jax
import jax.numpy as jnp
from jax import lax
from jax.experimental import pallas as pl
from jax.experimental.pallas import tpu as pltpu
from jax.sharding import PartitionSpec as P

WIDTH = 512
GROUP = 64
SIDE = 14
CROP = SIDE * SIDE
CROPS = 8
TOKENS = CROP * CROPS
SHARD = 128
TAPS = 49
EPSILON = 1e-06
LOW = jnp.bfloat16
FULL = jnp.float32
VMEM = 58 * 1024 * 1024

NN = (((1,), (0,)), ((), ()))
NT = (((1,), (1,)), ((), ()))
TN = (((0,), (0,)), ((), ()))

CORE_SWAP = [(0, 1), (1, 0), (2, 3), (3, 2)]
CHIP_SWAP = [(0, 2), (2, 0), (1, 3), (3, 1)]
BOTH_SWAP = [(0, 3), (3, 0), (1, 2), (2, 1)]

S_GATE3, S_GATE2, S_GATE1, S_CONV, S_EXPAND, S_OUT, S_ROWS = 0, 256, 320, 352, 560, 592, 1104
S_LANE = 64
(V_N1G, V_N1B, V_INB, V_CB, V_GB1, V_GB2, V_GB3, V_OB, V_LS1, V_N2G, V_N2B, V_RB, V_LS2) = range(13)
VECTORS = 13
E_OUT, E_VEC, E_EXPAND, E_ROWS = 0, 352 + 512, 496 + 512, 640 + 512
E_GATE = 512


def mm(left, right, dims=NN):
    return lax.dot_general(left, right, dims, preferred_element_type=FULL)


def call(body, out, weight=1.0, **kwargs):
    flops, moved = int(weight * 1.15e9 / 4), 1 << 10
    return pl.pallas_call(
        body,
        out_shape=out,
        compiler_params=pltpu.CompilerParams(vmem_limit_bytes=VMEM),
        cost_estimate=pl.CostEstimate(flops=flops, bytes_accessed=moved, transcendentals=0),
        **kwargs,
    )


def struct(shape, dtype):
    return jax.ShapeDtypeStruct(shape, dtype)


SMEM_SPEC = pl.BlockSpec(memory_space=pltpu.SMEM)


def whole(shape):
    return pl.BlockSpec(shape, lambda i: (0,) * len(shape))


def turn_blocks(me, x_ref, outs, wide, blocks):
    lanes = x_ref.shape[1]
    for dest in range(4):
        for crop in range(CROPS):
            start = CROP * (CROPS * dest + crop)
            base = start // 128 * 128
            window = x_ref[:, base : base + min(lanes - base, 384)].astype(FULL)
            wide[pl.ds(crop, CROP, stride=CROPS), :] = window[:, start - base : start - base + CROP].T
        blocks[dest ^ me] = wide[...].astype(LOW)
    for k in range(4):
        outs[k][...] = blocks[k]


PIXEL_SCRATCH = [pltpu.VMEM((TOKENS, SHARD), FULL), pltpu.VMEM((4, TOKENS, SHARD), LOW)]


W_FIRST = 2 * TOKENS
JOINT = W_FIRST + 4 * 1024


def second_body(me_ref, x_ref, expand, reduce, own, near, far, wide, blocks):
    places = (own, near.at[0:TOKENS], far.at[0:TOKENS], far.at[TOKENS:W_FIRST])
    turn_blocks(me_ref[0], x_ref, places, wide, blocks)
    for part in range(4):
        lanes = slice(part * 128, part * 128 + 128)
        first = W_FIRST + part * 1024
        for out in (near, far):
            out[first : first + 512, :] = expand[:, lanes]
            out[first + 512 : first + 1024, :] = reduce[:, lanes]


def second_kernel(me, x, expand, reduce):
    joint = struct((JOINT, SHARD), LOW)
    return call(
        second_body,
        (struct((TOKENS, SHARD), LOW), joint, joint),
        weight=0.05,
        in_specs=[SMEM_SPEC] + [pl.BlockSpec(memory_space=pltpu.VMEM)] * 3,
        scratch_shapes=PIXEL_SCRATCH,
    )(me, x, expand, reduce)


def first_body(me_ref, x_ref, *refs):
    pack_body(*refs[:19], refs[19], refs[24])
    turn_blocks(me_ref[0], x_ref, refs[20:24], refs[25], refs[26])


def first_kernel(me, x, small):
    return call(
        first_body,
        (struct((S_ROWS, 128), LOW),) + (struct((TOKENS, SHARD), LOW),) * 4,
        weight=0.05,
        in_specs=[SMEM_SPEC] + [pl.BlockSpec(memory_space=pltpu.VMEM)] * 20,
        scratch_shapes=[pltpu.VMEM((S_OUT, 128), FULL)] + PIXEL_SCRATCH,
    )(me, x, *small)


def from_pixels_body(me_ref, *refs):
    ins, out_ref, wide, blocks = refs[:4], refs[4], refs[5], refs[6]
    me = me_ref[0]
    for k in range(4):
        blocks[k ^ me] = ins[k][...]
    for source in range(4):
        wide[...] = blocks[source].astype(FULL)
        for crop in range(CROPS):
            start = CROP * (CROPS * source + crop)
            part = wide[pl.ds(crop, CROP, stride=CROPS), :].T
            out_ref[:, start : start + CROP] = part.astype(LOW)


def from_pixels(me, blocks):
    return call(
        from_pixels_body,
        struct((SHARD, 4 * TOKENS), LOW),
        weight=4.0,
        in_specs=[SMEM_SPEC] + [pl.BlockSpec(memory_space=pltpu.VMEM)] * 4,
        scratch_shapes=[pltpu.VMEM((TOKENS, SHARD), FULL), pltpu.VMEM((4, TOKENS, SHARD), LOW)],
    )(me, *blocks)


def pack_body(out_weight, g3, g2, g1, conv, *refs):
    vectors, expand, out_ref, slab = refs[:VECTORS], refs[VECTORS], refs[VECTORS + 1], refs[VECTORS + 2]
    slab[...] = jnp.zeros_like(slab)
    slab[S_GATE3 : S_GATE3 + 128, :] = g3[:, :128].astype(FULL)
    slab[S_GATE3 + 128 : S_GATE3 + 256, :] = g3[:, 128:].astype(FULL)
    slab[S_GATE2 : S_GATE2 + 64, :] = g2[...].astype(FULL)
    slab[S_GATE1 : S_GATE1 + 32, :GROUP] = g1[...].astype(FULL)
    slab[S_CONV : S_CONV + 240, :TAPS] = conv[...].astype(FULL)
    for number, ref in enumerate(vectors):
        first = S_CONV + 16 * number + (1 if number == V_CB else 0)
        slab[first : first + ref.shape[0], S_LANE : S_LANE + 16] = ref[...].astype(FULL)
    slab[S_EXPAND : S_EXPAND + 32, S_LANE : S_LANE + 16] = expand[...].astype(FULL).T
    out_ref[0:S_OUT, :] = slab[...].astype(LOW)
    for part in range(4):
        rows = slice(S_OUT + part * 128, S_OUT + part * 128 + 128)
        out_ref[rows, :] = out_weight[:, part * 128 : part * 128 + 128]


TILE_OF = (2, 0, 3, 1)


def iota(shape, dim):
    return lax.broadcasted_iota(jnp.int32, shape, dim)


def spread(lanes):
    return jnp.where(iota((128, lanes), 1) % 16 + S_LANE == iota((128, lanes), 0), 1.0, 0.0).astype(LOW)


def prepare_body(me_ref, *refs):
    slabs, ins = refs[0:4], refs[4:8]
    vec, expand, w1, w1_back, w2, w3, w_in, w_out, taps, perm, channels = refs[8:]
    me = me_ref[0]
    totals = jnp.zeros((VECTORS, 1024), FULL)
    spread_wide = spread(1024)
    row = iota((VECTORS * 16, 1024), 0) % 16
    lane = iota((VECTORS * 16, 1024), 1)
    in_row = row == lane // 64
    spread_expand = spread(512)
    expand_rows = iota((32, 512), 0) == iota((32, 512), 1) // 16
    w1[...] = jnp.zeros_like(w1)
    channels[0:GROUP, :] = jnp.where(iota((GROUP, 128), 1) == TAPS // 2, 3.0, 0.0)
    for k in range(4):
        source = me ^ k
        slab = slabs[k]
        values = mm(slab[S_CONV : S_CONV + VECTORS * 16, :], spread_wide)
        values = jnp.where(in_row & (lane // 16 % 4 == source), values, 0.0)
        totals = totals + jnp.sum(values.reshape(VECTORS, 16, 1024), axis=1)
        values = mm(slab[S_EXPAND : S_EXPAND + 32, :], spread_expand)
        values = jnp.sum(jnp.where(expand_rows, values, 0.0), axis=0, keepdims=True)
        slot = TILE_OF[k]
        expand[8 * slot : 8 * slot + 8, :] = jnp.broadcast_to(values, (8, 512))
        for a in range(16):
            place = pl.ds(pl.multiple_of(a * 64 + source * 16, 16), 16)
            rows = slice(a * 16, a * 16 + 16)
            w_in[place, :] = ins[k][rows, :]
            if a < 15:
                later = pl.ds(pl.multiple_of((a + 1) * 64 + source * 16, 16), 16)
                channels[later, :] = slab[S_CONV + a * 16 : S_CONV + a * 16 + 16, :].astype(FULL)
            if a < 8:
                for part in range(4):
                    first = S_OUT + part * 128 + a * 16
                    w_out[place, part * 128 : part * 128 + 128] = slab[first : first + 16, :]
                w3[place, 0:128] = slab[S_GATE3 + a * 16 : S_GATE3 + a * 16 + 16, :]
                w3[place, 128:256] = slab[S_GATE3 + 128 + a * 16 : S_GATE3 + 128 + a * 16 + 16, :]
            if a < 4:
                w2[place, :] = slab[S_GATE2 + a * 16 : S_GATE2 + a * 16 + 16, :]
            if a < 2:
                w1[place, :] = slab[S_GATE1 + a * 16 : S_GATE1 + a * 16 + 16, :]
        column = iota((SHARD, WIDTH), 0)
        target = column // 16 * 64 + source * 16 + column % 16
        perm[k * SHARD : (k + 1) * SHARD, :] = jnp.where(iota((SHARD, WIDTH), 1) == target, 1.0, 0.0).astype(LOW)
    vec[0:VECTORS, :] = totals
    vec[VECTORS:16, :] = jnp.zeros((16 - VECTORS, 1024), FULL)
    single = w1[...].astype(FULL)
    w1_back[...] = (single + pltpu.roll(single, GROUP, 1)).astype(LOW)
    taps[...] = channels[...].T[0:64, :]


def prepare(me, slabs, ins):
    return call(
        prepare_body,
        (
            struct((16, 1024), FULL),
            struct((32, 512), FULL),
            struct((128, 128), LOW),
            struct((128, 128), LOW),
            struct((256, 128), LOW),
            struct((512, 256), LOW),
            struct((1024, 512), LOW),
            struct((512, 512), LOW),
            struct((64, 1024), FULL),
            struct((512, 512), LOW),
        ),
        weight=0.05,
        in_specs=[SMEM_SPEC] + [pl.BlockSpec(memory_space=pltpu.VMEM)] * 8,
        scratch_shapes=[pltpu.VMEM((1024, 128), FULL)],
    )(me, *slabs, *ins)


def normed(values):
    center = jnp.sum(values, axis=1, keepdims=True) * (1.0 / WIDTH)
    away = values - center
    spread_sq = jnp.sum(away * away, axis=1, keepdims=True) * (1.0 / WIDTH)
    inverse = lax.rsqrt(spread_sq + EPSILON)
    return away * inverse, inverse


def norm_back(grad, unit, inverse, gain):
    grad_unit = grad * gain
    first = jnp.sum(grad_unit, axis=1, keepdims=True) * (1.0 / WIDTH)
    second = jnp.sum(grad_unit * unit, axis=1, keepdims=True) * (1.0 / WIDTH)
    return inverse * (grad_unit - first - unit * second)


def total(values):
    return jnp.sum(values, axis=0, keepdims=True)


def row(vec, number, lanes=WIDTH):
    return vec[number : number + 1, 0:lanes]


def rows_spec(tile, lanes):
    return pl.BlockSpec((tile, lanes), lambda i: (i, 0))


def chunks(count, size, body):
    def step(i, carry):
        body(pl.ds(pl.multiple_of(i * size, size), size))
        return carry

    lax.fori_loop(0, count // size, step, 0)


NORM_ROWS = 224
HALVES = (slice(0, TOKENS // 2), slice(TOKENS // 2, TOKENS))


def join(blocks, perm, rows):
    return mm(jnp.concatenate([r[rows, :] for r in blocks], axis=1), perm[...])


def conv_rows(source, weights, emit, flip):
    zero = jnp.zeros((CROPS, 128), FULL)

    def tap_row(i, r, sums):
        base = (i + r - 3) * SIDE
        values = [source[base + c] for c in range(SIDE)]
        first = (6 - r) * 7 if flip else r * 7
        taps = [weights[first + (6 - s if flip else s)] for s in range(7)]
        for s in range(7):
            for c in range(SIDE):
                if 0 <= c + s - 3 < SIDE:
                    sums[c] = sums[c] + taps[s] * values[c + s - 3]

    def one_row(i, first, last):
        sums = [zero] * SIDE
        for r in range(first, last):
            tap_row(i, r, sums)
        emit(i, sums)

    def inner_row(i, carry):
        one_row(i, 0, 7)
        return carry

    for i in range(3):
        one_row(i, 3 - i, 7)
    lax.fori_loop(3, SIDE - 3, inner_row, 0)
    for i in range(SIDE - 3, SIDE):
        one_row(i, 0, 17 - i)


def wide_taps(taps, weights):
    for tap in range(TAPS):
        weights[tap] = jnp.broadcast_to(taps[tap : tap + 1, :], (CROPS, 128))


PIXEL_BLOCK = pl.BlockSpec((CROP, CROPS, 128), lambda i: (0, 0, i))


def lane_block(rows):
    return pl.BlockSpec((rows, 128), lambda i: (0, i))


def front_body(r0, r1, r2, r3, perm, vec, w_in, taps, vec_part, x, z, u, dwv, weights):
    @pl.when(pl.program_id(0) == 0)
    def _():
        for rows in HALVES:
            x[rows, :] = join((r0, r1, r2, r3), perm, rows).astype(LOW)

        def norm_rows(rows):
            unit, _ = normed(x[rows, :].astype(FULL))
            z[rows, :] = (unit * row(vec, V_N1G) + row(vec, V_N1B)).astype(LOW)

        chunks(TOKENS, NORM_ROWS, norm_rows)

    wide_taps(taps, weights)
    values = mm(z[...], w_in[...], NT) + vec_part[V_INB : V_INB + 1, :]
    u[...] = values.reshape(CROP, CROPS, 128)
    bias = jnp.broadcast_to(vec_part[V_CB : V_CB + 1, :], (CROPS, 128))

    def emit(i, sums):
        for c in range(SIDE):
            dwv[i * SIDE + c] = (sums[c] + bias) * (1.0 / 3.0)

    conv_rows(u, weights, emit, False)


def front(blocks, perm, vec, w_in, taps):
    pixels = struct((CROP, CROPS, 1024), FULL)
    rows = struct((TOKENS, WIDTH), LOW)
    x, z, u, dwv = call(
        front_body,
        (rows, rows, pixels, pixels),
        weight=28.0,
        grid=(8,),
        in_specs=[whole((TOKENS, SHARD))] * 4
        + [
            whole((512, 512)),
            whole((16, 1024)),
            pl.BlockSpec((128, 512), lambda i: (i, 0)),
            lane_block(64),
            lane_block(16),
        ],
        out_specs=(whole((TOKENS, WIDTH)), whole((TOKENS, WIDTH)), PIXEL_BLOCK, PIXEL_BLOCK),
        scratch_shapes=[pltpu.VMEM((TAPS, CROPS, 128), FULL)],
    )(*blocks, perm, vec, w_in, taps, vec)
    return x, z, u, dwv.reshape(TOKENS, 1024)


def gate_chain(dwv, vec, w1, w2, w3):
    first = dwv[:, 0:128]
    turned = pltpu.roll(first, GROUP, 1)
    q0 = (first * turned).astype(LOW)
    t1 = mm(q0, w1[...], NT) + row(vec, V_GB1, 128)
    q1 = (t1 * dwv[:, 128:256]).astype(LOW)
    t2 = mm(q1, w2[...], NT) + row(vec, V_GB2, 256)
    q2 = (t2 * dwv[:, 256:512]).astype(LOW)
    t3 = mm(q2, w3[...], NT) + row(vec, V_GB3, 512)
    q3 = (t3 * dwv[:, 512:1024]).astype(LOW)
    return turned, (q0, q1, q2, q3), (t1, t2, t3)


def branch_body(dwv, x, vec, w1, w2, w3, w_out, z_out):
    _, orders, _ = gate_chain(dwv[...], vec, w1, w2, w3)
    branch = mm(orders[3], w_out[...], NT) + row(vec, V_OB)
    middle = x[...].astype(FULL) + row(vec, V_LS1) * branch
    unit, _ = normed(middle)
    z_out[...] = (unit * row(vec, V_N2G) + row(vec, V_N2B)).astype(LOW)


def branch_forward(dwv, x, vec, w1, w2, w3, w_out, tile=784):
    return call(
        branch_body,
        struct((TOKENS, WIDTH), LOW),
        weight=7.0,
        grid=(TOKENS // tile,),
        in_specs=[
            rows_spec(tile, 1024),
            rows_spec(tile, WIDTH),
            whole((16, 1024)),
            whole((128, 128)),
            whole((256, 128)),
            whole((512, 256)),
            whole((512, 512)),
        ],
        out_specs=rows_spec(tile, WIDTH),
    )(dwv, x, vec, w1, w2, w3, w_out)


def gelu_parts(s):
    bell = jnp.exp2((-0.5 * 1.4426950408889634) * (s * s))
    size = jnp.abs(s)
    t = pltpu.reciprocal(1.0 + (0.3275911 * 0.7071067811865476) * size, approx=True)
    poly = 0.5 * 1.061405429
    for coefficient in (-1.453152027, 1.421413741, -0.284496736, 0.254829592):
        poly = poly * t + 0.5 * coefficient
    tail = poly * t * bell
    cdf = jnp.where(s >= 0.0, 1.0 - tail, tail)
    return s * cdf, cdf + s * (bell * 0.3989422804014327)


PIECE = 16


def mlp_body(z, r0, perm, vec, expand, c0, c1, c2, c3, *refs):
    dy, f, dz, gb, sibling, keep = refs[0:6]
    r1, r2, r3, we, wr, df, s0, s1, g0, g1, hid, grad_s, grads, sums, sems = refs[6:]
    pre, grad_h = (s0, s1), (g0, g1)
    half = TOKENS // 2
    shards = (c1, c3, c0, c2)

    def copies(slot):
        for part in range(4):
            for number, matrix in enumerate((we, wr)):
                rows = pl.ds(W_FIRST + part * 1024 + number * 512, 512)
                yield pltpu.make_async_copy(
                    shards[slot].at[rows], matrix.at[slot, :, pl.ds(part * 128, 128)], sems.at[slot]
                )

    near = [
        pltpu.make_async_copy(shard.at[pl.ds(first, TOKENS)], r, sems.at[4 + number])
        for number, (shard, first, r) in enumerate(((c1, 0, r1), (c2, 0, r2), (c3, TOKENS, r3)))
    ]
    for copy in near:
        copy.start()
    for slot in range(4):
        for copy in copies(slot):
            copy.start()

    def arrived(slot):
        for matrix in (we, wr):
            pltpu.make_async_copy(matrix.at[slot], matrix.at[slot], sems.at[slot]).wait()

    def leave(tile):
        out = (sibling, keep)[tile // 2].at[tile % 2]
        return pltpu.make_async_copy(grads.at[tile], out, sems.at[7 + tile])

    for copy in near:
        copy.wait()
    for rows in HALVES:
        dy[rows, :] = join((r0, r1, r2, r3), perm, rows).astype(LOW)

    def scaled(rows):
        df[rows, :] = (dy[rows, :].astype(FULL) * row(vec, V_LS2)).astype(LOW)
        f[rows, :] = jnp.zeros((112, WIDTH), FULL)
        dz[rows, :] = jnp.zeros((112, WIDTH), FULL)

    chunks(TOKENS, 112, scaled)
    sums[...] = jnp.zeros_like(sums)
    hid[1] = jnp.zeros((TOKENS, 512), LOW)
    grad_s[1] = jnp.zeros((TOKENS, 512), LOW)
    arrived(0)
    s0[...] = mm(z[HALVES[0], :], we[0], NT)
    g0[...] = mm(df[HALVES[0], :], wr[0], NT)
    pieces = half // PIECE

    def unit(here, tile, before, after):
        there = 1 - here
        rows = HALVES[there]
        now, last = tile & 1, (tile & 1) ^ 1
        ready = last if here == 0 else now
        bias = expand[pl.ds(pl.multiple_of(tile * 8, 8), 1), :]
        done = [0]
        column = [jnp.zeros((8, 512), FULL)]

        def some(part):
            while done[0] < pieces * part // 6:
                first = done[0] * PIECE
                piece = slice(first, first + PIECE)
                place = slice(here * half + first, here * half + first + PIECE)
                act, slope = gelu_parts(pre[here][piece, :] + bias)
                hid[now, place, :] = act.astype(LOW)
                grad = (grad_h[here][piece, :] * slope).astype(LOW)
                grad_s[now, place, :] = grad
                grad = grad.astype(FULL)
                column[0] = column[0] + (grad[0:8] + grad[8:16])
                done[0] += 1

        f[rows, :] += mm(hid[ready, rows, :], wr[before if here == 0 else tile])
        some(1)
        dz[rows, :] += mm(grad_s[ready, rows, :], we[before if here == 0 else tile])
        some(2)
        pre[there][...] = mm(z[rows, :], we[after], NT)
        some(3)
        grad_h[there][...] = mm(df[rows, :], wr[after], NT)
        some(4)
        if here == 0:
            grads[before, 0:512, :] = mm(grad_s[last], z[...], TN).astype(LOW)
        else:
            grads[before, 512:1024, :] = mm(hid[last], df[...], TN).astype(LOW)
        some(6)
        sums[tile] += column[0]

    def one_tile(tile, carry):
        before = jnp.maximum(tile - 1, 0)
        for number in range(2):

            @pl.when(tile == number + 2)
            def _():
                leave(number).start()

        unit(0, tile, before, tile)

        @pl.when(tile < 3)
        def _():
            arrived(tile + 1)

        unit(1, tile, before, jnp.minimum(tile + 1, 3))
        return carry

    lax.fori_loop(0, 4, one_tile, 0)
    leave(2).start()
    rows = HALVES[1]
    grads[3, 0:512, :] = mm(grad_s[1], z[...], TN).astype(LOW)
    grads[3, 512:1024, :] = mm(hid[1], df[...], TN).astype(LOW)
    leave(3).start()
    f[rows, :] += mm(hid[1, rows, :], wr[3])
    dz[rows, :] += mm(grad_s[1, rows, :], we[3])
    for tile in range(4):
        gb[8 * tile : 8 * tile + 8, :] = sums[tile]
    for tile in range(4):
        leave(tile).wait()


def feed_forward(z, own_dy, joints, perm, vec, expand):
    vmem = pl.BlockSpec(memory_space=pltpu.VMEM)
    anywhere = pl.BlockSpec(memory_space=pl.ANY)
    half = TOKENS // 2
    pair = struct((2, 1024, 512), LOW)
    rows = struct((TOKENS, WIDTH), FULL)
    return call(
        mlp_body,
        (struct((TOKENS, WIDTH), LOW), rows, rows, struct((32, 512), FULL), pair, pair),
        weight=40.0,
        in_specs=[vmem] * 5 + [anywhere] * 4,
        out_specs=(vmem,) * 4 + (anywhere,) * 2,
        scratch_shapes=[pltpu.VMEM((TOKENS, SHARD), LOW)] * 3
        + [pltpu.VMEM((4, 512, 512), LOW)] * 2
        + [pltpu.VMEM((TOKENS, WIDTH), LOW)]
        + [pltpu.VMEM((half, 512), FULL)] * 4
        + [pltpu.VMEM((2, TOKENS, 512), LOW)] * 2
        + [pltpu.VMEM((4, 1024, 512), LOW)]
        + [pltpu.VMEM((4, 8, 512), FULL)]
        + [pltpu.SemaphoreType.DMA((11,))],
    )(z, own_dy, perm, vec, expand, *joints)


def pack_vectors(values, count, source):
    lane = iota((count * 16, 1024), 1)
    keep = (iota((count * 16, 1024), 0) % 16 == lane // 64) & (lane // 16 % 4 == source)
    tall = jnp.broadcast_to(values[:, None, :], (count, 16, 1024)).reshape(count * 16, 1024)
    gather = jnp.where(iota((1024, 128), 0) % 16 == iota((1024, 128), 1), 1.0, 0.0).astype(LOW)
    return mm(jnp.where(keep, tall, 0.0).astype(LOW), gather)


def part_pair(parts, sibling, keep):
    sibling[0] = parts[1]
    sibling[1] = parts[3]
    keep[0] = parts[0]
    keep[1] = parts[2]


def branch_back_body(steps, me_ref, dwv, x, dy, f, dz, vec, w1, w1_back, w2, w3, w_out, perm, gb, *refs):
    (o0, o1, o2, o3, g_out, dx_out, sibling, keep) = refs[0:8]
    acc_o, acc_3, acc_2, acc_1, sums, parts = refs[8:]
    step = pl.program_id(0)
    values = dwv[...]
    turned, orders, gates = gate_chain(values, vec, w1, w2, w3)
    branch = mm(orders[3], w_out[...], NT) + row(vec, V_OB)
    middle = x[...].astype(FULL) + row(vec, V_LS1) * branch
    unit, inverse = normed(middle)
    top = dy[...].astype(FULL)
    mlp = f[...] + row(vec, V_RB)
    output = (middle + row(vec, V_LS2) * mlp).astype(LOW)
    blocks = mm(output, perm[...], NT).astype(LOW)
    for k, ref in enumerate((o0, o1, o2, o3)):
        ref[...] = blocks[:, k * SHARD : (k + 1) * SHARD]
    grad = dz[...]
    middle_grad = top + norm_back(grad, unit, inverse, row(vec, V_N2G))
    dx_out[...] = middle_grad
    grad_branch = (middle_grad * row(vec, V_LS1)).astype(LOW)
    grad_o = mm(grad_branch, orders[3], TN)
    back = mm(grad_branch, w_out[...])
    gt3 = (back * values[:, 512:1024]).astype(LOW)
    g_out[:, 512:1024] = back * gates[2] * (1.0 / 3.0)
    grad_3 = mm(gt3, orders[2], TN)
    back = mm(gt3, w3[...])
    gt2 = (back * values[:, 256:512]).astype(LOW)
    g_out[:, 256:512] = back * gates[1] * (1.0 / 3.0)
    grad_2 = mm(gt2, orders[1], TN)
    back = mm(gt2, w2[...])
    gt1 = (back * values[:, 128:256]).astype(LOW)
    g_out[:, 128:256] = back * gates[0] * (1.0 / 3.0)
    grad_1 = mm(gt1, orders[0], TN)
    back = mm(gt1, w1_back[...])
    g_out[:, 0:128] = back * turned * (1.0 / 3.0)

    @pl.when(step == 0)
    def _():
        acc_o[...] = jnp.zeros_like(acc_o)
        acc_3[...] = jnp.zeros_like(acc_3)
        acc_2[...] = jnp.zeros_like(acc_2)
        acc_1[...] = jnp.zeros_like(acc_1)
        sums[...] = jnp.zeros_like(sums)

    acc_o[...] += grad_o
    acc_3[...] += grad_3
    acc_2[...] += grad_2
    acc_1[...] += grad_1
    sums[0:1, 0:128] += total(gt1.astype(FULL))
    sums[1:2, 0:256] += total(gt2.astype(FULL))
    sums[2:3, 0:512] += total(gt3.astype(FULL))
    sums[3:4, 0:512] += total(grad_branch.astype(FULL))
    sums[4:5, 0:512] += total(middle_grad * branch)
    sums[5:6, 0:512] += total(grad * unit)
    sums[6:7, 0:512] += total(grad)
    sums[7:8, 0:512] += total(top) * row(vec, V_LS2)
    sums[8:9, 0:512] += total(top * mlp)

    @pl.when(step == steps - 1)
    def _():
        me = me_ref[0]
        vectors = sums[0:9, :]
        expand_rows = iota((32, 512), 0) == iota((32, 512), 1) // 16
        gather = jnp.where(iota((512, 128), 0) % 16 == iota((512, 128), 1), 1.0, 0.0).astype(LOW)
        for source in range(4):
            k = source ^ me
            for a in range(8):
                rows = slice(a * 64 + source * 16, a * 64 + source * 16 + 16)
                for part in range(4):
                    first = part * 128 + a * 16
                    parts[k, first : first + 16, :] = acc_o[rows, part * 128 : part * 128 + 128].astype(LOW)
                first = E_GATE + a * 16
                parts[k, first : first + 16, :] = acc_3[rows, 0:128].astype(LOW)
                parts[k, first + 128 : first + 144, :] = acc_3[rows, 128:256].astype(LOW)
                if a < 4:
                    parts[k, first + 256 : first + 272, :] = acc_2[rows, :].astype(LOW)
                if a < 2:
                    parts[k, first + 320 : first + 336, :] = acc_1[rows, :].astype(LOW)
            parts[k, E_VEC : E_VEC + 144, :] = pack_vectors(vectors, 9, source).astype(LOW)
        for k in range(4):
            slot = TILE_OF[k]
            line = total(gb[8 * slot : 8 * slot + 8, :])
            tall = jnp.where(expand_rows, jnp.broadcast_to(line, (32, 512)), 0.0)
            parts[k, E_EXPAND : E_EXPAND + 32, :] = mm(tall.astype(LOW), gather).astype(LOW)
            parts[k, E_EXPAND + 32 : E_ROWS, :] = jnp.zeros((E_ROWS - E_EXPAND - 32, 128), LOW)
        part_pair(parts, sibling, keep)


def branch_backward(me, dwv, x, dy, f, dz, vec, w1, w1_back, w2, w3, w_out, perm, biases, tile=784):
    steps = TOKENS // tile
    wide = rows_spec(tile, WIDTH)
    block = rows_spec(tile, SHARD)
    pair = (2, E_ROWS, 128)
    return call(
        partial(branch_back_body, steps),
        (struct((TOKENS, SHARD), LOW),) * 4
        + (
            struct((TOKENS, 1024), FULL),
            struct((TOKENS, WIDTH), FULL),
            struct(pair, LOW),
            struct(pair, LOW),
        ),
        weight=20.0,
        grid=(steps,),
        in_specs=[
            SMEM_SPEC,
            rows_spec(tile, 1024),
            wide,
            wide,
            wide,
            wide,
            whole((16, 1024)),
            whole((128, 128)),
            whole((128, 128)),
            whole((256, 128)),
            whole((512, 256)),
            whole((512, 512)),
            whole((512, 512)),
        ]
        + [whole((32, 512))],
        out_specs=(block,) * 4
        + (rows_spec(tile, 1024), wide, whole(pair), whole(pair)),
        scratch_shapes=[
            pltpu.VMEM((512, 512), FULL),
            pltpu.VMEM((512, 256), FULL),
            pltpu.VMEM((256, 128), FULL),
            pltpu.VMEM((128, 128), FULL),
            pltpu.VMEM((16, 1024), FULL),
            pltpu.VMEM((4, E_ROWS, 128), LOW),
        ],
    )(me, dwv, x, dy, f, dz, vec, w1, w1_back, w2, w3, w_out, perm, biases)


def conv_back_body(me_ref, g, u, taps, z, du, sibling, keep, weights, grad_taps, parts):
    step, steps = pl.program_id(0), pl.num_programs(0)
    me = me_ref[0]
    wide_taps(taps, weights)
    zero = jnp.zeros((CROPS, 128), FULL)

    def emit(i, sums):
        stacked = jnp.concatenate(list(sums), axis=0).astype(LOW)
        first = i * SIDE * CROPS if isinstance(i, int) else pl.multiple_of(i * SIDE * CROPS, 16)
        du[pl.ds(first, SIDE * CROPS), :] = stacked

    conv_rows(g, weights, emit, True)

    for r in range(7):

        def one_row(i, sums):
            grads = [g[i * SIDE + c] for c in range(SIDE)]
            values = [u[(i + r - 3) * SIDE + c] for c in range(SIDE)]
            sums = list(sums)
            for c in range(SIDE):
                for s in range(7):
                    if 0 <= c + s - 3 < SIDE:
                        sums[s] = sums[s] + grads[c] * values[c + s - 3]
            return tuple(sums)

        sums = lax.fori_loop(max(0, 3 - r), min(SIDE, SIDE + 3 - r), one_row, (zero,) * 7)
        for s in range(7):
            grad_taps[r * 7 + s : r * 7 + s + 1, :] = total(sums[s])
    grad_taps[49:50, :] = total(jnp.sum(g[...], axis=0))
    grad_taps[50:51, :] = total(du[...].astype(FULL))
    grad_taps[51:128, :] = jnp.zeros((77, 128), FULL)
    grad_w = mm(du[...], z[...], TN)
    tall = grad_taps[...].T.astype(LOW)
    for a in range(2):
        for source in range(4):
            k = source ^ me
            rows = slice(a * 64 + source * 16, a * 64 + source * 16 + 16)
            for part in range(4):
                place = pl.ds(pl.multiple_of(part * 128 + step * 32 + a * 16, 16), 16)
                parts[k, place, :] = grad_w[rows, part * 128 : part * 128 + 128].astype(LOW)
            place = pl.ds(pl.multiple_of(512 + step * 32 + a * 16, 16), 16)
            parts[k, place, :] = tall[rows, :]

    @pl.when(step == steps - 1)
    def _():
        part_pair(parts, sibling, keep)


C_ROWS = 640


def conv_backward(me, g, u, taps, z, base):
    pixels = pl.BlockSpec((CROP, CROPS, 128), lambda i: (0, 0, i + base))
    pair = (2, C_ROWS, 128)
    return call(
        conv_back_body,
        (struct((TOKENS, 512), LOW), struct(pair, LOW), struct(pair, LOW)),
        weight=24.0,
        grid=(4,),
        in_specs=[
            SMEM_SPEC,
            pixels,
            pixels,
            pl.BlockSpec((64, 128), lambda i: (0, i + base)),
            whole((TOKENS, WIDTH)),
        ],
        out_specs=(lane_block(TOKENS), whole(pair), whole(pair)),
        scratch_shapes=[
            pltpu.VMEM((TAPS, CROPS, 128), FULL),
            pltpu.VMEM((128, 128), FULL),
            pltpu.VMEM((4, C_ROWS, 128), LOW),
        ],
    )(me, g.reshape(CROP, CROPS, 1024), u, taps, z)


def input_back_body(steps, me_ref, du0, du1, x, dx, vec, w_in, perm, *refs):
    (o0, o1, o2, o3, e0, e1, e2, e3, sums, parts) = refs
    step = pl.program_id(0)
    unit, inverse = normed(x[...].astype(FULL))
    grad = mm(jnp.concatenate([du0[...], du1[...]], axis=1), w_in[...])
    grad_x = (dx[...] + norm_back(grad, unit, inverse, row(vec, V_N1G))).astype(LOW)
    blocks = mm(grad_x, perm[...], NT).astype(LOW)
    for k, ref in enumerate((o0, o1, o2, o3)):
        ref[...] = blocks[:, k * SHARD : (k + 1) * SHARD]

    @pl.when(step == 0)
    def _():
        sums[...] = jnp.zeros_like(sums)

    sums[0:1, 0:512] += total(grad * unit)
    sums[1:2, 0:512] += total(grad)

    @pl.when(step == steps - 1)
    def _():
        me = me_ref[0]
        vectors = sums[0:2, :]
        for source in range(4):
            parts[source ^ me, :, :] = pack_vectors(vectors, 2, source).astype(LOW)
        for k, ref in enumerate((e0, e1, e2, e3)):
            ref[...] = parts[k]


def input_backward(me, dus, x, dx, vec, w_in, perm, tile=784):
    steps = TOKENS // tile
    wide = rows_spec(tile, WIDTH)
    end = (32, 128)
    return call(
        partial(input_back_body, steps),
        (struct((TOKENS, SHARD), LOW),) * 4 + (struct(end, LOW),) * 4,
        weight=8.0,
        grid=(steps,),
        in_specs=[
            SMEM_SPEC,
            *[rows_spec(tile, 512)] * 2,
            wide,
            wide,
            whole((16, 1024)),
            whole((1024, 512)),
            whole((512, 512)),
        ],
        out_specs=(rows_spec(tile, SHARD),) * 4 + (whole(end),) * 4,
        scratch_shapes=[pltpu.VMEM((16, 1024), FULL), pltpu.VMEM((4, 32, 128), LOW)],
    )(me, *dus, x, dx, vec, w_in, perm)


def unpack_body(full, final, *refs):
    (g1, g2, g3, conv, w_out, w_in), late_refs, expand = refs[0:6], refs[6:15], refs[15]
    (in_bias, conv_bias, gain, bias), low = refs[16:20], refs[20]
    size = final.shape[1] - 32
    last = jnp.zeros((32, 128), FULL)
    for piece in range(final.shape[0]):
        low[piece * size : (piece + 1) * size, :] = final[piece, 0:size, :]
        last = last + final[piece, size : size + 32, :].astype(FULL)
    gates = full[E_GATE:E_VEC, :].astype(FULL)
    g3[:, 0:128] = gates[0:128]
    g3[:, 128:256] = gates[128:256]
    g2[...] = gates[256:320]
    g1[...] = gates[320:352, 0:GROUP]
    taps = []
    for j, (source, first) in enumerate(((low, 0), (full, E_ROWS))):
        for part in range(4):
            rows = slice(first + part * 128, first + part * 128 + 128)
            w_in[j * 128 : j * 128 + 128, part * 128 : part * 128 + 128] = source[rows, :].astype(FULL)
        taps.append(source[first + 512 : first + 640, :])
    for part in range(4):
        lanes = slice(part * 128, part * 128 + 128)
        w_out[:, lanes] = full[lanes, :].astype(FULL)
    taps = jnp.concatenate(taps, axis=0).astype(FULL)
    conv[...] = taps[16:256, 0:TAPS]
    vectors = full[E_VEC : E_VEC + 144, :].astype(FULL)
    for number, ref in enumerate(late_refs):
        ref[...] = vectors[16 * number : 16 * number + ref.shape[0], 0:16]
    expand[...] = full[E_EXPAND : E_EXPAND + 32, 0:16].astype(FULL).T
    gain[...] = last[0:8, 0:16]
    bias[...] = last[16:24, 0:16]
    own = jnp.where(iota((256, 16), 0) % 16 == iota((256, 16), 1), 1.0, 0.0)
    rows = jnp.where(iota((16, 256), 0) == iota((16, 256), 1) // 16, 1.0, 0.0).astype(LOW)
    conv_bias[...] = mm(rows, (taps[:, 49:50] * own).astype(LOW))[1:16, :]
    in_bias[...] = mm(rows, (taps[:, 50:51] * own).astype(LOW))


VMEM_SPEC = pl.BlockSpec(memory_space=pltpu.VMEM)


def unpack_small(full, final):
    vector = lambda rows: struct((rows, 16), FULL)
    return call(
        unpack_body,
        (struct((32, 64), FULL), struct((64, 128), FULL), struct((128, 256), FULL), struct((240, 49), FULL))
        + (struct((128, 512), FULL), struct((256, 512), FULL))
        + (vector(2), vector(4))
        + (vector(8),) * 7
        + (struct((16, 32), FULL), vector(16), vector(15), vector(8), vector(8)),
        in_specs=[VMEM_SPEC] * 2,
        scratch_shapes=[pltpu.VMEM((C_ROWS, 128), LOW)],
    )(full, final)


def widen_body(values, out_e, out_r):
    out_e[...] = values[0:512, :].astype(FULL)
    out_r[...] = values[512:1024, :].astype(FULL)


def widen(values):
    return call(widen_body, (struct((512, 512), FULL),) * 2)(values)


def swap(values, pairs):
    return lax.ppermute(values, "dp", pairs)


def exchange(blocks):
    return (
        blocks[0],
        swap(blocks[1], CORE_SWAP),
        swap(blocks[2], CHIP_SWAP),
        swap(blocks[3], BOTH_SWAP),
    )


def gather(values):
    across = swap(values, CHIP_SWAP)
    return (values, swap(values, CORE_SWAP), across, swap(across, CORE_SWAP))


def hold(*values):
    return lax.optimization_barrier(values)


def onward(keeps, gots):
    parts = [(k[1].astype(FULL) + g[1].astype(FULL)).astype(LOW) for k, g in zip(keeps, gots)]
    return parts[0] if len(parts) == 1 else jnp.concatenate(parts, axis=0)


def own(keeps, gots, other):
    parts, row = [], 0
    for k, g in zip(keeps, gots):
        value = k[0].astype(FULL) + g[0].astype(FULL) + other[row : row + k.shape[1]].astype(FULL)
        parts.append(value.astype(LOW))
        row += k.shape[1]
    return parts[0] if len(parts) == 1 else jnp.concatenate(parts, axis=0)


def split(values, count):
    return values.reshape(count, -1, values.shape[-1])


def trade(parts):
    return lax.all_to_all(parts, "mp", split_axis=0, concat_axis=0, tiled=True)


def spread_sum(parts):
    value = jnp.sum(parts.astype(FULL), axis=0).astype(LOW)
    return jnp.broadcast_to(value[None], parts.shape)


def flat(parts):
    return parts.reshape(-1, parts.shape[2])


def per_device(
    mp_count,
    block_input,
    norm1_gain,
    norm1_bias,
    input_weight,
    input_bias,
    conv_weight,
    conv_bias,
    gate_weight1,
    gate_bias1,
    gate_weight2,
    gate_bias2,
    gate_weight3,
    gate_bias3,
    output_weight,
    output_bias,
    layer_scale1,
    norm2_gain,
    norm2_bias,
    expand_weight,
    expand_bias,
    reduce_weight,
    reduce_bias,
    layer_scale2,
    cotangent,
):
    me = lax.axis_index("dp").astype(jnp.int32).reshape(1)

    def turned(weight):
        return jnp.transpose(weight, (1, 2, 0)).reshape(-1, weight.shape[0])

    small, *x_blocks = first_kernel(
        me,
        block_input.reshape(SHARD, -1),
        (
            turned(output_weight),
            turned(gate_weight3),
            turned(gate_weight2),
            turned(gate_weight1),
            turned(conv_weight),
            norm1_gain,
            norm1_bias,
            input_bias,
            conv_bias,
            gate_bias1,
            gate_bias2,
            gate_bias3,
            output_bias,
            layer_scale1,
            norm2_gain,
            norm2_bias,
            reduce_bias,
            layer_scale2,
            expand_bias.T,
        ),
    )
    in_weight = turned(input_weight)
    in_across = swap(in_weight, CHIP_SWAP)
    small, x_blocks, in_across = hold(small, x_blocks, in_across)
    small_across = swap(small, CHIP_SWAP)
    x_blocks = exchange(x_blocks)
    slabs = (small, swap(small, CORE_SWAP), small_across, swap(small_across, CORE_SWAP))
    in_shards = (in_weight, swap(in_weight, CORE_SWAP), in_across, swap(in_across, CORE_SWAP))
    own_dy, near, far = second_kernel(
        me, cotangent.reshape(SHARD, -1), turned(expand_weight), reduce_weight.reshape(-1, WIDTH)
    )
    vec, expand, w1, w1_back, w2, w3, w_in, w_out, taps, perm = prepare(me, slabs, in_shards)
    x_blocks, near, far, vec = hold(x_blocks, near, far, vec)
    core, across = swap(near, CORE_SWAP), swap(far, CHIP_SWAP)
    x, z1, u, dwv = front(x_blocks, perm, vec, w_in, taps)
    dwv, core = hold(dwv, core)
    z2 = branch_forward(dwv, x, vec, w1, w2, w3, w_out)
    z2, across = hold(z2, across)
    joints = (near, core, across, swap(across, CORE_SWAP))
    dy, f, dz, bias_grads, sib_g, keep_g = feed_forward(z2, own_dy, joints, perm, vec, expand)


    got_g = swap(sib_g, CORE_SWAP)
    on_g = onward([keep_g], [got_g])
    dz, on_g = hold(dz, on_g)
    other_g = swap(on_g, CHIP_SWAP)
    *outs, g, dx1, sib, keep_late = branch_backward(
        me, dwv, x, dy, f, dz, vec, w1, w1_back, w2, w3, w_out, perm, bias_grads
    )
    got_late = swap(sib, CORE_SWAP)
    g, other_g, outs = hold(g, other_g, outs)
    part_g = split(own([keep_g], [got_g], other_g), mp_count)
    g, part_g = hold(g, part_g)
    part_g = trade(part_g)
    outs = exchange(outs)

    du1, sib, keep1 = conv_backward(me, g, u, taps, z1, 4)
    got1 = swap(sib, CORE_SWAP)
    du1, part_g, got_late, got1 = hold(du1, part_g, got_late, got1)
    high = [keep_late, keep1], [got_late, got1]
    full_g, on_h = spread_sum(part_g), onward(*high)
    g, full_g, on_h = hold(g, full_g, on_h)
    full_g = trade(full_g)
    other_h = swap(on_h, CHIP_SWAP)

    du0, sib, keep0 = conv_backward(me, g, u, taps, z1, 0)
    got0 = swap(sib, CORE_SWAP)
    du0, full_g, other_h, got0, outs = hold(du0, full_g, other_h, got0, outs)
    part_h, on_l = split(own(*high, other_h), mp_count), onward([keep0], [got0])
    du0, part_h, on_l = hold(du0, part_h, on_l)
    part_h = trade(part_h)
    other_l = swap(on_l, CHIP_SWAP)

    *ins, e0, e1, e2, e3 = input_backward(me, (du0, du1), x, dx1, vec, w_in, perm)
    ins = exchange(ins)
    ends = exchange((e0, e1, e2, e3))
    e0, other_l, part_h = hold(e0, other_l, part_h)
    part_l = split(own([keep0], [got0], other_l), mp_count)
    mixed = trade(jnp.concatenate([spread_sum(part_h), part_l], axis=1))
    mixed, ins = hold(mixed, ins)
    full_h, part_l = mixed[:, : -part_l.shape[1]], mixed[:, -part_l.shape[1] :]
    end = sum(e.astype(FULL) for e in ends).astype(LOW)
    end = jnp.broadcast_to(end[None], (mp_count,) + end.shape)
    full_l = trade(jnp.concatenate([spread_sum(part_l), end], axis=1))

    def back(values, blocks):
        return jnp.transpose(values.reshape(blocks, 16, values.shape[1]), (2, 0, 1))

    sum_e, sum_r = widen(flat(full_g))
    (
        g1, g2, g3, gconv, gout, gin, gb1, gb2, gb3, gob, gls1, gn2g, gn2b, grb, gls2, geb, ginb, gcb, gn1g, gn1b,
    ) = unpack_small(flat(full_h), full_l)
    block_output = from_pixels(me, outs).reshape(block_input.shape)
    input_grad = from_pixels(me, ins).reshape(block_input.shape)
    return (
        block_output,
        input_grad,
        gn1g,
        gn1b,
        back(gin, 16),
        ginb,
        back(gconv, 15),
        gcb,
        back(g1, 2),
        gb1,
        back(g2, 4),
        gb2,
        back(g3, 8),
        gb3,
        back(gout, 8),
        gob,
        gls1,
        gn2g,
        gn2b,
        back(sum_e, 32),
        geb.T,
        sum_r.reshape(32, 16, WIDTH),
        grb,
        gls2,
    )


def solution(mesh):
    pixels = P(None, "dp", "mp")
    vector = P(None, "dp")
    matrix = P(None, None, "dp")
    params = (
        vector, vector, matrix, vector, matrix, vector, matrix, vector, matrix, vector, matrix, vector,
        matrix, vector, vector, vector, vector, matrix, vector, P(None, "dp", None), vector, vector,
    )
    return jax.shard_map(
        partial(per_device, mesh.shape["mp"]),
        mesh=mesh,
        in_specs=(pixels,) + params + (pixels,),
        out_specs=(pixels, pixels) + params,
        check_vma=False,
    )
```

```python
from functools import partial

import jax
import jax.numpy as jnp
from jax import lax
from jax.experimental import pallas as pl
from jax.experimental.pallas import tpu as pltpu
from jax.sharding import PartitionSpec as P

WIDTH = 512
GROUP = 64
SIDE = 14
CROP = SIDE * SIDE
CROPS = 8
TOKENS = CROP * CROPS
SHARD = 128
TAPS = 49
EPSILON = 1e-06
LOW = jnp.bfloat16
FULL = jnp.float32
VMEM = 58 * 1024 * 1024

NN = (((1,), (0,)), ((), ()))
NT = (((1,), (1,)), ((), ()))
TN = (((0,), (0,)), ((), ()))

CORE_SWAP = [(0, 1), (1, 0), (2, 3), (3, 2)]
CHIP_SWAP = [(0, 2), (2, 0), (1, 3), (3, 1)]
BOTH_SWAP = [(0, 3), (3, 0), (1, 2), (2, 1)]

S_GATE3, S_GATE2, S_GATE1, S_CONV, S_EXPAND, S_OUT, S_ROWS = 0, 256, 320, 352, 560, 592, 1104
S_LANE = 64
(V_N1G, V_N1B, V_INB, V_CB, V_GB1, V_GB2, V_GB3, V_OB, V_LS1, V_N2G, V_N2B, V_RB, V_LS2) = range(13)
VECTORS = 13
E_OUT, E_VEC, E_EXPAND, E_ROWS = 0, 352 + 512, 496 + 512, 640 + 512
E_GATE = 512


def mm(left, right, dims=NN):
    return lax.dot_general(left, right, dims, preferred_element_type=FULL)


def call(body, out, weight=1.0, **kwargs):
    flops, moved = int(weight * 1.15e9 / 4), 1 << 10
    return pl.pallas_call(
        body,
        out_shape=out,
        compiler_params=pltpu.CompilerParams(vmem_limit_bytes=VMEM),
        cost_estimate=pl.CostEstimate(flops=flops, bytes_accessed=moved, transcendentals=0),
        **kwargs,
    )


def struct(shape, dtype):
    return jax.ShapeDtypeStruct(shape, dtype)


SMEM_SPEC = pl.BlockSpec(memory_space=pltpu.SMEM)


def whole(shape):
    return pl.BlockSpec(shape, lambda i: (0,) * len(shape))


def turn_blocks(me, x_ref, outs, wide, blocks):
    lanes = x_ref.shape[1]
    for dest in range(4):
        for crop in range(CROPS):
            start = CROP * (CROPS * dest + crop)
            base = start // 128 * 128
            window = x_ref[:, base : base + min(lanes - base, 384)].astype(FULL)
            wide[pl.ds(crop, CROP, stride=CROPS), :] = window[:, start - base : start - base + CROP].T
        blocks[dest ^ me] = wide[...].astype(LOW)
    for k in range(4):
        outs[k][...] = blocks[k]


PIXEL_SCRATCH = [pltpu.VMEM((TOKENS, SHARD), FULL), pltpu.VMEM((4, TOKENS, SHARD), LOW)]


W_FIRST = 2 * TOKENS
JOINT = W_FIRST + 4 * 1024


def second_body(me_ref, x_ref, expand, reduce, own, near, far, wide, blocks):
    places = (own, near.at[0:TOKENS], far.at[0:TOKENS], far.at[TOKENS:W_FIRST])
    turn_blocks(me_ref[0], x_ref, places, wide, blocks)
    for part in range(4):
        lanes = slice(part * 128, part * 128 + 128)
        first = W_FIRST + part * 1024
        for out in (near, far):
            out[first : first + 512, :] = expand[:, lanes]
            out[first + 512 : first + 1024, :] = reduce[:, lanes]


def second_kernel(me, x, expand, reduce):
    joint = struct((JOINT, SHARD), LOW)
    return call(
        second_body,
        (struct((TOKENS, SHARD), LOW), joint, joint),
        weight=0.05,
        in_specs=[SMEM_SPEC] + [pl.BlockSpec(memory_space=pltpu.VMEM)] * 3,
        scratch_shapes=PIXEL_SCRATCH,
    )(me, x, expand, reduce)


def first_body(me_ref, x_ref, *refs):
    pack_body(*refs[:19], refs[19], refs[24])
    turn_blocks(me_ref[0], x_ref, refs[20:24], refs[25], refs[26])


def first_kernel(me, x, small):
    return call(
        first_body,
        (struct((S_ROWS, 128), LOW),) + (struct((TOKENS, SHARD), LOW),) * 4,
        weight=0.05,
        in_specs=[SMEM_SPEC] + [pl.BlockSpec(memory_space=pltpu.VMEM)] * 20,
        scratch_shapes=[pltpu.VMEM((S_OUT, 128), FULL)] + PIXEL_SCRATCH,
    )(me, x, *small)


def from_pixels_body(me_ref, own, core, across, passed, out_ref, wide, blocks):
    me = me_ref[0]
    blocks[me] = own[...]
    blocks[1 ^ me] = core[...]
    blocks[2 ^ me] = across[0]
    blocks[3 ^ me] = passed[1]
    for source in range(4):
        wide[...] = blocks[source].astype(FULL)
        for crop in range(CROPS):
            start = CROP * (CROPS * source + crop)
            part = wide[pl.ds(crop, CROP, stride=CROPS), :].T
            out_ref[:, start : start + CROP] = part.astype(LOW)


def from_pixels(me, blocks):
    return call(
        from_pixels_body,
        struct((SHARD, 4 * TOKENS), LOW),
        weight=4.0,
        in_specs=[SMEM_SPEC] + [pl.BlockSpec(memory_space=pltpu.VMEM)] * 4,
        scratch_shapes=[pltpu.VMEM((TOKENS, SHARD), FULL), pltpu.VMEM((4, TOKENS, SHARD), LOW)],
    )(me, *blocks)


FAR = (2, TOKENS, SHARD)


def far_spec(tile):
    return pl.BlockSpec((2, tile, SHARD), lambda i: (0, i, 0))


def pack_body(out_weight, g3, g2, g1, conv, *refs):
    vectors, expand, out_ref, slab = refs[:VECTORS], refs[VECTORS], refs[VECTORS + 1], refs[VECTORS + 2]
    slab[...] = jnp.zeros_like(slab)
    slab[S_GATE3 : S_GATE3 + 128, :] = g3[:, :128].astype(FULL)
    slab[S_GATE3 + 128 : S_GATE3 + 256, :] = g3[:, 128:].astype(FULL)
    slab[S_GATE2 : S_GATE2 + 64, :] = g2[...].astype(FULL)
    slab[S_GATE1 : S_GATE1 + 32, :GROUP] = g1[...].astype(FULL)
    slab[S_CONV : S_CONV + 240, :TAPS] = conv[...].astype(FULL)
    for number, ref in enumerate(vectors):
        first = S_CONV + 16 * number + (1 if number == V_CB else 0)
        slab[first : first + ref.shape[0], S_LANE : S_LANE + 16] = ref[...].astype(FULL)
    slab[S_EXPAND : S_EXPAND + 32, S_LANE : S_LANE + 16] = expand[...].astype(FULL).T
    out_ref[0:S_OUT, :] = slab[...].astype(LOW)
    for part in range(4):
        rows = slice(S_OUT + part * 128, S_OUT + part * 128 + 128)
        out_ref[rows, :] = out_weight[:, part * 128 : part * 128 + 128]


TILE_OF = (2, 0, 3, 1)


def iota(shape, dim):
    return lax.broadcasted_iota(jnp.int32, shape, dim)


def spread(lanes):
    return jnp.where(iota((128, lanes), 1) % 16 + S_LANE == iota((128, lanes), 0), 1.0, 0.0).astype(LOW)


def prepare_body(me_ref, *refs):
    slabs, ins = refs[0:4], refs[4:8]
    vec, expand, w1, w1_back, w2, w3, w_in, w_out, taps, perm, channels = refs[8:]
    me = me_ref[0]
    totals = jnp.zeros((VECTORS, 1024), FULL)
    spread_wide = spread(1024)
    row = iota((VECTORS * 16, 1024), 0) % 16
    lane = iota((VECTORS * 16, 1024), 1)
    in_row = row == lane // 64
    spread_expand = spread(512)
    expand_rows = iota((32, 512), 0) == iota((32, 512), 1) // 16
    w1[...] = jnp.zeros_like(w1)
    channels[0:GROUP, :] = jnp.where(iota((GROUP, 128), 1) == TAPS // 2, 3.0, 0.0)
    for k in range(4):
        source = me ^ k
        slab = slabs[k]
        values = mm(slab[S_CONV : S_CONV + VECTORS * 16, :], spread_wide)
        values = jnp.where(in_row & (lane // 16 % 4 == source), values, 0.0)
        totals = totals + jnp.sum(values.reshape(VECTORS, 16, 1024), axis=1)
        values = mm(slab[S_EXPAND : S_EXPAND + 32, :], spread_expand)
        values = jnp.sum(jnp.where(expand_rows, values, 0.0), axis=0, keepdims=True)
        slot = TILE_OF[k]
        expand[8 * slot : 8 * slot + 8, :] = jnp.broadcast_to(values, (8, 512))
        for a in range(16):
            place = pl.ds(pl.multiple_of(a * 64 + source * 16, 16), 16)
            rows = slice(a * 16, a * 16 + 16)
            w_in[place, :] = ins[k][rows, :]
            if a < 15:
                later = pl.ds(pl.multiple_of((a + 1) * 64 + source * 16, 16), 16)
                channels[later, :] = slab[S_CONV + a * 16 : S_CONV + a * 16 + 16, :].astype(FULL)
            if a < 8:
                for part in range(4):
                    first = S_OUT + part * 128 + a * 16
                    w_out[place, part * 128 : part * 128 + 128] = slab[first : first + 16, :]
                w3[place, 0:128] = slab[S_GATE3 + a * 16 : S_GATE3 + a * 16 + 16, :]
                w3[place, 128:256] = slab[S_GATE3 + 128 + a * 16 : S_GATE3 + 128 + a * 16 + 16, :]
            if a < 4:
                w2[place, :] = slab[S_GATE2 + a * 16 : S_GATE2 + a * 16 + 16, :]
            if a < 2:
                w1[place, :] = slab[S_GATE1 + a * 16 : S_GATE1 + a * 16 + 16, :]
        column = iota((SHARD, WIDTH), 0)
        target = column // 16 * 64 + source * 16 + column % 16
        perm[k * SHARD : (k + 1) * SHARD, :] = jnp.where(iota((SHARD, WIDTH), 1) == target, 1.0, 0.0).astype(LOW)
    vec[0:VECTORS, :] = totals
    vec[VECTORS:16, :] = jnp.zeros((16 - VECTORS, 1024), FULL)
    single = w1[...].astype(FULL)
    w1_back[...] = (single + pltpu.roll(single, GROUP, 1)).astype(LOW)
    taps[...] = channels[...].T[0:64, :]


def prepare(me, slabs, ins):
    return call(
        prepare_body,
        (
            struct((16, 1024), FULL),
            struct((32, 512), FULL),
            struct((128, 128), LOW),
            struct((128, 128), LOW),
            struct((256, 128), LOW),
            struct((512, 256), LOW),
            struct((1024, 512), LOW),
            struct((512, 512), LOW),
            struct((64, 1024), FULL),
            struct((512, 512), LOW),
        ),
        weight=0.05,
        in_specs=[SMEM_SPEC] + [pl.BlockSpec(memory_space=pltpu.VMEM)] * 8,
        scratch_shapes=[pltpu.VMEM((1024, 128), FULL)],
    )(me, *slabs, *ins)


def normed(values):
    center = jnp.sum(values, axis=1, keepdims=True) * (1.0 / WIDTH)
    away = values - center
    spread_sq = jnp.sum(away * away, axis=1, keepdims=True) * (1.0 / WIDTH)
    inverse = lax.rsqrt(spread_sq + EPSILON)
    return away * inverse, inverse


def norm_back(grad, unit, inverse, gain):
    grad_unit = grad * gain
    first = jnp.sum(grad_unit, axis=1, keepdims=True) * (1.0 / WIDTH)
    second = jnp.sum(grad_unit * unit, axis=1, keepdims=True) * (1.0 / WIDTH)
    return inverse * (grad_unit - first - unit * second)


def total(values):
    return jnp.sum(values, axis=0, keepdims=True)


def row(vec, number, lanes=WIDTH):
    return vec[number : number + 1, 0:lanes]


def rows_spec(tile, lanes):
    return pl.BlockSpec((tile, lanes), lambda i: (i, 0))


def chunks(count, size, body):
    def step(i, carry):
        body(pl.ds(pl.multiple_of(i * size, size), size))
        return carry

    lax.fori_loop(0, count // size, step, 0)


NORM_ROWS = 224
HALVES = (slice(0, TOKENS // 2), slice(TOKENS // 2, TOKENS))


def stagger(chain, height, lead):
    cut = height // 32 * 16
    ahead, behind = chain(slice(0, cut)), chain(slice(cut, height))
    for _ in range(lead):
        next(ahead)
    for _ in ahead:
        next(behind)
    for _ in behind:
        pass


def join(blocks, perm, rows):
    return mm(jnp.concatenate([r[rows, :] for r in blocks], axis=1), perm[...])


def conv_rows(source, weights, emit, flip):
    zero = jnp.zeros((CROPS, 128), FULL)

    def tap_row(i, r, sums):
        base = (i + r - 3) * SIDE
        values = [source[base + c] for c in range(SIDE)]
        first = (6 - r) * 7 if flip else r * 7
        taps = [weights[first + (6 - s if flip else s)] for s in range(7)]
        for s in range(7):
            for c in range(SIDE):
                if 0 <= c + s - 3 < SIDE:
                    sums[c] = sums[c] + taps[s] * values[c + s - 3]

    def one_row(i, first, last):
        sums = [zero] * SIDE
        for r in range(first, last):
            tap_row(i, r, sums)
        emit(i, sums)

    def inner_row(i, carry):
        one_row(i, 0, 7)
        return carry

    for i in range(3):
        one_row(i, 3 - i, 7)
    lax.fori_loop(3, SIDE - 3, inner_row, 0)
    for i in range(SIDE - 3, SIDE):
        one_row(i, 0, 17 - i)


def wide_taps(taps, weights):
    for tap in range(TAPS):
        weights[tap] = jnp.broadcast_to(taps[tap : tap + 1, :], (CROPS, 128))


PIXEL_BLOCK = pl.BlockSpec((CROP, CROPS, 128), lambda i: (0, 0, i))


def lane_block(rows):
    return pl.BlockSpec((rows, 128), lambda i: (0, i))


def front_body(r0, r1, r2, r3, perm, vec, w_in, taps, vec_part, x, z, u, dwv, weights):
    @pl.when(pl.program_id(0) == 0)
    def _():
        for rows in HALVES:
            x[rows, :] = join((r0, r1, r2, r3), perm, rows).astype(LOW)

        def norm_rows(rows):
            unit, _ = normed(x[rows, :].astype(FULL))
            z[rows, :] = (unit * row(vec, V_N1G) + row(vec, V_N1B)).astype(LOW)

        chunks(TOKENS, NORM_ROWS, norm_rows)

    wide_taps(taps, weights)
    values = mm(z[...], w_in[...], NT) + vec_part[V_INB : V_INB + 1, :]
    u[...] = values.reshape(CROP, CROPS, 128)
    bias = jnp.broadcast_to(vec_part[V_CB : V_CB + 1, :], (CROPS, 128))

    def emit(i, sums):
        for c in range(SIDE):
            dwv[i * SIDE + c] = (sums[c] + bias) * (1.0 / 3.0)

    conv_rows(u, weights, emit, False)


def front(blocks, perm, vec, w_in, taps):
    pixels = struct((CROP, CROPS, 1024), FULL)
    rows = struct((TOKENS, WIDTH), LOW)
    x, z, u, dwv = call(
        front_body,
        (rows, rows, pixels, pixels),
        weight=28.0,
        grid=(8,),
        in_specs=[whole((TOKENS, SHARD))] * 4
        + [
            whole((512, 512)),
            whole((16, 1024)),
            pl.BlockSpec((128, 512), lambda i: (i, 0)),
            lane_block(64),
            lane_block(16),
        ],
        out_specs=(whole((TOKENS, WIDTH)), whole((TOKENS, WIDTH)), PIXEL_BLOCK, PIXEL_BLOCK),
        scratch_shapes=[pltpu.VMEM((TAPS, CROPS, 128), FULL)],
    )(*blocks, perm, vec, w_in, taps, vec)
    return x, z, u, dwv.reshape(TOKENS, 1024)


def branch_body(dwv, x, vec, w1, w2, w3, w_out, z_out):
    def chain(rows):
        first = dwv[rows, 0:128]
        q = (first * pltpu.roll(first, GROUP, 1)).astype(LOW)
        yield
        t = mm(q, w1[...], NT) + row(vec, V_GB1, 128)
        q = (t * dwv[rows, 128:256]).astype(LOW)
        yield
        t = mm(q, w2[...], NT) + row(vec, V_GB2, 256)
        q = (t * dwv[rows, 256:512]).astype(LOW)
        yield
        t = mm(q, w3[...], NT) + row(vec, V_GB3, 512)
        q = (t * dwv[rows, 512:1024]).astype(LOW)
        yield
        branch = mm(q, w_out[...], NT) + row(vec, V_OB)
        middle = x[rows, :].astype(FULL) + row(vec, V_LS1) * branch
        yield
        unit, _ = normed(middle)
        z_out[rows, :] = (unit * row(vec, V_N2G) + row(vec, V_N2B)).astype(LOW)
        yield

    stagger(chain, dwv.shape[0], 2)


def branch_forward(dwv, x, vec, w1, w2, w3, w_out, tile=784):
    return call(
        branch_body,
        struct((TOKENS, WIDTH), LOW),
        weight=7.0,
        grid=(TOKENS // tile,),
        in_specs=[
            rows_spec(tile, 1024),
            rows_spec(tile, WIDTH),
            whole((16, 1024)),
            whole((128, 128)),
            whole((256, 128)),
            whole((512, 256)),
            whole((512, 512)),
        ],
        out_specs=rows_spec(tile, WIDTH),
    )(dwv, x, vec, w1, w2, w3, w_out)


def gelu_parts(s):
    bell = jnp.exp2((-0.5 * 1.4426950408889634) * (s * s))
    size = jnp.abs(s)
    t = pltpu.reciprocal(1.0 + (0.3275911 * 0.7071067811865476) * size, approx=True)
    poly = 0.5 * 1.061405429
    for coefficient in (-1.453152027, 1.421413741, -0.284496736, 0.254829592):
        poly = poly * t + 0.5 * coefficient
    tail = poly * t * bell
    cdf = jnp.where(s >= 0.0, 1.0 - tail, tail)
    return s * cdf, cdf + s * (bell * 0.3989422804014327)


PIECE = 16


def mlp_body(z, r0, perm, vec, expand, c0, c1, c2, c3, *refs):
    dy, f, dz, gb, sibling, keep = refs[0:6]
    r1, r2, r3, we, wr, df, s0, s1, g0, g1, hid, grad_s, grads, sums, sems = refs[6:]
    pre, grad_h = (s0, s1), (g0, g1)
    half = TOKENS // 2
    shards = (c1, c3, c0, c2)

    def copies(slot):
        for part in range(4):
            for number, matrix in enumerate((we, wr)):
                rows = pl.ds(W_FIRST + part * 1024 + number * 512, 512)
                yield pltpu.make_async_copy(
                    shards[slot].at[rows], matrix.at[slot, :, pl.ds(part * 128, 128)], sems.at[slot]
                )

    near = [
        pltpu.make_async_copy(shard.at[pl.ds(first, TOKENS)], r, sems.at[4 + number])
        for number, (shard, first, r) in enumerate(((c1, 0, r1), (c2, 0, r2), (c3, TOKENS, r3)))
    ]
    for copy in near:
        copy.start()
    for slot in range(4):
        for copy in copies(slot):
            copy.start()

    def arrived(slot):
        for matrix in (we, wr):
            pltpu.make_async_copy(matrix.at[slot], matrix.at[slot], sems.at[slot]).wait()

    def leave(tile):
        out = (sibling, keep)[tile // 2]
        return [
            pltpu.make_async_copy(
                grads.at[tile, :, pl.ds(part * 128, 128)],
                out.at[tile % 2, pl.ds(part * 1024, 1024)],
                sems.at[7 + tile],
            )
            for part in range(4)
        ]

    def start(copies):
        for copy in copies:
            copy.start()

    for copy in near:
        copy.wait()
    for rows in HALVES:
        dy[rows, :] = join((r0, r1, r2, r3), perm, rows).astype(LOW)

    def scaled(rows):
        df[rows, :] = (dy[rows, :].astype(FULL) * row(vec, V_LS2)).astype(LOW)
        f[rows, :] = jnp.zeros((112, WIDTH), FULL)
        dz[rows, :] = jnp.zeros((112, WIDTH), FULL)

    chunks(TOKENS, 112, scaled)
    sums[...] = jnp.zeros_like(sums)
    hid[1] = jnp.zeros((TOKENS, 512), LOW)
    grad_s[1] = jnp.zeros((TOKENS, 512), LOW)
    arrived(0)
    s0[...] = mm(z[HALVES[0], :], we[0], NT)
    g0[...] = mm(df[HALVES[0], :], wr[0], NT)
    pieces = half // PIECE

    def unit(here, tile, before, after):
        there = 1 - here
        rows = HALVES[there]
        now, last = tile & 1, (tile & 1) ^ 1
        ready = last if here == 0 else now
        bias = expand[pl.ds(pl.multiple_of(tile * 8, 8), 1), :]
        done = [0]
        column = [jnp.zeros((8, 512), FULL)]

        def some(part):
            while done[0] < pieces * part // 6:
                first = done[0] * PIECE
                piece = slice(first, first + PIECE)
                place = slice(here * half + first, here * half + first + PIECE)
                act, slope = gelu_parts(pre[here][piece, :] + bias)
                hid[now, place, :] = act.astype(LOW)
                grad = (grad_h[here][piece, :] * slope).astype(LOW)
                grad_s[now, place, :] = grad
                grad = grad.astype(FULL)
                column[0] = column[0] + (grad[0:8] + grad[8:16])
                done[0] += 1

        if here == 0:
            grads[before, 0:512, :] = mm(grad_s[last], z[...], TN).astype(LOW)
        else:
            grads[before, 512:1024, :] = mm(hid[last], df[...], TN).astype(LOW)
        some(2)
        pre[there][...] = mm(z[rows, :], we[after], NT)
        some(3)
        grad_h[there][...] = mm(df[rows, :], wr[after], NT)
        some(4)
        f[rows, :] += mm(hid[ready, rows, :], wr[before if here == 0 else tile])
        some(5)
        dz[rows, :] += mm(grad_s[ready, rows, :], we[before if here == 0 else tile])
        some(6)
        sums[tile] += column[0]

    def one_tile(tile, carry):
        before = jnp.maximum(tile - 1, 0)
        for number in range(2):

            @pl.when(tile == number + 2)
            def _():
                start(leave(number))

        unit(0, tile, before, tile)

        @pl.when(tile < 3)
        def _():
            arrived(tile + 1)

        unit(1, tile, before, jnp.minimum(tile + 1, 3))
        return carry

    lax.fori_loop(0, 4, one_tile, 0)
    start(leave(2))
    rows = HALVES[1]
    grads[3, 0:512, :] = mm(grad_s[1], z[...], TN).astype(LOW)
    grads[3, 512:1024, :] = mm(hid[1], df[...], TN).astype(LOW)
    start(leave(3))
    f[rows, :] += mm(hid[1, rows, :], wr[3])
    dz[rows, :] += mm(grad_s[1, rows, :], we[3])
    for tile in range(4):
        gb[8 * tile : 8 * tile + 8, :] = sums[tile]
    for tile in range(4):
        for copy in leave(tile):
            copy.wait()


def feed_forward(z, own_dy, joints, perm, vec, expand):
    vmem = pl.BlockSpec(memory_space=pltpu.VMEM)
    anywhere = pl.BlockSpec(memory_space=pl.ANY)
    half = TOKENS // 2
    pair = struct((2, 4096, 128), LOW)
    rows = struct((TOKENS, WIDTH), FULL)
    return call(
        mlp_body,
        (struct((TOKENS, WIDTH), LOW), rows, rows, struct((32, 512), FULL), pair, pair),
        weight=40.0,
        in_specs=[vmem] * 5 + [anywhere] * 4,
        out_specs=(vmem,) * 4 + (anywhere,) * 2,
        scratch_shapes=[pltpu.VMEM((TOKENS, SHARD), LOW)] * 3
        + [pltpu.VMEM((4, 512, 512), LOW)] * 2
        + [pltpu.VMEM((TOKENS, WIDTH), LOW)]
        + [pltpu.VMEM((half, 512), FULL)] * 4
        + [pltpu.VMEM((2, TOKENS, 512), LOW)] * 2
        + [pltpu.VMEM((4, 1024, 512), LOW)]
        + [pltpu.VMEM((4, 8, 512), FULL)]
        + [pltpu.SemaphoreType.DMA((11,))],
    )(z, own_dy, perm, vec, expand, *joints)


def pack_vectors(values, count, source):
    lane = iota((count * 16, 1024), 1)
    keep = (iota((count * 16, 1024), 0) % 16 == lane // 64) & (lane // 16 % 4 == source)
    tall = jnp.broadcast_to(values[:, None, :], (count, 16, 1024)).reshape(count * 16, 1024)
    gather = jnp.where(iota((1024, 128), 0) % 16 == iota((1024, 128), 1), 1.0, 0.0).astype(LOW)
    return mm(jnp.where(keep, tall, 0.0).astype(LOW), gather)


def part_pair(parts, sibling, keep):
    sibling[0] = parts[1]
    sibling[1] = parts[3]
    keep[0] = parts[0]
    keep[1] = parts[2]


def branch_back_body(steps, me_ref, dwv, x, dy, f, dz, vec, w1, w1_back, w2, w3, w_out, perm, gb, *refs):
    (o0, o1, far, g_out, dx_out, sibling, keep) = refs[0:7]
    acc_o, acc_3, acc_2, acc_1, sums, parts = refs[7:]
    step = pl.program_id(0)

    @pl.when(step == 0)
    def _():
        acc_o[...] = jnp.zeros_like(acc_o)
        acc_3[...] = jnp.zeros_like(acc_3)
        acc_2[...] = jnp.zeros_like(acc_2)
        acc_1[...] = jnp.zeros_like(acc_1)
        sums[...] = jnp.zeros_like(sums)

    third = 1.0 / 3.0

    def chain(rows):
        first = dwv[rows, 0:128]
        turned = pltpu.roll(first, GROUP, 1)
        q0 = (first * turned).astype(LOW)
        yield
        t1 = mm(q0, w1[...], NT) + row(vec, V_GB1, 128)
        q1 = (t1 * dwv[rows, 128:256]).astype(LOW)
        yield
        t2 = mm(q1, w2[...], NT) + row(vec, V_GB2, 256)
        q2 = (t2 * dwv[rows, 256:512]).astype(LOW)
        yield
        t3 = mm(q2, w3[...], NT) + row(vec, V_GB3, 512)
        q3 = (t3 * dwv[rows, 512:1024]).astype(LOW)
        yield
        branch = mm(q3, w_out[...], NT) + row(vec, V_OB)
        middle = x[rows, :].astype(FULL) + row(vec, V_LS1) * branch
        yield
        unit, inverse = normed(middle)
        yield
        grad = dz[rows, :]
        top = dy[rows, :].astype(FULL)
        middle_grad = top + norm_back(grad, unit, inverse, row(vec, V_N2G))
        dx_out[rows, :] = middle_grad
        sums[4:5, 0:512] += total(middle_grad * branch)
        sums[5:6, 0:512] += total(grad * unit)
        sums[6:7, 0:512] += total(grad)
        grad_branch = (middle_grad * row(vec, V_LS1)).astype(LOW)
        yield
        back = mm(grad_branch, w_out[...])
        gt3 = (back * dwv[rows, 512:1024]).astype(LOW)
        g_out[rows, 512:1024] = back * t3 * third
        yield
        back = mm(gt3, w3[...])
        acc_o[...] += mm(grad_branch, q3, TN)
        sums[3:4, 0:512] += total(grad_branch.astype(FULL))
        gt2 = (back * dwv[rows, 256:512]).astype(LOW)
        g_out[rows, 256:512] = back * t2 * third
        yield
        back = mm(gt2, w2[...])
        acc_3[...] += mm(gt3, q2, TN)
        sums[2:3, 0:512] += total(gt3.astype(FULL))
        gt1 = (back * dwv[rows, 128:256]).astype(LOW)
        g_out[rows, 128:256] = back * t1 * third
        yield
        back = mm(gt1, w1_back[...])
        acc_2[...] += mm(gt2, q1, TN)
        acc_1[...] += mm(gt1, q0, TN)
        sums[1:2, 0:256] += total(gt2.astype(FULL))
        sums[0:1, 0:128] += total(gt1.astype(FULL))
        g_out[rows, 0:128] = back * turned * third
        yield
        mlp = f[rows, :] + row(vec, V_RB)
        output = (middle + row(vec, V_LS2) * mlp).astype(LOW)
        sums[7:8, 0:512] += total(top) * row(vec, V_LS2)
        sums[8:9, 0:512] += total(top * mlp)
        yield
        blocks = mm(output, perm[...], NT).astype(LOW)
        for k, ref in enumerate((o0, o1, far.at[0], far.at[1])):
            ref[rows, :] = blocks[:, k * SHARD : (k + 1) * SHARD]
        yield

    height = dwv.shape[0]
    stagger(chain, height, 3)

    @pl.when(step == steps - 1)
    def _():
        me = me_ref[0]
        vectors = sums[0:9, :]
        expand_rows = iota((32, 512), 0) == iota((32, 512), 1) // 16
        gather = jnp.where(iota((512, 128), 0) % 16 == iota((512, 128), 1), 1.0, 0.0).astype(LOW)
        for source in range(4):
            k = source ^ me
            for a in range(8):
                rows = slice(a * 64 + source * 16, a * 64 + source * 16 + 16)
                for part in range(4):
                    first = part * 128 + a * 16
                    parts[k, first : first + 16, :] = acc_o[rows, part * 128 : part * 128 + 128].astype(LOW)
                first = E_GATE + a * 16
                parts[k, first : first + 16, :] = acc_3[rows, 0:128].astype(LOW)
                parts[k, first + 128 : first + 144, :] = acc_3[rows, 128:256].astype(LOW)
                if a < 4:
                    parts[k, first + 256 : first + 272, :] = acc_2[rows, :].astype(LOW)
                if a < 2:
                    parts[k, first + 320 : first + 336, :] = acc_1[rows, :].astype(LOW)
            parts[k, E_VEC : E_VEC + 144, :] = pack_vectors(vectors, 9, source).astype(LOW)
        for k in range(4):
            slot = TILE_OF[k]
            line = total(gb[8 * slot : 8 * slot + 8, :])
            tall = jnp.where(expand_rows, jnp.broadcast_to(line, (32, 512)), 0.0)
            parts[k, E_EXPAND : E_EXPAND + 32, :] = mm(tall.astype(LOW), gather).astype(LOW)
            parts[k, E_EXPAND + 32 : E_ROWS, :] = jnp.zeros((E_ROWS - E_EXPAND - 32, 128), LOW)
        part_pair(parts, sibling, keep)


def branch_backward(me, dwv, x, dy, f, dz, vec, w1, w1_back, w2, w3, w_out, perm, biases, tile=784):
    steps = TOKENS // tile
    wide = rows_spec(tile, WIDTH)
    block = rows_spec(tile, SHARD)
    pair = (2, E_ROWS, 128)
    return call(
        partial(branch_back_body, steps),
        (struct((TOKENS, SHARD), LOW),) * 2
        + (
            struct(FAR, LOW),
            struct((TOKENS, 1024), FULL),
            struct((TOKENS, WIDTH), FULL),
            struct(pair, LOW),
            struct(pair, LOW),
        ),
        weight=20.0,
        grid=(steps,),
        in_specs=[
            SMEM_SPEC,
            rows_spec(tile, 1024),
            wide,
            wide,
            wide,
            wide,
            whole((16, 1024)),
            whole((128, 128)),
            whole((128, 128)),
            whole((256, 128)),
            whole((512, 256)),
            whole((512, 512)),
            whole((512, 512)),
        ]
        + [whole((32, 512))],
        out_specs=(block,) * 2 + (far_spec(tile), rows_spec(tile, 1024), wide, whole(pair), whole(pair)),
        scratch_shapes=[
            pltpu.VMEM((512, 512), FULL),
            pltpu.VMEM((512, 256), FULL),
            pltpu.VMEM((256, 128), FULL),
            pltpu.VMEM((128, 128), FULL),
            pltpu.VMEM((16, 1024), FULL),
            pltpu.VMEM((4, E_ROWS, 128), LOW),
        ],
    )(me, dwv, x, dy, f, dz, vec, w1, w1_back, w2, w3, w_out, perm, biases)


def conv_back_body(me_ref, g, u, taps, z, du, sibling, keep, weights, grad_taps, parts):
    step, steps = pl.program_id(0), pl.num_programs(0)
    me = me_ref[0]
    wide_taps(taps, weights)
    zero = jnp.zeros((CROPS, 128), FULL)

    def emit(i, sums):
        stacked = jnp.concatenate(list(sums), axis=0).astype(LOW)
        first = i * SIDE * CROPS if isinstance(i, int) else pl.multiple_of(i * SIDE * CROPS, 16)
        du[pl.ds(first, SIDE * CROPS), :] = stacked

    conv_rows(g, weights, emit, True)

    for r in range(7):

        def one_row(i, sums):
            grads = [g[i * SIDE + c] for c in range(SIDE)]
            values = [u[(i + r - 3) * SIDE + c] for c in range(SIDE)]
            sums = list(sums)
            for c in range(SIDE):
                for s in range(7):
                    if 0 <= c + s - 3 < SIDE:
                        sums[s] = sums[s] + grads[c] * values[c + s - 3]
            return tuple(sums)

        sums = lax.fori_loop(max(0, 3 - r), min(SIDE, SIDE + 3 - r), one_row, (zero,) * 7)
        for s in range(7):
            grad_taps[r * 7 + s : r * 7 + s + 1, :] = total(sums[s])
    grad_taps[49:50, :] = total(jnp.sum(g[...], axis=0))
    grad_taps[50:51, :] = total(du[...].astype(FULL))
    grad_taps[51:128, :] = jnp.zeros((77, 128), FULL)
    grad_w = mm(du[...], z[...], TN)
    tall = grad_taps[...].T.astype(LOW)
    for a in range(2):
        for source in range(4):
            k = source ^ me
            rows = slice(a * 64 + source * 16, a * 64 + source * 16 + 16)
            for part in range(4):
                place = pl.ds(pl.multiple_of(part * 128 + step * 32 + a * 16, 16), 16)
                parts[k, place, :] = grad_w[rows, part * 128 : part * 128 + 128].astype(LOW)
            place = pl.ds(pl.multiple_of(512 + step * 32 + a * 16, 16), 16)
            parts[k, place, :] = tall[rows, :]

    @pl.when(step == steps - 1)
    def _():
        part_pair(parts, sibling, keep)


C_ROWS = 640


def conv_backward(me, g, u, taps, z, base):
    pixels = pl.BlockSpec((CROP, CROPS, 128), lambda i: (0, 0, i + base))
    pair = (2, C_ROWS, 128)
    return call(
        conv_back_body,
        (struct((TOKENS, 512), LOW), struct(pair, LOW), struct(pair, LOW)),
        weight=24.0,
        grid=(4,),
        in_specs=[
            SMEM_SPEC,
            pixels,
            pixels,
            pl.BlockSpec((64, 128), lambda i: (0, i + base)),
            whole((TOKENS, WIDTH)),
        ],
        out_specs=(lane_block(TOKENS), whole(pair), whole(pair)),
        scratch_shapes=[
            pltpu.VMEM((TAPS, CROPS, 128), FULL),
            pltpu.VMEM((128, 128), FULL),
            pltpu.VMEM((4, C_ROWS, 128), LOW),
        ],
    )(me, g.reshape(CROP, CROPS, 1024), u, taps, z)


def input_back_body(steps, me_ref, du0, du1, x, dx, vec, w_in, perm, *refs):
    (o0, o1, far, e0, e1, e2, e3, sums, parts) = refs
    step = pl.program_id(0)

    @pl.when(step == 0)
    def _():
        sums[...] = jnp.zeros_like(sums)

    def chain(rows):
        grad = mm(jnp.concatenate([du0[rows, :], du1[rows, :]], axis=1), w_in[...])
        yield
        unit, inverse = normed(x[rows, :].astype(FULL))
        sums[0:1, 0:512] += total(grad * unit)
        sums[1:2, 0:512] += total(grad)
        yield
        grad_x = (dx[rows, :] + norm_back(grad, unit, inverse, row(vec, V_N1G))).astype(LOW)
        yield
        blocks = mm(grad_x, perm[...], NT).astype(LOW)
        for k, ref in enumerate((o0, o1, far.at[0], far.at[1])):
            ref[rows, :] = blocks[:, k * SHARD : (k + 1) * SHARD]
        yield

    stagger(chain, x.shape[0], 1)

    @pl.when(step == steps - 1)
    def _():
        me = me_ref[0]
        vectors = sums[0:2, :]
        for source in range(4):
            parts[source ^ me, :, :] = pack_vectors(vectors, 2, source).astype(LOW)
        for k, ref in enumerate((e0, e1, e2, e3)):
            ref[...] = parts[k]


def input_backward(me, dus, x, dx, vec, w_in, perm, tile=784):
    steps = TOKENS // tile
    wide = rows_spec(tile, WIDTH)
    end = (32, 128)
    return call(
        partial(input_back_body, steps),
        (struct((TOKENS, SHARD), LOW),) * 2 + (struct(FAR, LOW),) + (struct(end, LOW),) * 4,
        weight=8.0,
        grid=(steps,),
        in_specs=[
            SMEM_SPEC,
            *[rows_spec(tile, 512)] * 2,
            wide,
            wide,
            whole((16, 1024)),
            whole((1024, 512)),
            whole((512, 512)),
        ],
        out_specs=(rows_spec(tile, SHARD),) * 2 + (far_spec(tile),) + (whole(end),) * 4,
        scratch_shapes=[pltpu.VMEM((16, 1024), FULL), pltpu.VMEM((4, 32, 128), LOW)],
    )(me, *dus, x, dx, vec, w_in, perm)


def unpack_body(full, final, *refs):
    (g1, g2, g3, conv, w_out, w_in), late_refs, expand = refs[0:6], refs[6:15], refs[15]
    (in_bias, conv_bias, gain, bias), low = refs[16:20], refs[20]
    size = final.shape[1] - 32
    last = jnp.zeros((32, 128), FULL)
    for piece in range(final.shape[0]):
        low[piece * size : (piece + 1) * size, :] = final[piece, 0:size, :]
        last = last + final[piece, size : size + 32, :].astype(FULL)
    gates = full[E_GATE:E_VEC, :].astype(FULL)
    g3[:, 0:128] = gates[0:128]
    g3[:, 128:256] = gates[128:256]
    g2[...] = gates[256:320]
    g1[...] = gates[320:352, 0:GROUP]
    taps = []
    for j, (source, first) in enumerate(((low, 0), (low, C_ROWS))):
        for part in range(4):
            rows = slice(first + part * 128, first + part * 128 + 128)
            w_in[j * 128 : j * 128 + 128, part * 128 : part * 128 + 128] = source[rows, :].astype(FULL)
        taps.append(source[first + 512 : first + 640, :])
    for part in range(4):
        lanes = slice(part * 128, part * 128 + 128)
        w_out[:, lanes] = full[lanes, :].astype(FULL)
    taps = jnp.concatenate(taps, axis=0).astype(FULL)
    conv[...] = taps[16:256, 0:TAPS]
    vectors = full[E_VEC : E_VEC + 144, :].astype(FULL)
    for number, ref in enumerate(late_refs):
        ref[...] = vectors[16 * number : 16 * number + ref.shape[0], 0:16]
    expand[...] = full[E_EXPAND : E_EXPAND + 32, 0:16].astype(FULL).T
    gain[...] = last[0:8, 0:16]
    bias[...] = last[16:24, 0:16]
    own = jnp.where(iota((256, 16), 0) % 16 == iota((256, 16), 1), 1.0, 0.0)
    rows = jnp.where(iota((16, 256), 0) == iota((16, 256), 1) // 16, 1.0, 0.0).astype(LOW)
    conv_bias[...] = mm(rows, (taps[:, 49:50] * own).astype(LOW))[1:16, :]
    in_bias[...] = mm(rows, (taps[:, 50:51] * own).astype(LOW))


VMEM_SPEC = pl.BlockSpec(memory_space=pltpu.VMEM)


def unpack_small(full, final):
    vector = lambda rows: struct((rows, 16), FULL)
    return call(
        unpack_body,
        (struct((32, 64), FULL), struct((64, 128), FULL), struct((128, 256), FULL), struct((240, 49), FULL))
        + (struct((128, 512), FULL), struct((256, 512), FULL))
        + (vector(2), vector(4))
        + (vector(8),) * 7
        + (struct((16, 32), FULL), vector(16), vector(15), vector(8), vector(8)),
        in_specs=[VMEM_SPEC] * 2,
        scratch_shapes=[pltpu.VMEM((2 * C_ROWS, 128), LOW)],
    )(full, final)


def widen_body(values, out_e, out_r):
    size = values.shape[1]
    for piece in range(values.shape[0]):
        for first in range(piece * size, (piece + 1) * size, min(size, 512)):
            part, rest = first // 1024, first % 1024
            out = (out_e, out_r)[rest // 512]
            rows = slice(rest % 512, rest % 512 + min(size, 512))
            here = slice(first - piece * size, first - piece * size + min(size, 512))
            out[rows, part * 128 : part * 128 + 128] = values[piece, here, :].astype(FULL)


def widen(values):
    return call(widen_body, (struct((512, 512), FULL),) * 2)(values)


def swap(values, pairs):
    return lax.ppermute(values, "dp", pairs)


def exchange(blocks):
    return (
        blocks[0],
        swap(blocks[1], CORE_SWAP),
        swap(blocks[2], CHIP_SWAP),
        swap(blocks[3], BOTH_SWAP),
    )


def exchange_far(own, near, far):
    across = swap(far, CHIP_SWAP)
    return [own, swap(near, CORE_SWAP), across, swap(across, CORE_SWAP)]


def gather(values):
    across = swap(values, CHIP_SWAP)
    return (values, swap(values, CORE_SWAP), across, swap(across, CORE_SWAP))


def hold(*values):
    return lax.optimization_barrier(values)


def onward(keeps, gots):
    parts = [(k[1].astype(FULL) + g[1].astype(FULL)).astype(LOW) for k, g in zip(keeps, gots)]
    return parts[0] if len(parts) == 1 else jnp.concatenate(parts, axis=0)


def own(keeps, gots, other):
    parts, row = [], 0
    for k, g in zip(keeps, gots):
        value = k[0].astype(FULL) + g[0].astype(FULL) + other[row : row + k.shape[1]].astype(FULL)
        parts.append(value.astype(LOW))
        row += k.shape[1]
    return parts[0] if len(parts) == 1 else jnp.concatenate(parts, axis=0)


def split(values, count):
    return values.reshape(count, -1, values.shape[-1])


def trade(parts):
    return lax.all_to_all(parts, "mp", split_axis=0, concat_axis=0, tiled=True)


def spread_sum(parts):
    value = jnp.sum(parts.astype(FULL), axis=0).astype(LOW)
    return jnp.broadcast_to(value[None], parts.shape)


def flat(parts):
    return parts.reshape(-1, parts.shape[2])


def per_device(
    mp_count,
    block_input,
    norm1_gain,
    norm1_bias,
    input_weight,
    input_bias,
    conv_weight,
    conv_bias,
    gate_weight1,
    gate_bias1,
    gate_weight2,
    gate_bias2,
    gate_weight3,
    gate_bias3,
    output_weight,
    output_bias,
    layer_scale1,
    norm2_gain,
    norm2_bias,
    expand_weight,
    expand_bias,
    reduce_weight,
    reduce_bias,
    layer_scale2,
    cotangent,
):
    me = lax.axis_index("dp").astype(jnp.int32).reshape(1)

    def turned(weight):
        return jnp.transpose(weight, (1, 2, 0)).reshape(-1, weight.shape[0])

    small, *x_blocks = first_kernel(
        me,
        block_input.reshape(SHARD, -1),
        (
            turned(output_weight),
            turned(gate_weight3),
            turned(gate_weight2),
            turned(gate_weight1),
            turned(conv_weight),
            norm1_gain,
            norm1_bias,
            input_bias,
            conv_bias,
            gate_bias1,
            gate_bias2,
            gate_bias3,
            output_bias,
            layer_scale1,
            norm2_gain,
            norm2_bias,
            reduce_bias,
            layer_scale2,
            expand_bias.T,
        ),
    )
    in_weight = turned(input_weight)
    in_across = swap(in_weight, CHIP_SWAP)
    small, x_blocks, in_across = hold(small, x_blocks, in_across)
    small_across = swap(small, CHIP_SWAP)
    x_blocks = exchange(x_blocks)
    slabs = (small, swap(small, CORE_SWAP), small_across, swap(small_across, CORE_SWAP))
    in_shards = (in_weight, swap(in_weight, CORE_SWAP), in_across, swap(in_across, CORE_SWAP))
    own_dy, near, far = second_kernel(
        me, cotangent.reshape(SHARD, -1), turned(expand_weight), reduce_weight.reshape(-1, WIDTH)
    )
    vec, expand, w1, w1_back, w2, w3, w_in, w_out, taps, perm = prepare(me, slabs, in_shards)
    x_blocks, near, far, vec = hold(x_blocks, near, far, vec)
    core, across = swap(near, CORE_SWAP), swap(far, CHIP_SWAP)
    x, z1, u, dwv = front(x_blocks, perm, vec, w_in, taps)
    dwv, core = hold(dwv, core)
    z2 = branch_forward(dwv, x, vec, w1, w2, w3, w_out)
    z2, across = hold(z2, across)
    joints = (near, core, across, swap(across, CORE_SWAP))
    dy, f, dz, bias_grads, sib_g, keep_g = feed_forward(z2, own_dy, joints, perm, vec, expand)


    got_g = swap(sib_g, CORE_SWAP)
    on_g = onward([keep_g], [got_g])
    dz, on_g = hold(dz, on_g)
    other_g = swap(on_g, CHIP_SWAP)
    *outs, g, dx1, sib, keep_late = branch_backward(
        me, dwv, x, dy, f, dz, vec, w1, w1_back, w2, w3, w_out, perm, bias_grads
    )
    got_late = swap(sib, CORE_SWAP)
    g, other_g, outs, got_late = hold(g, other_g, outs, got_late)
    part_g = split(own([keep_g], [got_g], other_g), mp_count)
    on_late = onward([keep_late], [got_late])
    g, part_g, on_late = hold(g, part_g, on_late)
    part_g = trade(part_g)
    other_late = swap(on_late, CHIP_SWAP)
    outs = exchange_far(*outs)

    du1, sib, keep1 = conv_backward(me, g, u, taps, z1, 4)
    got1 = swap(sib, CORE_SWAP)
    du1, part_g, other_late = hold(du1, part_g, other_late)
    part_late = split(own([keep_late], [got_late], other_late), mp_count)
    mixed = jnp.concatenate([spread_sum(part_g), part_late], axis=1)
    g, mixed = hold(g, mixed)
    mixed = trade(mixed)

    du0, sib, keep0 = conv_backward(me, g, u, taps, z1, 0)
    got0 = swap(sib, CORE_SWAP)
    du0, got0, got1, outs = hold(du0, got0, got1, outs)
    on_c = onward([keep0, keep1], [got0, got1])
    du0, on_c = hold(du0, on_c)
    other_c = swap(on_c, CHIP_SWAP)

    *ins, e0, e1, e2, e3 = input_backward(me, (du0, du1), x, dx1, vec, w_in, perm)
    ins, other_c = hold(ins, other_c)
    ins = exchange_far(*ins)
    block_output = from_pixels(me, outs).reshape(block_input.shape)
    ends = exchange((e0, e1, e2, e3))
    ins[1], other_c, mixed = hold(ins[1], other_c, mixed)
    rows = part_g.shape[1]
    full_g, part_late = mixed[:, :rows], mixed[:, rows:]
    part_c = split(own([keep0, keep1], [got0, got1], other_c), mp_count)
    mixed = trade(jnp.concatenate([spread_sum(part_late), part_c], axis=1))
    sum_e, sum_r = widen(full_g)
    mixed, ins = hold(mixed, ins)
    rows = part_late.shape[1]
    full_late, part_c = mixed[:, :rows], mixed[:, rows:]
    end = sum(e.astype(FULL) for e in ends).astype(LOW)
    end = jnp.broadcast_to(end[None], (mp_count,) + end.shape)
    full_c = trade(jnp.concatenate([spread_sum(part_c), end], axis=1))

    def back(values, blocks):
        return jnp.transpose(values.reshape(blocks, 16, values.shape[1]), (2, 0, 1))

    (
        g1, g2, g3, gconv, gout, gin, gb1, gb2, gb3, gob, gls1, gn2g, gn2b, grb, gls2, geb, ginb, gcb, gn1g, gn1b,
    ) = unpack_small(flat(full_late), full_c)
    input_grad = from_pixels(me, ins).reshape(block_input.shape)
    return (
        block_output,
        input_grad,
        gn1g,
        gn1b,
        back(gin, 16),
        ginb,
        back(gconv, 15),
        gcb,
        back(g1, 2),
        gb1,
        back(g2, 4),
        gb2,
        back(g3, 8),
        gb3,
        back(gout, 8),
        gob,
        gls1,
        gn2g,
        gn2b,
        back(sum_e, 32),
        geb.T,
        sum_r.reshape(32, 16, WIDTH),
        grb,
        gls2,
    )


def solution(mesh):
    pixels = P(None, "dp", "mp")
    vector = P(None, "dp")
    matrix = P(None, None, "dp")
    params = (
        vector, vector, matrix, vector, matrix, vector, matrix, vector, matrix, vector, matrix, vector,
        matrix, vector, vector, vector, vector, matrix, vector, P(None, "dp", None), vector, vector,
    )
    return jax.shard_map(
        partial(per_device, mesh.shape["mp"]),
        mesh=mesh,
        in_specs=(pixels,) + params + (pixels,),
        out_specs=(pixels, pixels) + params,
        check_vma=False,
    )
```

```python
from functools import partial

import jax
import jax.numpy as jnp
from jax import lax
from jax.experimental import pallas as pl
from jax.experimental.pallas import tpu as pltpu
from jax.sharding import PartitionSpec as P

WIDTH = 512
GROUP = 64
SIDE = 14
CROP = SIDE * SIDE
CROPS = 8
TOKENS = CROP * CROPS
SHARD = 128
TAPS = 49
EPSILON = 1e-06
LOW = jnp.bfloat16
FULL = jnp.float32
VMEM = 58 * 1024 * 1024

NN = (((1,), (0,)), ((), ()))
NT = (((1,), (1,)), ((), ()))
TN = (((0,), (0,)), ((), ()))

CORE_SWAP = [(0, 1), (1, 0), (2, 3), (3, 2)]
CHIP_SWAP = [(0, 2), (2, 0), (1, 3), (3, 1)]
BOTH_SWAP = [(0, 3), (3, 0), (1, 2), (2, 1)]

S_GATE3, S_GATE2, S_GATE1, S_CONV, S_EXPAND, S_OUT, S_ROWS = 0, 256, 320, 352, 560, 592, 1104
S_LANE = 64
(V_N1G, V_N1B, V_INB, V_CB, V_GB1, V_GB2, V_GB3, V_OB, V_LS1, V_N2G, V_N2B, V_RB, V_LS2) = range(13)
VECTORS = 13
E_OUT, E_VEC, E_EXPAND, E_ROWS = 0, 352 + 512, 496 + 512, 640 + 512
E_GATE = 512


def mm(left, right, dims=NN):
    return lax.dot_general(left, right, dims, preferred_element_type=FULL)


def call(body, out, weight=1.0, **kwargs):
    flops, moved = int(weight * 1.15e9 / 4), 1 << 10
    return pl.pallas_call(
        body,
        out_shape=out,
        compiler_params=pltpu.CompilerParams(vmem_limit_bytes=VMEM),
        cost_estimate=pl.CostEstimate(flops=flops, bytes_accessed=moved, transcendentals=0),
        **kwargs,
    )


def struct(shape, dtype):
    return jax.ShapeDtypeStruct(shape, dtype)


SMEM_SPEC = pl.BlockSpec(memory_space=pltpu.SMEM)


def whole(shape):
    return pl.BlockSpec(shape, lambda i: (0,) * len(shape))


def turn_blocks(me, x_ref, outs, wide, blocks):
    lanes = x_ref.shape[1]
    for dest in range(4):
        for crop in range(CROPS):
            start = CROP * (CROPS * dest + crop)
            base = start // 128 * 128
            window = x_ref[:, base : base + min(lanes - base, 384)].astype(FULL)
            wide[pl.ds(crop, CROP, stride=CROPS), :] = window[:, start - base : start - base + CROP].T
        blocks[dest ^ me] = wide[...].astype(LOW)
    for k in range(4):
        outs[k][...] = blocks[k]


PIXEL_SCRATCH = [pltpu.VMEM((TOKENS, SHARD), FULL), pltpu.VMEM((4, TOKENS, SHARD), LOW)]


JOINT = TOKENS + 4 * 1024


def second_body(me_ref, x_ref, expand, reduce, own, near, far, wide, blocks):
    turn_blocks(me_ref[0], x_ref, (own, near.at[0:TOKENS], far.at[0], far.at[1]), wide, blocks)
    for part in range(4):
        lanes = slice(part * 128, part * 128 + 128)
        first = TOKENS + part * 1024
        near[first : first + 512, :] = expand[:, lanes]
        near[first + 512 : first + 1024, :] = reduce[:, lanes]


def second_kernel(me, x, expand, reduce):
    return call(
        second_body,
        (struct((TOKENS, SHARD), LOW), struct((JOINT, SHARD), LOW), struct(FAR, LOW)),
        weight=0.05,
        in_specs=[SMEM_SPEC] + [pl.BlockSpec(memory_space=pltpu.VMEM)] * 3,
        scratch_shapes=PIXEL_SCRATCH,
    )(me, x, expand, reduce)


def first_body(part, me_ref, part_ref, x_ref, expand, reduce, *refs):
    small, far = refs[19], refs[20]
    pack_body(*refs[:19], small, refs[25])
    far[0:S_ROWS, :] = small[...]
    size = 4096 // part
    for number in range(part):
        lanes, rest = number * size // 1024, number * size % 1024
        source = (expand, reduce)[rest // 512]

        @pl.when(part_ref[0] == number)
        def _():
            far[S_ROWS:, :] = source[rest % 512 : rest % 512 + size, lanes * 128 : lanes * 128 + 128]

    turn_blocks(me_ref[0], x_ref, refs[21:25], refs[26], refs[27])


def first_kernel(me, where, parts, x, expand, reduce, small):
    slab = (S_ROWS, 128)
    return call(
        partial(first_body, parts),
        (struct(slab, LOW), struct((S_ROWS + 4096 // parts, 128), LOW)) + (struct((TOKENS, SHARD), LOW),) * 4,
        weight=0.05,
        in_specs=[SMEM_SPEC] * 2 + [pl.BlockSpec(memory_space=pltpu.VMEM)] * 22,
        scratch_shapes=[pltpu.VMEM((S_OUT, 128), FULL)] + PIXEL_SCRATCH,
    )(me, where, x, expand, reduce, *small)


def from_pixels_body(me_ref, own, core, across, passed, out_ref, wide, blocks):
    me = me_ref[0]
    blocks[me] = own[...]
    blocks[1 ^ me] = core[...]
    blocks[2 ^ me] = across[0]
    blocks[3 ^ me] = passed[1]
    for source in range(4):
        wide[...] = blocks[source].astype(FULL)
        for crop in range(CROPS):
            start = CROP * (CROPS * source + crop)
            part = wide[pl.ds(crop, CROP, stride=CROPS), :].T
            out_ref[:, start : start + CROP] = part.astype(LOW)


def from_pixels(me, blocks):
    return call(
        from_pixels_body,
        struct((SHARD, 4 * TOKENS), LOW),
        weight=4.0,
        in_specs=[SMEM_SPEC] + [pl.BlockSpec(memory_space=pltpu.VMEM)] * 4,
        scratch_shapes=[pltpu.VMEM((TOKENS, SHARD), FULL), pltpu.VMEM((4, TOKENS, SHARD), LOW)],
    )(me, *blocks)


FAR = (2, TOKENS, SHARD)


def far_spec(tile):
    return pl.BlockSpec((2, tile, SHARD), lambda i: (0, i, 0))


def pack_body(out_weight, g3, g2, g1, conv, *refs):
    vectors, expand, out_ref, slab = refs[:VECTORS], refs[VECTORS], refs[VECTORS + 1], refs[VECTORS + 2]
    slab[...] = jnp.zeros_like(slab)
    slab[S_GATE3 : S_GATE3 + 128, :] = g3[:, :128].astype(FULL)
    slab[S_GATE3 + 128 : S_GATE3 + 256, :] = g3[:, 128:].astype(FULL)
    slab[S_GATE2 : S_GATE2 + 64, :] = g2[...].astype(FULL)
    slab[S_GATE1 : S_GATE1 + 32, :GROUP] = g1[...].astype(FULL)
    slab[S_CONV : S_CONV + 240, :TAPS] = conv[...].astype(FULL)
    for number, ref in enumerate(vectors):
        first = S_CONV + 16 * number + (1 if number == V_CB else 0)
        slab[first : first + ref.shape[0], S_LANE : S_LANE + 16] = ref[...].astype(FULL)
    slab[S_EXPAND : S_EXPAND + 32, S_LANE : S_LANE + 16] = expand[...].astype(FULL).T
    out_ref[0:S_OUT, :] = slab[...].astype(LOW)
    for part in range(4):
        rows = slice(S_OUT + part * 128, S_OUT + part * 128 + 128)
        out_ref[rows, :] = out_weight[:, part * 128 : part * 128 + 128]


TILE_OF = (2, 0, 3, 1)


def iota(shape, dim):
    return lax.broadcasted_iota(jnp.int32, shape, dim)


def spread(lanes):
    return jnp.where(iota((128, lanes), 1) % 16 + S_LANE == iota((128, lanes), 0), 1.0, 0.0).astype(LOW)


def prepare_body(me_ref, *refs):
    slabs, ins = refs[0:4], refs[4:8]
    vec, expand, w1, w1_back, w2, w3, w_in, w_out, taps, perm, channels = refs[8:]
    me = me_ref[0]
    totals = jnp.zeros((VECTORS, 1024), FULL)
    spread_wide = spread(1024)
    row = iota((VECTORS * 16, 1024), 0) % 16
    lane = iota((VECTORS * 16, 1024), 1)
    in_row = row == lane // 64
    spread_expand = spread(512)
    expand_rows = iota((32, 512), 0) == iota((32, 512), 1) // 16
    w1[...] = jnp.zeros_like(w1)
    channels[0:GROUP, :] = jnp.where(iota((GROUP, 128), 1) == TAPS // 2, 3.0, 0.0)
    for k in range(4):
        source = me ^ k
        slab = slabs[k]
        values = mm(slab[S_CONV : S_CONV + VECTORS * 16, :], spread_wide)
        values = jnp.where(in_row & (lane // 16 % 4 == source), values, 0.0)
        totals = totals + jnp.sum(values.reshape(VECTORS, 16, 1024), axis=1)
        values = mm(slab[S_EXPAND : S_EXPAND + 32, :], spread_expand)
        values = jnp.sum(jnp.where(expand_rows, values, 0.0), axis=0, keepdims=True)
        slot = TILE_OF[k]
        expand[8 * slot : 8 * slot + 8, :] = jnp.broadcast_to(values, (8, 512))
        for a in range(16):
            place = pl.ds(pl.multiple_of(a * 64 + source * 16, 16), 16)
            rows = slice(a * 16, a * 16 + 16)
            w_in[place, :] = ins[k][rows, :]
            if a < 15:
                later = pl.ds(pl.multiple_of((a + 1) * 64 + source * 16, 16), 16)
                channels[later, :] = slab[S_CONV + a * 16 : S_CONV + a * 16 + 16, :].astype(FULL)
            if a < 8:
                for part in range(4):
                    first = S_OUT + part * 128 + a * 16
                    w_out[place, part * 128 : part * 128 + 128] = slab[first : first + 16, :]
                w3[place, 0:128] = slab[S_GATE3 + a * 16 : S_GATE3 + a * 16 + 16, :]
                w3[place, 128:256] = slab[S_GATE3 + 128 + a * 16 : S_GATE3 + 128 + a * 16 + 16, :]
            if a < 4:
                w2[place, :] = slab[S_GATE2 + a * 16 : S_GATE2 + a * 16 + 16, :]
            if a < 2:
                w1[place, :] = slab[S_GATE1 + a * 16 : S_GATE1 + a * 16 + 16, :]
        column = iota((SHARD, WIDTH), 0)
        target = column // 16 * 64 + source * 16 + column % 16
        perm[k * SHARD : (k + 1) * SHARD, :] = jnp.where(iota((SHARD, WIDTH), 1) == target, 1.0, 0.0).astype(LOW)
    vec[0:VECTORS, :] = totals
    vec[VECTORS:16, :] = jnp.zeros((16 - VECTORS, 1024), FULL)
    single = w1[...].astype(FULL)
    w1_back[...] = (single + pltpu.roll(single, GROUP, 1)).astype(LOW)
    taps[...] = channels[...].T[0:64, :]


def prepare(me, slabs, ins):
    return call(
        prepare_body,
        (
            struct((16, 1024), FULL),
            struct((32, 512), FULL),
            struct((128, 128), LOW),
            struct((128, 128), LOW),
            struct((256, 128), LOW),
            struct((512, 256), LOW),
            struct((1024, 512), LOW),
            struct((512, 512), LOW),
            struct((64, 1024), FULL),
            struct((512, 512), LOW),
        ),
        weight=0.05,
        in_specs=[SMEM_SPEC] + [pl.BlockSpec(memory_space=pltpu.VMEM)] * 8,
        scratch_shapes=[pltpu.VMEM((1024, 128), FULL)],
    )(me, *slabs, *ins)


def normed(values):
    center = jnp.sum(values, axis=1, keepdims=True) * (1.0 / WIDTH)
    away = values - center
    spread_sq = jnp.sum(away * away, axis=1, keepdims=True) * (1.0 / WIDTH)
    inverse = lax.rsqrt(spread_sq + EPSILON)
    return away * inverse, inverse


def norm_back(grad, unit, inverse, gain):
    grad_unit = grad * gain
    first = jnp.sum(grad_unit, axis=1, keepdims=True) * (1.0 / WIDTH)
    second = jnp.sum(grad_unit * unit, axis=1, keepdims=True) * (1.0 / WIDTH)
    return inverse * (grad_unit - first - unit * second)


def total(values):
    return jnp.sum(values, axis=0, keepdims=True)


def row(vec, number, lanes=WIDTH):
    return vec[number : number + 1, 0:lanes]


def rows_spec(tile, lanes):
    return pl.BlockSpec((tile, lanes), lambda i: (i, 0))


def chunks(count, size, body):
    def step(i, carry):
        body(pl.ds(pl.multiple_of(i * size, size), size))
        return carry

    lax.fori_loop(0, count // size, step, 0)


NORM_ROWS = 224
HALVES = (slice(0, TOKENS // 2), slice(TOKENS // 2, TOKENS))


def stagger(chain, height, lead):
    cut = height // 32 * 16
    ahead, behind = chain(slice(0, cut)), chain(slice(cut, height))
    for _ in range(lead):
        next(ahead)
    for _ in ahead:
        next(behind)
    for _ in behind:
        pass


def join(blocks, perm, rows):
    return mm(jnp.concatenate([r[rows, :] for r in blocks], axis=1), perm[...])


def conv_rows(source, weights, emit, flip):
    zero = jnp.zeros((CROPS, 128), FULL)

    def tap_row(i, r, sums):
        base = (i + r - 3) * SIDE
        values = [source[base + c] for c in range(SIDE)]
        first = (6 - r) * 7 if flip else r * 7
        taps = [weights[first + (6 - s if flip else s)] for s in range(7)]
        for s in range(7):
            for c in range(SIDE):
                if 0 <= c + s - 3 < SIDE:
                    sums[c] = sums[c] + taps[s] * values[c + s - 3]

    def one_row(i, first, last):
        sums = [zero] * SIDE
        for r in range(first, last):
            tap_row(i, r, sums)
        emit(i, sums)

    def inner_row(i, carry):
        one_row(i, 0, 7)
        return carry

    for i in range(3):
        one_row(i, 3 - i, 7)
    lax.fori_loop(3, SIDE - 3, inner_row, 0)
    for i in range(SIDE - 3, SIDE):
        one_row(i, 0, 17 - i)


def wide_taps(taps, weights):
    for tap in range(TAPS):
        weights[tap] = jnp.broadcast_to(taps[tap : tap + 1, :], (CROPS, 128))


PIXEL_BLOCK = pl.BlockSpec((CROP, CROPS, 128), lambda i: (0, 0, i))


def lane_block(rows):
    return pl.BlockSpec((rows, 128), lambda i: (0, i))


def front_body(r0, r1, r2, r3, perm, vec, w_in, taps, vec_part, x, z, u, dwv, weights):
    @pl.when(pl.program_id(0) == 0)
    def _():
        for rows in HALVES:
            x[rows, :] = join((r0, r1, r2, r3), perm, rows).astype(LOW)

        def norm_rows(rows):
            unit, _ = normed(x[rows, :].astype(FULL))
            z[rows, :] = (unit * row(vec, V_N1G) + row(vec, V_N1B)).astype(LOW)

        chunks(TOKENS, NORM_ROWS, norm_rows)

    wide_taps(taps, weights)
    values = mm(z[...], w_in[...], NT) + vec_part[V_INB : V_INB + 1, :]
    u[...] = values.reshape(CROP, CROPS, 128)
    bias = jnp.broadcast_to(vec_part[V_CB : V_CB + 1, :], (CROPS, 128))

    def emit(i, sums):
        for c in range(SIDE):
            dwv[i * SIDE + c] = (sums[c] + bias) * (1.0 / 3.0)

    conv_rows(u, weights, emit, False)


def front(blocks, perm, vec, w_in, taps):
    pixels = struct((CROP, CROPS, 1024), FULL)
    rows = struct((TOKENS, WIDTH), LOW)
    x, z, u, dwv = call(
        front_body,
        (rows, rows, pixels, pixels),
        weight=28.0,
        grid=(8,),
        in_specs=[whole((TOKENS, SHARD))] * 4
        + [
            whole((512, 512)),
            whole((16, 1024)),
            pl.BlockSpec((128, 512), lambda i: (i, 0)),
            lane_block(64),
            lane_block(16),
        ],
        out_specs=(whole((TOKENS, WIDTH)), whole((TOKENS, WIDTH)), PIXEL_BLOCK, PIXEL_BLOCK),
        scratch_shapes=[pltpu.VMEM((TAPS, CROPS, 128), FULL)],
    )(*blocks, perm, vec, w_in, taps, vec)
    return x, z, u, dwv.reshape(TOKENS, 1024)


def branch_body(dwv, x, vec, w1, w2, w3, w_out, z_out):
    def chain(rows):
        first = dwv[rows, 0:128]
        q = (first * pltpu.roll(first, GROUP, 1)).astype(LOW)
        yield
        t = mm(q, w1[...], NT) + row(vec, V_GB1, 128)
        q = (t * dwv[rows, 128:256]).astype(LOW)
        yield
        t = mm(q, w2[...], NT) + row(vec, V_GB2, 256)
        q = (t * dwv[rows, 256:512]).astype(LOW)
        yield
        t = mm(q, w3[...], NT) + row(vec, V_GB3, 512)
        q = (t * dwv[rows, 512:1024]).astype(LOW)
        yield
        branch = mm(q, w_out[...], NT) + row(vec, V_OB)
        middle = x[rows, :].astype(FULL) + row(vec, V_LS1) * branch
        yield
        unit, _ = normed(middle)
        z_out[rows, :] = (unit * row(vec, V_N2G) + row(vec, V_N2B)).astype(LOW)
        yield

    stagger(chain, dwv.shape[0], 2)


def branch_forward(dwv, x, vec, w1, w2, w3, w_out, tile=784):
    return call(
        branch_body,
        struct((TOKENS, WIDTH), LOW),
        weight=7.0,
        grid=(TOKENS // tile,),
        in_specs=[
            rows_spec(tile, 1024),
            rows_spec(tile, WIDTH),
            whole((16, 1024)),
            whole((128, 128)),
            whole((256, 128)),
            whole((512, 256)),
            whole((512, 512)),
        ],
        out_specs=rows_spec(tile, WIDTH),
    )(dwv, x, vec, w1, w2, w3, w_out)


def gelu_parts(s):
    bell = jnp.exp2((-0.5 * 1.4426950408889634) * (s * s))
    size = jnp.abs(s)
    t = pltpu.reciprocal(1.0 + (0.3275911 * 0.7071067811865476) * size, approx=True)
    poly = 0.5 * 1.061405429
    for coefficient in (-1.453152027, 1.421413741, -0.284496736, 0.254829592):
        poly = poly * t + 0.5 * coefficient
    tail = poly * t * bell
    cdf = jnp.where(s >= 0.0, 1.0 - tail, tail)
    return s * cdf, cdf + s * (bell * 0.3989422804014327)


PIECE = 16


def mlp_body(z, r0, perm, vec, expand, c0, c1, w2, w3, y2, y3, *refs):
    dy_out, f_out, dz_out, gb, sibling, keep = refs[0:6]
    dy, f, dz, r1, r2, r3, we, wr, df, s0, s1, g0, g1, hid, grad_s, grads, sums, sems = refs[6:]
    pre, grad_h = (s0, s1), (g0, g1)
    half = TOKENS // 2
    shards = ((c1, TOKENS), (w3, 0), (c0, TOKENS), (w2, 0))

    def copies(slot):
        for part in range(4):
            for number, matrix in enumerate((we, wr)):
                shard, first = shards[slot]
                rows = pl.ds(first + part * 1024 + number * 512, 512)
                yield pltpu.make_async_copy(
                    shard.at[rows], matrix.at[slot, :, pl.ds(part * 128, 128)], sems.at[slot]
                )

    near = [
        pltpu.make_async_copy(block, r, sems.at[4 + number])
        for number, (block, r) in enumerate(((c1.at[pl.ds(0, TOKENS)], r1), (y2.at[0], r2), (y3.at[1], r3)))
    ]
    for copy in near:
        copy.start()
    for slot in range(4):
        for copy in copies(slot):
            copy.start()

    def arrived(slot):
        for matrix in (we, wr):
            pltpu.make_async_copy(matrix.at[slot], matrix.at[slot], sems.at[slot]).wait()

    def leave(tile):
        out = (sibling, keep)[tile // 2]
        return [
            pltpu.make_async_copy(
                grads.at[tile, :, pl.ds(part * 128, 128)],
                out.at[tile % 2, pl.ds(part * 1024, 1024)],
                sems.at[7 + tile],
            )
            for part in range(4)
        ]

    def start(copies):
        for copy in copies:
            copy.start()

    for copy in near:
        copy.wait()
    for rows in HALVES:
        dy[rows, :] = join((r0, r1, r2, r3), perm, rows).astype(LOW)
    dy_leaves = pltpu.make_async_copy(dy, dy_out, sems.at[11])
    dy_leaves.start()

    def scaled(rows):
        df[rows, :] = (dy[rows, :].astype(FULL) * row(vec, V_LS2)).astype(LOW)
        f[rows, :] = jnp.zeros((112, WIDTH), FULL)
        dz[rows, :] = jnp.zeros((112, WIDTH), FULL)

    chunks(TOKENS, 112, scaled)
    sums[...] = jnp.zeros_like(sums)
    hid[1, HALVES[1], :] = jnp.zeros((half, 512), LOW)
    grad_s[1, HALVES[1], :] = jnp.zeros((half, 512), LOW)
    arrived(0)
    s0[...] = mm(z[HALVES[0], :], we[0], NT)
    g0[...] = mm(df[HALVES[0], :], wr[0], NT)
    pieces = half // PIECE

    def unit(here, tile, before, after):
        there = 1 - here
        rows = HALVES[there]
        now, last = tile & 1, (tile & 1) ^ 1
        ready = last if here == 0 else now
        bias = expand[pl.ds(pl.multiple_of(tile * 8, 8), 1), :]
        done = [0]
        column = [jnp.zeros((8, 512), FULL)]

        def some(part):
            while done[0] < pieces * part // 6:
                first = done[0] * PIECE
                piece = slice(first, first + PIECE)
                place = slice(here * half + first, here * half + first + PIECE)
                act, slope = gelu_parts(pre[here][piece, :] + bias)
                hid[now, place, :] = act.astype(LOW)
                grad = (grad_h[here][piece, :] * slope).astype(LOW)
                grad_s[now, place, :] = grad
                grad = grad.astype(FULL)
                column[0] = column[0] + (grad[0:8] + grad[8:16])
                done[0] += 1

        if here == 0:
            grads[before, 0:512, :] = mm(grad_s[last], z[...], TN).astype(LOW)
        else:
            grads[before, 512:1024, :] = mm(hid[last], df[...], TN).astype(LOW)
        some(2)
        pre[there][...] = mm(z[rows, :], we[after], NT)
        some(3)
        grad_h[there][...] = mm(df[rows, :], wr[after], NT)
        some(4)
        f[rows, :] += mm(hid[ready, rows, :], wr[before if here == 0 else tile])
        some(5)
        dz[rows, :] += mm(grad_s[ready, rows, :], we[before if here == 0 else tile])
        some(6)
        sums[tile] += column[0]

    def one_tile(tile, carry):
        before = jnp.maximum(tile - 1, 0)
        for number in range(2):

            @pl.when(tile == number + 2)
            def _():
                start(leave(number))

        unit(0, tile, before, tile)

        @pl.when(tile < 3)
        def _():
            arrived(tile + 1)

        unit(1, tile, before, jnp.minimum(tile + 1, 3))
        return carry

    lax.fori_loop(0, 4, one_tile, 0)
    start(leave(2))

    def results(number):
        rows = pl.ds(number * half, half)
        return [
            pltpu.make_async_copy(value.at[rows], out.at[rows], sems.at[12 + number])
            for value, out in ((f, f_out), (dz, dz_out))
        ]

    start(results(0))
    rows = HALVES[1]
    f[rows, :] += mm(hid[1, rows, :], wr[3])
    dz[rows, :] += mm(grad_s[1, rows, :], we[3])
    start(results(1))
    grads[3, 0:512, :] = mm(grad_s[1], z[...], TN).astype(LOW)
    grads[3, 512:1024, :] = mm(hid[1], df[...], TN).astype(LOW)
    start(leave(3))
    for tile in range(4):
        gb[8 * tile : 8 * tile + 8, :] = sums[tile]
    dy_leaves.wait()
    for copies in [results(0), results(1)] + [leave(tile) for tile in range(4)]:
        for copy in copies:
            copy.wait()


def feed_forward(z, own_dy, others, perm, vec, expand):
    vmem = pl.BlockSpec(memory_space=pltpu.VMEM)
    anywhere = pl.BlockSpec(memory_space=pl.ANY)
    half = TOKENS // 2
    pair = struct((2, 4096, 128), LOW)
    rows = struct((TOKENS, WIDTH), FULL)
    return call(
        mlp_body,
        (struct((TOKENS, WIDTH), LOW), rows, rows, struct((32, 512), FULL), pair, pair),
        weight=40.0,
        in_specs=[vmem] * 5 + [anywhere] * 6,
        out_specs=(anywhere,) * 3 + (vmem,) + (anywhere,) * 2,
        scratch_shapes=[pltpu.VMEM((TOKENS, WIDTH), LOW)]
        + [pltpu.VMEM((TOKENS, WIDTH), FULL)] * 2
        + [pltpu.VMEM((TOKENS, SHARD), LOW)] * 3
        + [pltpu.VMEM((4, 512, 512), LOW)] * 2
        + [pltpu.VMEM((TOKENS, WIDTH), LOW)]
        + [pltpu.VMEM((half, 512), FULL)] * 4
        + [pltpu.VMEM((2, TOKENS, 512), LOW)] * 2
        + [pltpu.VMEM((4, 1024, 512), LOW)]
        + [pltpu.VMEM((4, 8, 512), FULL)]
        + [pltpu.SemaphoreType.DMA((14,))],
    )(z, own_dy, perm, vec, expand, *others)


def pack_vectors(values, count, source):
    lane = iota((count * 16, 1024), 1)
    keep = (iota((count * 16, 1024), 0) % 16 == lane // 64) & (lane // 16 % 4 == source)
    tall = jnp.broadcast_to(values[:, None, :], (count, 16, 1024)).reshape(count * 16, 1024)
    gather = jnp.where(iota((1024, 128), 0) % 16 == iota((1024, 128), 1), 1.0, 0.0).astype(LOW)
    return mm(jnp.where(keep, tall, 0.0).astype(LOW), gather)


def part_pair(parts, sibling, keep):
    sibling[0] = parts[1]
    sibling[1] = parts[3]
    keep[0] = parts[0]
    keep[1] = parts[2]


def branch_back_body(steps, me_ref, dwv, x, dy, f, dz, vec, w1, w1_back, w2, w3, w_out, perm, gb, *refs):
    (o0, o1, far, g_out, dx_out, sibling, keep) = refs[0:7]
    acc_o, acc_3, acc_2, acc_1, sums, parts = refs[7:]
    step = pl.program_id(0)

    @pl.when(step == 0)
    def _():
        acc_o[...] = jnp.zeros_like(acc_o)
        acc_3[...] = jnp.zeros_like(acc_3)
        acc_2[...] = jnp.zeros_like(acc_2)
        acc_1[...] = jnp.zeros_like(acc_1)
        sums[...] = jnp.zeros_like(sums)

    third = 1.0 / 3.0

    def chain(rows):
        first = dwv[rows, 0:128]
        turned = pltpu.roll(first, GROUP, 1)
        q0 = (first * turned).astype(LOW)
        yield
        t1 = mm(q0, w1[...], NT) + row(vec, V_GB1, 128)
        q1 = (t1 * dwv[rows, 128:256]).astype(LOW)
        yield
        t2 = mm(q1, w2[...], NT) + row(vec, V_GB2, 256)
        q2 = (t2 * dwv[rows, 256:512]).astype(LOW)
        yield
        t3 = mm(q2, w3[...], NT) + row(vec, V_GB3, 512)
        q3 = (t3 * dwv[rows, 512:1024]).astype(LOW)
        yield
        branch = mm(q3, w_out[...], NT) + row(vec, V_OB)
        middle = x[rows, :].astype(FULL) + row(vec, V_LS1) * branch
        yield
        unit, inverse = normed(middle)
        yield
        grad = dz[rows, :]
        top = dy[rows, :].astype(FULL)
        middle_grad = top + norm_back(grad, unit, inverse, row(vec, V_N2G))
        dx_out[rows, :] = middle_grad
        sums[4:5, 0:512] += total(middle_grad * branch)
        sums[5:6, 0:512] += total(grad * unit)
        sums[6:7, 0:512] += total(grad)
        grad_branch = (middle_grad * row(vec, V_LS1)).astype(LOW)
        yield
        back = mm(grad_branch, w_out[...])
        gt3 = (back * dwv[rows, 512:1024]).astype(LOW)
        g_out[rows, 512:1024] = back * t3 * third
        yield
        back = mm(gt3, w3[...])
        acc_o[...] += mm(grad_branch, q3, TN)
        sums[3:4, 0:512] += total(grad_branch.astype(FULL))
        gt2 = (back * dwv[rows, 256:512]).astype(LOW)
        g_out[rows, 256:512] = back * t2 * third
        yield
        back = mm(gt2, w2[...])
        acc_3[...] += mm(gt3, q2, TN)
        sums[2:3, 0:512] += total(gt3.astype(FULL))
        gt1 = (back * dwv[rows, 128:256]).astype(LOW)
        g_out[rows, 128:256] = back * t1 * third
        yield
        back = mm(gt1, w1_back[...])
        acc_2[...] += mm(gt2, q1, TN)
        acc_1[...] += mm(gt1, q0, TN)
        sums[1:2, 0:256] += total(gt2.astype(FULL))
        sums[0:1, 0:128] += total(gt1.astype(FULL))
        g_out[rows, 0:128] = back * turned * third
        yield
        mlp = f[rows, :] + row(vec, V_RB)
        output = (middle + row(vec, V_LS2) * mlp).astype(LOW)
        sums[7:8, 0:512] += total(top) * row(vec, V_LS2)
        sums[8:9, 0:512] += total(top * mlp)
        yield
        blocks = mm(output, perm[...], NT).astype(LOW)
        for k, ref in enumerate((o0, o1, far.at[0], far.at[1])):
            ref[rows, :] = blocks[:, k * SHARD : (k + 1) * SHARD]
        yield

    height = dwv.shape[0]
    stagger(chain, height, 3)

    @pl.when(step == steps - 1)
    def _():
        me = me_ref[0]
        vectors = sums[0:9, :]
        expand_rows = iota((32, 512), 0) == iota((32, 512), 1) // 16
        gather = jnp.where(iota((512, 128), 0) % 16 == iota((512, 128), 1), 1.0, 0.0).astype(LOW)
        for source in range(4):
            k = source ^ me
            for a in range(8):
                rows = slice(a * 64 + source * 16, a * 64 + source * 16 + 16)
                for part in range(4):
                    first = part * 128 + a * 16
                    parts[k, first : first + 16, :] = acc_o[rows, part * 128 : part * 128 + 128].astype(LOW)
                first = E_GATE + a * 16
                parts[k, first : first + 16, :] = acc_3[rows, 0:128].astype(LOW)
                parts[k, first + 128 : first + 144, :] = acc_3[rows, 128:256].astype(LOW)
                if a < 4:
                    parts[k, first + 256 : first + 272, :] = acc_2[rows, :].astype(LOW)
                if a < 2:
                    parts[k, first + 320 : first + 336, :] = acc_1[rows, :].astype(LOW)
            parts[k, E_VEC : E_VEC + 144, :] = pack_vectors(vectors, 9, source).astype(LOW)
        for k in range(4):
            slot = TILE_OF[k]
            line = total(gb[8 * slot : 8 * slot + 8, :])
            tall = jnp.where(expand_rows, jnp.broadcast_to(line, (32, 512)), 0.0)
            parts[k, E_EXPAND : E_EXPAND + 32, :] = mm(tall.astype(LOW), gather).astype(LOW)
            parts[k, E_EXPAND + 32 : E_ROWS, :] = jnp.zeros((E_ROWS - E_EXPAND - 32, 128), LOW)
        part_pair(parts, sibling, keep)


def branch_backward(me, dwv, x, dy, f, dz, vec, w1, w1_back, w2, w3, w_out, perm, biases, tile=784):
    steps = TOKENS // tile
    wide = rows_spec(tile, WIDTH)
    block = rows_spec(tile, SHARD)
    pair = (2, E_ROWS, 128)
    return call(
        partial(branch_back_body, steps),
        (struct((TOKENS, SHARD), LOW),) * 2
        + (
            struct(FAR, LOW),
            struct((TOKENS, 1024), FULL),
            struct((TOKENS, WIDTH), FULL),
            struct(pair, LOW),
            struct(pair, LOW),
        ),
        weight=20.0,
        grid=(steps,),
        in_specs=[
            SMEM_SPEC,
            rows_spec(tile, 1024),
            wide,
            wide,
            wide,
            wide,
            whole((16, 1024)),
            whole((128, 128)),
            whole((128, 128)),
            whole((256, 128)),
            whole((512, 256)),
            whole((512, 512)),
            whole((512, 512)),
        ]
        + [whole((32, 512))],
        out_specs=(block,) * 2 + (far_spec(tile), rows_spec(tile, 1024), wide, whole(pair), whole(pair)),
        scratch_shapes=[
            pltpu.VMEM((512, 512), FULL),
            pltpu.VMEM((512, 256), FULL),
            pltpu.VMEM((256, 128), FULL),
            pltpu.VMEM((128, 128), FULL),
            pltpu.VMEM((16, 1024), FULL),
            pltpu.VMEM((4, E_ROWS, 128), LOW),
        ],
    )(me, dwv, x, dy, f, dz, vec, w1, w1_back, w2, w3, w_out, perm, biases)


def conv_back_body(me_ref, g, u, taps, z, du, sibling, keep, weights, grad_taps, parts):
    step, steps = pl.program_id(0), pl.num_programs(0)
    me = me_ref[0]
    wide_taps(taps, weights)
    zero = jnp.zeros((CROPS, 128), FULL)

    def emit(i, sums):
        stacked = jnp.concatenate(list(sums), axis=0).astype(LOW)
        first = i * SIDE * CROPS if isinstance(i, int) else pl.multiple_of(i * SIDE * CROPS, 16)
        du[pl.ds(first, SIDE * CROPS), :] = stacked

    conv_rows(g, weights, emit, True)

    for r in range(7):

        def one_row(i, sums):
            grads = [g[i * SIDE + c] for c in range(SIDE)]
            values = [u[(i + r - 3) * SIDE + c] for c in range(SIDE)]
            sums = list(sums)
            for c in range(SIDE):
                for s in range(7):
                    if 0 <= c + s - 3 < SIDE:
                        sums[s] = sums[s] + grads[c] * values[c + s - 3]
            return tuple(sums)

        sums = lax.fori_loop(max(0, 3 - r), min(SIDE, SIDE + 3 - r), one_row, (zero,) * 7)
        for s in range(7):
            grad_taps[r * 7 + s : r * 7 + s + 1, :] = total(sums[s])
    grad_taps[49:50, :] = total(jnp.sum(g[...], axis=0))
    grad_taps[50:51, :] = total(du[...].astype(FULL))
    grad_taps[51:128, :] = jnp.zeros((77, 128), FULL)
    grad_w = mm(du[...], z[...], TN)
    tall = grad_taps[...].T.astype(LOW)
    for a in range(2):
        for source in range(4):
            k = source ^ me
            rows = slice(a * 64 + source * 16, a * 64 + source * 16 + 16)
            for part in range(4):
                place = pl.ds(pl.multiple_of(part * 128 + step * 32 + a * 16, 16), 16)
                parts[k, place, :] = grad_w[rows, part * 128 : part * 128 + 128].astype(LOW)
            place = pl.ds(pl.multiple_of(512 + step * 32 + a * 16, 16), 16)
            parts[k, place, :] = tall[rows, :]

    @pl.when(step == steps - 1)
    def _():
        part_pair(parts, sibling, keep)


C_ROWS = 640


def conv_backward(me, g, u, taps, z, base):
    pixels = pl.BlockSpec((CROP, CROPS, 128), lambda i: (0, 0, i + base))
    pair = (2, C_ROWS, 128)
    return call(
        conv_back_body,
        (struct((TOKENS, 512), LOW), struct(pair, LOW), struct(pair, LOW)),
        weight=24.0,
        grid=(4,),
        in_specs=[
            SMEM_SPEC,
            pixels,
            pixels,
            pl.BlockSpec((64, 128), lambda i: (0, i + base)),
            whole((TOKENS, WIDTH)),
        ],
        out_specs=(lane_block(TOKENS), whole(pair), whole(pair)),
        scratch_shapes=[
            pltpu.VMEM((TAPS, CROPS, 128), FULL),
            pltpu.VMEM((128, 128), FULL),
            pltpu.VMEM((4, C_ROWS, 128), LOW),
        ],
    )(me, g.reshape(CROP, CROPS, 1024), u, taps, z)


def input_back_body(steps, me_ref, du0, du1, x, dx, vec, w_in, perm, *refs):
    (o0, o1, far, e0, e1, e2, e3, sums, parts) = refs
    step = pl.program_id(0)

    @pl.when(step == 0)
    def _():
        sums[...] = jnp.zeros_like(sums)

    def chain(rows):
        grad = mm(jnp.concatenate([du0[rows, :], du1[rows, :]], axis=1), w_in[...])
        yield
        unit, inverse = normed(x[rows, :].astype(FULL))
        sums[0:1, 0:512] += total(grad * unit)
        sums[1:2, 0:512] += total(grad)
        yield
        grad_x = (dx[rows, :] + norm_back(grad, unit, inverse, row(vec, V_N1G))).astype(LOW)
        yield
        blocks = mm(grad_x, perm[...], NT).astype(LOW)
        for k, ref in enumerate((o0, o1, far.at[0], far.at[1])):
            ref[rows, :] = blocks[:, k * SHARD : (k + 1) * SHARD]
        yield

    stagger(chain, x.shape[0], 1)

    @pl.when(step == steps - 1)
    def _():
        me = me_ref[0]
        vectors = sums[0:2, :]
        for source in range(4):
            parts[source ^ me, :, :] = pack_vectors(vectors, 2, source).astype(LOW)
        for k, ref in enumerate((e0, e1, e2, e3)):
            ref[...] = parts[k]


def input_backward(me, dus, x, dx, vec, w_in, perm, tile=784):
    steps = TOKENS // tile
    wide = rows_spec(tile, WIDTH)
    end = (32, 128)
    return call(
        partial(input_back_body, steps),
        (struct((TOKENS, SHARD), LOW),) * 2 + (struct(FAR, LOW),) + (struct(end, LOW),) * 4,
        weight=8.0,
        grid=(steps,),
        in_specs=[
            SMEM_SPEC,
            *[rows_spec(tile, 512)] * 2,
            wide,
            wide,
            whole((16, 1024)),
            whole((1024, 512)),
            whole((512, 512)),
        ],
        out_specs=(rows_spec(tile, SHARD),) * 2 + (far_spec(tile),) + (whole(end),) * 4,
        scratch_shapes=[pltpu.VMEM((16, 1024), FULL), pltpu.VMEM((4, 32, 128), LOW)],
    )(me, *dus, x, dx, vec, w_in, perm)


def unpack_body(full, final, *refs):
    (g1, g2, g3, conv, w_out, w_in), late_refs, expand = refs[0:6], refs[6:15], refs[15]
    (in_bias, conv_bias, gain, bias), low = refs[16:20], refs[20]
    size = final.shape[1] - 32
    last = jnp.zeros((32, 128), FULL)
    for piece in range(final.shape[0]):
        low[piece * size : (piece + 1) * size, :] = final[piece, 0:size, :]
        last = last + final[piece, size : size + 32, :].astype(FULL)
    gates = full[E_GATE:E_VEC, :].astype(FULL)
    g3[:, 0:128] = gates[0:128]
    g3[:, 128:256] = gates[128:256]
    g2[...] = gates[256:320]
    g1[...] = gates[320:352, 0:GROUP]
    taps = []
    for j, (source, first) in enumerate(((low, 0), (low, C_ROWS))):
        for part in range(4):
            rows = slice(first + part * 128, first + part * 128 + 128)
            w_in[j * 128 : j * 128 + 128, part * 128 : part * 128 + 128] = source[rows, :].astype(FULL)
        taps.append(source[first + 512 : first + 640, :])
    for part in range(4):
        lanes = slice(part * 128, part * 128 + 128)
        w_out[:, lanes] = full[lanes, :].astype(FULL)
    taps = jnp.concatenate(taps, axis=0).astype(FULL)
    conv[...] = taps[16:256, 0:TAPS]
    vectors = full[E_VEC : E_VEC + 144, :].astype(FULL)
    for number, ref in enumerate(late_refs):
        ref[...] = vectors[16 * number : 16 * number + ref.shape[0], 0:16]
    expand[...] = full[E_EXPAND : E_EXPAND + 32, 0:16].astype(FULL).T
    gain[...] = last[0:8, 0:16]
    bias[...] = last[16:24, 0:16]
    own = jnp.where(iota((256, 16), 0) % 16 == iota((256, 16), 1), 1.0, 0.0)
    rows = jnp.where(iota((16, 256), 0) == iota((16, 256), 1) // 16, 1.0, 0.0).astype(LOW)
    conv_bias[...] = mm(rows, (taps[:, 49:50] * own).astype(LOW))[1:16, :]
    in_bias[...] = mm(rows, (taps[:, 50:51] * own).astype(LOW))


VMEM_SPEC = pl.BlockSpec(memory_space=pltpu.VMEM)


def unpack_small(full, final):
    vector = lambda rows: struct((rows, 16), FULL)
    return call(
        unpack_body,
        (struct((32, 64), FULL), struct((64, 128), FULL), struct((128, 256), FULL), struct((240, 49), FULL))
        + (struct((128, 512), FULL), struct((256, 512), FULL))
        + (vector(2), vector(4))
        + (vector(8),) * 7
        + (struct((16, 32), FULL), vector(16), vector(15), vector(8), vector(8)),
        in_specs=[VMEM_SPEC] * 2,
        scratch_shapes=[pltpu.VMEM((2 * C_ROWS, 128), LOW)],
    )(full, final)


def widen_body(values, out_e, out_r):
    size = values.shape[1]
    for piece in range(values.shape[0]):
        for first in range(piece * size, (piece + 1) * size, min(size, 512)):
            part, rest = first // 1024, first % 1024
            out = (out_e, out_r)[rest // 512]
            rows = slice(rest % 512, rest % 512 + min(size, 512))
            here = slice(first - piece * size, first - piece * size + min(size, 512))
            out[rows, part * 128 : part * 128 + 128] = values[piece, here, :].astype(FULL)


def widen(values):
    return call(widen_body, (struct((512, 512), FULL),) * 2)(values)


def swap(values, pairs):
    return lax.ppermute(values, "dp", pairs)


def exchange(blocks):
    return (
        blocks[0],
        swap(blocks[1], CORE_SWAP),
        swap(blocks[2], CHIP_SWAP),
        swap(blocks[3], BOTH_SWAP),
    )


def exchange_far(own, near, far):
    across = swap(far, CHIP_SWAP)
    return [own, swap(near, CORE_SWAP), across, swap(across, CORE_SWAP)]


def gather(values):
    across = swap(values, CHIP_SWAP)
    return (values, swap(values, CORE_SWAP), across, swap(across, CORE_SWAP))


def hold(*values):
    return lax.optimization_barrier(values)


def onward(keeps, gots):
    parts = [(k[1].astype(FULL) + g[1].astype(FULL)).astype(LOW) for k, g in zip(keeps, gots)]
    return parts[0] if len(parts) == 1 else jnp.concatenate(parts, axis=0)


def own(keeps, gots, other):
    parts, row = [], 0
    for k, g in zip(keeps, gots):
        value = k[0].astype(FULL) + g[0].astype(FULL) + other[row : row + k.shape[1]].astype(FULL)
        parts.append(value.astype(LOW))
        row += k.shape[1]
    return parts[0] if len(parts) == 1 else jnp.concatenate(parts, axis=0)


def split(values, count):
    return values.reshape(count, -1, values.shape[-1])


def trade(parts):
    return lax.all_to_all(parts, "mp", split_axis=0, concat_axis=0, tiled=True)


def spread_sum(parts):
    value = jnp.sum(parts.astype(FULL), axis=0).astype(LOW)
    return jnp.broadcast_to(value[None], parts.shape)


def flat(parts):
    return parts.reshape(-1, parts.shape[2])


def per_device(
    mp_count,
    block_input,
    norm1_gain,
    norm1_bias,
    input_weight,
    input_bias,
    conv_weight,
    conv_bias,
    gate_weight1,
    gate_bias1,
    gate_weight2,
    gate_bias2,
    gate_weight3,
    gate_bias3,
    output_weight,
    output_bias,
    layer_scale1,
    norm2_gain,
    norm2_bias,
    expand_weight,
    expand_bias,
    reduce_weight,
    reduce_bias,
    layer_scale2,
    cotangent,
):
    me = lax.axis_index("dp").astype(jnp.int32).reshape(1)

    def turned(weight):
        return jnp.transpose(weight, (1, 2, 0)).reshape(-1, weight.shape[0])

    where = lax.axis_index("mp").astype(jnp.int32).reshape(1)
    late_weights = turned(expand_weight), reduce_weight.reshape(-1, WIDTH)
    small, far_small, *x_blocks = first_kernel(
        me,
        where,
        mp_count,
        block_input.reshape(SHARD, -1),
        *late_weights,
        (
            turned(output_weight),
            turned(gate_weight3),
            turned(gate_weight2),
            turned(gate_weight1),
            turned(conv_weight),
            norm1_gain,
            norm1_bias,
            input_bias,
            conv_bias,
            gate_bias1,
            gate_bias2,
            gate_bias3,
            output_bias,
            layer_scale1,
            norm2_gain,
            norm2_bias,
            reduce_bias,
            layer_scale2,
            expand_bias.T,
        ),
    )
    in_weight = turned(input_weight)
    in_across = swap(in_weight, CHIP_SWAP)
    small, far_small, x_blocks, in_across = hold(small, far_small, x_blocks, in_across)
    small_across = swap(far_small, CHIP_SWAP)
    x_blocks = exchange(x_blocks)
    own_dy, near, far = second_kernel(me, cotangent.reshape(SHARD, -1), *late_weights)
    small_across, near, far, in_weight, in_across = hold(small_across, near, far, in_weight, in_across)
    slabs = (small, swap(small, CORE_SWAP), small_across, swap(small_across, CORE_SWAP))
    in_shards = (in_weight, swap(in_weight, CORE_SWAP), in_across, swap(in_across, CORE_SWAP))
    vec, expand, w1, w1_back, w2, w3, w_in, w_out, taps, perm = prepare(me, slabs, in_shards)
    piece = small_across[S_ROWS:]
    vec, near, far, piece = hold(vec, near, far, piece)
    late_across = trade(jnp.broadcast_to(piece[None], (mp_count,) + piece.shape))
    x_blocks, near, far, vec = hold(x_blocks, near, far, vec)
    core, across = swap(near, CORE_SWAP), swap(far, CHIP_SWAP)
    x, z1, u, dwv = front(x_blocks, perm, vec, w_in, taps)
    dwv, core, across, late_across = hold(dwv, core, across, flat(late_across))
    passed, late_passed = swap(across, CORE_SWAP), swap(late_across, CORE_SWAP)
    z2 = branch_forward(dwv, x, vec, w1, w2, w3, w_out)
    others = (near, core, late_across, late_passed, across, passed)
    dy, f, dz, bias_grads, sib_g, keep_g = feed_forward(z2, own_dy, others, perm, vec, expand)


    got_g = swap(sib_g, CORE_SWAP)
    on_g = onward([keep_g], [got_g])
    dz, on_g = hold(dz, on_g)
    other_g = swap(on_g, CHIP_SWAP)
    *outs, g, dx1, sib, keep_late = branch_backward(
        me, dwv, x, dy, f, dz, vec, w1, w1_back, w2, w3, w_out, perm, bias_grads
    )
    got_late = swap(sib, CORE_SWAP)
    g, other_g, outs, got_late = hold(g, other_g, outs, got_late)
    part_g = split(own([keep_g], [got_g], other_g), mp_count)
    on_late = onward([keep_late], [got_late])
    g, part_g, on_late = hold(g, part_g, on_late)
    part_g = trade(part_g)
    other_late = swap(on_late, CHIP_SWAP)
    outs = exchange_far(*outs)

    du1, sib, keep1 = conv_backward(me, g, u, taps, z1, 4)
    got1 = swap(sib, CORE_SWAP)
    du1, part_g, other_late = hold(du1, part_g, other_late)
    part_late = split(own([keep_late], [got_late], other_late), mp_count)
    mixed = jnp.concatenate([spread_sum(part_g), part_late], axis=1)
    g, mixed = hold(g, mixed)
    mixed = trade(mixed)

    du0, sib, keep0 = conv_backward(me, g, u, taps, z1, 0)
    got0 = swap(sib, CORE_SWAP)
    du0, got0, got1, outs = hold(du0, got0, got1, outs)
    on_c = onward([keep0, keep1], [got0, got1])
    du0, on_c = hold(du0, on_c)
    other_c = swap(on_c, CHIP_SWAP)

    *ins, e0, e1, e2, e3 = input_backward(me, (du0, du1), x, dx1, vec, w_in, perm)
    ins, other_c = hold(ins, other_c)
    ins = exchange_far(*ins)
    block_output = from_pixels(me, outs).reshape(block_input.shape)
    ends = exchange((e0, e1, e2, e3))
    ins[1], other_c, mixed = hold(ins[1], other_c, mixed)
    rows = part_g.shape[1]
    full_g, part_late = mixed[:, :rows], mixed[:, rows:]
    part_c = split(own([keep0, keep1], [got0, got1], other_c), mp_count)
    mixed = trade(jnp.concatenate([spread_sum(part_late), part_c], axis=1))
    sum_e, sum_r = widen(full_g)
    mixed, ins = hold(mixed, ins)
    rows = part_late.shape[1]
    full_late, part_c = mixed[:, :rows], mixed[:, rows:]
    end = sum(e.astype(FULL) for e in ends).astype(LOW)
    end = jnp.broadcast_to(end[None], (mp_count,) + end.shape)
    full_c = trade(jnp.concatenate([spread_sum(part_c), end], axis=1))

    def back(values, blocks):
        return jnp.transpose(values.reshape(blocks, 16, values.shape[1]), (2, 0, 1))

    (
        g1, g2, g3, gconv, gout, gin, gb1, gb2, gb3, gob, gls1, gn2g, gn2b, grb, gls2, geb, ginb, gcb, gn1g, gn1b,
    ) = unpack_small(flat(full_late), full_c)
    input_grad = from_pixels(me, ins).reshape(block_input.shape)
    return (
        block_output,
        input_grad,
        gn1g,
        gn1b,
        back(gin, 16),
        ginb,
        back(gconv, 15),
        gcb,
        back(g1, 2),
        gb1,
        back(g2, 4),
        gb2,
        back(g3, 8),
        gb3,
        back(gout, 8),
        gob,
        gls1,
        gn2g,
        gn2b,
        back(sum_e, 32),
        geb.T,
        sum_r.reshape(32, 16, WIDTH),
        grb,
        gls2,
    )


def solution(mesh):
    pixels = P(None, "dp", "mp")
    vector = P(None, "dp")
    matrix = P(None, None, "dp")
    params = (
        vector, vector, matrix, vector, matrix, vector, matrix, vector, matrix, vector, matrix, vector,
        matrix, vector, vector, vector, vector, matrix, vector, P(None, "dp", None), vector, vector,
    )
    return jax.shard_map(
        partial(per_device, mesh.shape["mp"]),
        mesh=mesh,
        in_specs=(pixels,) + params + (pixels,),
        out_specs=(pixels, pixels) + params,
        check_vma=False,
    )
```

```python
from functools import partial

import jax
import jax.numpy as jnp
from jax import lax
from jax.experimental import pallas as pl
from jax.experimental.pallas import tpu as pltpu
from jax.sharding import PartitionSpec as P

WIDTH = 512
GROUP = 64
SIDE = 14
CROP = SIDE * SIDE
CROPS = 8
TOKENS = CROP * CROPS
SHARD = 128
TAPS = 49
EPSILON = 1e-06
LOW = jnp.bfloat16
FULL = jnp.float32
VMEM = 58 * 1024 * 1024

NN = (((1,), (0,)), ((), ()))
NT = (((1,), (1,)), ((), ()))
TN = (((0,), (0,)), ((), ()))

CORE_SWAP = [(0, 1), (1, 0), (2, 3), (3, 2)]
CHIP_SWAP = [(0, 2), (2, 0), (1, 3), (3, 1)]
BOTH_SWAP = [(0, 3), (3, 0), (1, 2), (2, 1)]

S_GATE3, S_GATE2, S_GATE1, S_CONV, S_EXPAND, S_OUT, S_ROWS = 0, 256, 320, 352, 560, 592, 1104
S_LANE = 64
(V_N1G, V_N1B, V_INB, V_CB, V_GB1, V_GB2, V_GB3, V_OB, V_LS1, V_N2G, V_N2B, V_RB, V_LS2) = range(13)
VECTORS = 13
E_OUT, E_VEC, E_EXPAND, E_ROWS = 0, 352 + 512, 496 + 512, 640 + 512
E_GATE = 512


def mm(left, right, dims=NN):
    return lax.dot_general(left, right, dims, preferred_element_type=FULL)


def call(body, out, weight=1.0, **kwargs):
    flops, moved = int(weight * 1.15e9 / 4), 1 << 10
    return pl.pallas_call(
        body,
        out_shape=out,
        compiler_params=pltpu.CompilerParams(vmem_limit_bytes=VMEM),
        cost_estimate=pl.CostEstimate(flops=flops, bytes_accessed=moved, transcendentals=0),
        **kwargs,
    )


def struct(shape, dtype):
    return jax.ShapeDtypeStruct(shape, dtype)


SMEM_SPEC = pl.BlockSpec(memory_space=pltpu.SMEM)


def whole(shape):
    return pl.BlockSpec(shape, lambda i: (0,) * len(shape))


def turn_blocks(me, x_ref, outs, wide, blocks):
    lanes = x_ref.shape[1]
    for dest in range(4):
        for crop in range(CROPS):
            start = CROP * (CROPS * dest + crop)
            base = start // 128 * 128
            window = x_ref[:, base : base + min(lanes - base, 384)].astype(FULL)
            wide[pl.ds(crop, CROP, stride=CROPS), :] = window[:, start - base : start - base + CROP].T
        blocks[dest ^ me] = wide[...].astype(LOW)
    for k in range(4):
        outs[k][...] = blocks[k]


PIXEL_SCRATCH = [pltpu.VMEM((TOKENS, SHARD), FULL), pltpu.VMEM((4, TOKENS, SHARD), LOW)]


JOINT = TOKENS + 4 * 1024


def second_body(me_ref, x_ref, expand, reduce, own, near, far, wide, blocks):
    turn_blocks(me_ref[0], x_ref, (own, near.at[0:TOKENS], far.at[0], far.at[1]), wide, blocks)
    for part in range(4):
        lanes = slice(part * 128, part * 128 + 128)
        first = TOKENS + part * 1024
        near[first : first + 512, :] = expand[:, lanes]
        near[first + 512 : first + 1024, :] = reduce[:, lanes]


def second_kernel(me, x, expand, reduce):
    return call(
        second_body,
        (struct((TOKENS, SHARD), LOW), struct((JOINT, SHARD), LOW), struct(FAR, LOW)),
        weight=0.05,
        in_specs=[SMEM_SPEC] + [pl.BlockSpec(memory_space=pltpu.VMEM)] * 3,
        scratch_shapes=PIXEL_SCRATCH,
    )(me, x, expand, reduce)


def first_body(part, me_ref, part_ref, x_ref, expand, reduce, *refs):
    small, far = refs[19], refs[20]
    pack_body(*refs[:19], small, refs[25])
    far[0:S_ROWS, :] = small[...]
    size = 4096 // part
    for number in range(part):
        lanes, rest = number * size // 1024, number * size % 1024
        source = (expand, reduce)[rest // 512]

        @pl.when(part_ref[0] == number)
        def _():
            far[S_ROWS:, :] = source[rest % 512 : rest % 512 + size, lanes * 128 : lanes * 128 + 128]

    turn_blocks(me_ref[0], x_ref, refs[21:25], refs[26], refs[27])


def first_kernel(me, where, parts, x, expand, reduce, small):
    slab = (S_ROWS, 128)
    return call(
        partial(first_body, parts),
        (struct(slab, LOW), struct((S_ROWS + 4096 // parts, 128), LOW)) + (struct((TOKENS, SHARD), LOW),) * 4,
        weight=0.05,
        in_specs=[SMEM_SPEC] * 2 + [pl.BlockSpec(memory_space=pltpu.VMEM)] * 22,
        scratch_shapes=[pltpu.VMEM((S_OUT, 128), FULL)] + PIXEL_SCRATCH,
    )(me, where, x, expand, reduce, *small)


def from_pixels_body(me_ref, own, core, across, passed, out_ref, wide, blocks):
    me = me_ref[0]
    blocks[me] = own[...]
    blocks[1 ^ me] = core[...]
    blocks[2 ^ me] = across[0]
    blocks[3 ^ me] = passed[1]
    for source in range(4):
        wide[...] = blocks[source].astype(FULL)
        for crop in range(CROPS):
            start = CROP * (CROPS * source + crop)
            part = wide[pl.ds(crop, CROP, stride=CROPS), :].T
            out_ref[:, start : start + CROP] = part.astype(LOW)


def from_pixels(me, blocks):
    return call(
        from_pixels_body,
        struct((SHARD, 4 * TOKENS), LOW),
        weight=4.0,
        in_specs=[SMEM_SPEC] + [pl.BlockSpec(memory_space=pltpu.VMEM)] * 4,
        scratch_shapes=[pltpu.VMEM((TOKENS, SHARD), FULL), pltpu.VMEM((4, TOKENS, SHARD), LOW)],
    )(me, *blocks)


FAR = (2, TOKENS, SHARD)


def far_spec(tile):
    return pl.BlockSpec((2, tile, SHARD), lambda i: (0, i, 0))


def pack_body(out_weight, g3, g2, g1, conv, *refs):
    vectors, expand, out_ref, slab = refs[:VECTORS], refs[VECTORS], refs[VECTORS + 1], refs[VECTORS + 2]
    slab[...] = jnp.zeros_like(slab)
    slab[S_GATE3 : S_GATE3 + 128, :] = g3[:, :128].astype(FULL)
    slab[S_GATE3 + 128 : S_GATE3 + 256, :] = g3[:, 128:].astype(FULL)
    slab[S_GATE2 : S_GATE2 + 64, :] = g2[...].astype(FULL)
    slab[S_GATE1 : S_GATE1 + 32, :GROUP] = g1[...].astype(FULL)
    slab[S_CONV : S_CONV + 240, :TAPS] = conv[...].astype(FULL)
    for number, ref in enumerate(vectors):
        first = S_CONV + 16 * number + (1 if number == V_CB else 0)
        slab[first : first + ref.shape[0], S_LANE : S_LANE + 16] = ref[...].astype(FULL)
    slab[S_EXPAND : S_EXPAND + 32, S_LANE : S_LANE + 16] = expand[...].astype(FULL).T
    out_ref[0:S_OUT, :] = slab[...].astype(LOW)
    for part in range(4):
        rows = slice(S_OUT + part * 128, S_OUT + part * 128 + 128)
        out_ref[rows, :] = out_weight[:, part * 128 : part * 128 + 128]


TILE_OF = (2, 0, 3, 1)


def iota(shape, dim):
    return lax.broadcasted_iota(jnp.int32, shape, dim)


def spread(lanes):
    return jnp.where(iota((128, lanes), 1) % 16 + S_LANE == iota((128, lanes), 0), 1.0, 0.0).astype(LOW)


def prepare_body(me_ref, *refs):
    slabs, ins = refs[0:4], refs[4:8]
    vec, expand, w1, w1_back, w2, w3, w_in, w_out, taps, perm, channels = refs[8:]
    me = me_ref[0]
    totals = jnp.zeros((VECTORS, 1024), FULL)
    spread_wide = spread(1024)
    row = iota((VECTORS * 16, 1024), 0) % 16
    lane = iota((VECTORS * 16, 1024), 1)
    in_row = row == lane // 64
    spread_expand = spread(512)
    expand_rows = iota((32, 512), 0) == iota((32, 512), 1) // 16
    w1[...] = jnp.zeros_like(w1)
    channels[0:GROUP, :] = jnp.where(iota((GROUP, 128), 1) == TAPS // 2, 3.0, 0.0)
    for k in range(4):
        source = me ^ k
        slab = slabs[k]
        values = mm(slab[S_CONV : S_CONV + VECTORS * 16, :], spread_wide)
        values = jnp.where(in_row & (lane // 16 % 4 == source), values, 0.0)
        totals = totals + jnp.sum(values.reshape(VECTORS, 16, 1024), axis=1)
        values = mm(slab[S_EXPAND : S_EXPAND + 32, :], spread_expand)
        values = jnp.sum(jnp.where(expand_rows, values, 0.0), axis=0, keepdims=True)
        slot = TILE_OF[k]
        expand[8 * slot : 8 * slot + 8, :] = jnp.broadcast_to(values, (8, 512))
        for a in range(16):
            place = pl.ds(pl.multiple_of(a * 64 + source * 16, 16), 16)
            rows = slice(a * 16, a * 16 + 16)
            w_in[place, :] = ins[k][rows, :]
            if a < 15:
                later = pl.ds(pl.multiple_of((a + 1) * 64 + source * 16, 16), 16)
                channels[later, :] = slab[S_CONV + a * 16 : S_CONV + a * 16 + 16, :].astype(FULL)
            if a < 8:
                for part in range(4):
                    first = S_OUT + part * 128 + a * 16
                    w_out[place, part * 128 : part * 128 + 128] = slab[first : first + 16, :]
                w3[place, 0:128] = slab[S_GATE3 + a * 16 : S_GATE3 + a * 16 + 16, :]
                w3[place, 128:256] = slab[S_GATE3 + 128 + a * 16 : S_GATE3 + 128 + a * 16 + 16, :]
            if a < 4:
                w2[place, :] = slab[S_GATE2 + a * 16 : S_GATE2 + a * 16 + 16, :]
            if a < 2:
                w1[place, :] = slab[S_GATE1 + a * 16 : S_GATE1 + a * 16 + 16, :]
        column = iota((SHARD, WIDTH), 0)
        target = column // 16 * 64 + source * 16 + column % 16
        perm[k * SHARD : (k + 1) * SHARD, :] = jnp.where(iota((SHARD, WIDTH), 1) == target, 1.0, 0.0).astype(LOW)
    vec[0:VECTORS, :] = totals
    vec[VECTORS:16, :] = jnp.zeros((16 - VECTORS, 1024), FULL)
    single = w1[...].astype(FULL)
    w1_back[...] = (single + pltpu.roll(single, GROUP, 1)).astype(LOW)
    taps[...] = channels[...].T[0:64, :]


def prepare(me, slabs, ins):
    return call(
        prepare_body,
        (
            struct((16, 1024), FULL),
            struct((32, 512), FULL),
            struct((128, 128), LOW),
            struct((128, 128), LOW),
            struct((256, 128), LOW),
            struct((512, 256), LOW),
            struct((1024, 512), LOW),
            struct((512, 512), LOW),
            struct((64, 1024), FULL),
            struct((512, 512), LOW),
        ),
        weight=0.05,
        in_specs=[SMEM_SPEC] + [pl.BlockSpec(memory_space=pltpu.VMEM)] * 8,
        scratch_shapes=[pltpu.VMEM((1024, 128), FULL)],
    )(me, *slabs, *ins)


def normed(values):
    center = jnp.sum(values, axis=1, keepdims=True) * (1.0 / WIDTH)
    away = values - center
    spread_sq = jnp.sum(away * away, axis=1, keepdims=True) * (1.0 / WIDTH)
    inverse = lax.rsqrt(spread_sq + EPSILON)
    return away * inverse, inverse


def norm_back(grad, unit, inverse, gain):
    grad_unit = grad * gain
    first = jnp.sum(grad_unit, axis=1, keepdims=True) * (1.0 / WIDTH)
    second = jnp.sum(grad_unit * unit, axis=1, keepdims=True) * (1.0 / WIDTH)
    return inverse * (grad_unit - first - unit * second)


def total(values):
    return jnp.sum(values, axis=0, keepdims=True)


def row(vec, number, lanes=WIDTH):
    return vec[number : number + 1, 0:lanes]


def rows_spec(tile, lanes):
    return pl.BlockSpec((tile, lanes), lambda i: (i, 0))


def chunks(count, size, body):
    def step(i, carry):
        body(pl.ds(pl.multiple_of(i * size, size), size))
        return carry

    lax.fori_loop(0, count // size, step, 0)


NORM_ROWS = 224
HALVES = (slice(0, TOKENS // 2), slice(TOKENS // 2, TOKENS))


def stagger(chain, height, lead):
    cut = height // 32 * 16
    ahead, behind = chain(slice(0, cut)), chain(slice(cut, height))
    for _ in range(lead):
        next(ahead)
    for _ in ahead:
        next(behind)
    for _ in behind:
        pass


def join(blocks, perm, rows):
    return mm(jnp.concatenate([r[rows, :] for r in blocks], axis=1), perm[...])


def conv_rows(source, weights, emit, flip):
    zero = jnp.zeros((CROPS, 128), FULL)

    def tap_row(i, r, sums):
        base = (i + r - 3) * SIDE
        values = [source[base + c] for c in range(SIDE)]
        first = (6 - r) * 7 if flip else r * 7
        taps = [weights[first + (6 - s if flip else s)] for s in range(7)]
        for s in range(7):
            for c in range(SIDE):
                if 0 <= c + s - 3 < SIDE:
                    sums[c] = sums[c] + taps[s] * values[c + s - 3]

    def one_row(i, first, last):
        sums = [zero] * SIDE
        for r in range(first, last):
            tap_row(i, r, sums)
        emit(i, sums)

    def inner_row(i, carry):
        one_row(i, 0, 7)
        return carry

    for i in range(3):
        one_row(i, 3 - i, 7)
    lax.fori_loop(3, SIDE - 3, inner_row, 0)
    for i in range(SIDE - 3, SIDE):
        one_row(i, 0, 17 - i)


def wide_taps(taps, weights):
    for tap in range(TAPS):
        weights[tap] = jnp.broadcast_to(taps[tap : tap + 1, :], (CROPS, 128))


PIXEL_BLOCK = pl.BlockSpec((CROP, CROPS, 128), lambda i: (0, 0, i))


def lane_block(rows):
    return pl.BlockSpec((rows, 128), lambda i: (0, i))


def front_body(r0, r1, r2, r3, perm, vec, w_in, taps, vec_part, x, z, u, dwv, weights):
    @pl.when(pl.program_id(0) == 0)
    def _():
        for rows in HALVES:
            x[rows, :] = join((r0, r1, r2, r3), perm, rows).astype(LOW)

        def norm_rows(rows):
            unit, _ = normed(x[rows, :].astype(FULL))
            z[rows, :] = (unit * row(vec, V_N1G) + row(vec, V_N1B)).astype(LOW)

        chunks(TOKENS, NORM_ROWS, norm_rows)

    wide_taps(taps, weights)
    values = mm(z[...], w_in[...], NT) + vec_part[V_INB : V_INB + 1, :]
    u[...] = values.reshape(CROP, CROPS, 128)
    bias = jnp.broadcast_to(vec_part[V_CB : V_CB + 1, :], (CROPS, 128))

    def emit(i, sums):
        for c in range(SIDE):
            dwv[i * SIDE + c] = (sums[c] + bias) * (1.0 / 3.0)

    conv_rows(u, weights, emit, False)


def front(blocks, perm, vec, w_in, taps):
    pixels = struct((CROP, CROPS, 1024), FULL)
    rows = struct((TOKENS, WIDTH), LOW)
    x, z, u, dwv = call(
        front_body,
        (rows, rows, pixels, pixels),
        weight=28.0,
        grid=(8,),
        in_specs=[whole((TOKENS, SHARD))] * 4
        + [
            whole((512, 512)),
            whole((16, 1024)),
            pl.BlockSpec((128, 512), lambda i: (i, 0)),
            lane_block(64),
            lane_block(16),
        ],
        out_specs=(whole((TOKENS, WIDTH)), whole((TOKENS, WIDTH)), PIXEL_BLOCK, PIXEL_BLOCK),
        scratch_shapes=[pltpu.VMEM((TAPS, CROPS, 128), FULL)],
    )(*blocks, perm, vec, w_in, taps, vec)
    return x, z, u, dwv.reshape(TOKENS, 1024)


def branch_body(dwv, x, vec, w1, w2, w3, w_out, z_out):
    def chain(rows):
        first = dwv[rows, 0:128]
        q = (first * pltpu.roll(first, GROUP, 1)).astype(LOW)
        yield
        t = mm(q, w1[...], NT) + row(vec, V_GB1, 128)
        q = (t * dwv[rows, 128:256]).astype(LOW)
        yield
        t = mm(q, w2[...], NT) + row(vec, V_GB2, 256)
        q = (t * dwv[rows, 256:512]).astype(LOW)
        yield
        t = mm(q, w3[...], NT) + row(vec, V_GB3, 512)
        q = (t * dwv[rows, 512:1024]).astype(LOW)
        yield
        branch = mm(q, w_out[...], NT) + row(vec, V_OB)
        middle = x[rows, :].astype(FULL) + row(vec, V_LS1) * branch
        yield
        unit, _ = normed(middle)
        z_out[rows, :] = (unit * row(vec, V_N2G) + row(vec, V_N2B)).astype(LOW)
        yield

    stagger(chain, dwv.shape[0], 2)


def branch_forward(dwv, x, vec, w1, w2, w3, w_out, tile=784):
    return call(
        branch_body,
        struct((TOKENS, WIDTH), LOW),
        weight=7.0,
        grid=(TOKENS // tile,),
        in_specs=[
            rows_spec(tile, 1024),
            rows_spec(tile, WIDTH),
            whole((16, 1024)),
            whole((128, 128)),
            whole((256, 128)),
            whole((512, 256)),
            whole((512, 512)),
        ],
        out_specs=rows_spec(tile, WIDTH),
    )(dwv, x, vec, w1, w2, w3, w_out)


def gelu_parts(s):
    bell = jnp.exp2((-0.5 * 1.4426950408889634) * (s * s))
    size = jnp.abs(s)
    t = pltpu.reciprocal(1.0 + (0.3275911 * 0.7071067811865476) * size, approx=True)
    poly = 0.5 * 1.061405429
    for coefficient in (-1.453152027, 1.421413741, -0.284496736, 0.254829592):
        poly = poly * t + 0.5 * coefficient
    tail = poly * t * bell
    cdf = jnp.where(s >= 0.0, 1.0 - tail, tail)
    return s * cdf, cdf + s * (bell * 0.3989422804014327)


PIECE = 16


def mlp_body(z, r0, perm, vec, expand, c0, c1, w2, w3, y2, y3, *refs):
    dy_out, f_out, dz_out, gb, sibling, keep = refs[0:6]
    dy, f, dz, r1, r2, r3, we, wr, df, s0, s1, g0, g1, hid, grad_s, grads, sums, sems = refs[6:]
    pre, grad_h = (s0, s1), (g0, g1)
    half = TOKENS // 2
    shards = ((c1, TOKENS), (w3, 0), (c0, TOKENS), (w2, 0))

    def copies(slot):
        for part in range(4):
            for number, matrix in enumerate((we, wr)):
                shard, first = shards[slot]
                rows = pl.ds(first + part * 1024 + number * 512, 512)
                yield pltpu.make_async_copy(
                    shard.at[rows], matrix.at[slot, :, pl.ds(part * 128, 128)], sems.at[slot]
                )

    near = [
        pltpu.make_async_copy(block, r, sems.at[4 + number])
        for number, (block, r) in enumerate(((c1.at[pl.ds(0, TOKENS)], r1), (y2.at[0], r2), (y3.at[1], r3)))
    ]
    for copy in near:
        copy.start()
    for slot in range(4):
        for copy in copies(slot):
            copy.start()

    def arrived(slot):
        for matrix in (we, wr):
            pltpu.make_async_copy(matrix.at[slot], matrix.at[slot], sems.at[slot]).wait()

    def leave(tile):
        out = (sibling, keep)[tile // 2]
        return [
            pltpu.make_async_copy(
                grads.at[tile, :, pl.ds(part * 128, 128)],
                out.at[tile % 2, pl.ds(part * 1024, 1024)],
                sems.at[7 + tile],
            )
            for part in range(4)
        ]

    def start(copies):
        for copy in copies:
            copy.start()

    for copy in near:
        copy.wait()
    for rows in HALVES:
        dy[rows, :] = join((r0, r1, r2, r3), perm, rows).astype(LOW)
    dy_leaves = pltpu.make_async_copy(dy, dy_out, sems.at[11])
    dy_leaves.start()

    def scaled(rows):
        df[rows, :] = (dy[rows, :].astype(FULL) * row(vec, V_LS2)).astype(LOW)
        f[rows, :] = jnp.zeros((112, WIDTH), FULL)
        dz[rows, :] = jnp.zeros((112, WIDTH), FULL)

    chunks(TOKENS, 112, scaled)
    sums[...] = jnp.zeros_like(sums)
    hid[1, HALVES[1], :] = jnp.zeros((half, 512), LOW)
    grad_s[1, HALVES[1], :] = jnp.zeros((half, 512), LOW)
    arrived(0)
    s0[...] = mm(z[HALVES[0], :], we[0], NT)
    g0[...] = mm(df[HALVES[0], :], wr[0], NT)
    pieces = half // PIECE

    def unit(here, tile, before, after):
        there = 1 - here
        rows = HALVES[there]
        now, last = tile & 1, (tile & 1) ^ 1
        ready = last if here == 0 else now
        bias = expand[pl.ds(pl.multiple_of(tile * 8, 8), 1), :]
        done = [0]
        column = [jnp.zeros((8, 512), FULL)]

        def some(part):
            while done[0] < pieces * part // 6:
                first = done[0] * PIECE
                piece = slice(first, first + PIECE)
                place = slice(here * half + first, here * half + first + PIECE)
                act, slope = gelu_parts(pre[here][piece, :] + bias)
                hid[now, place, :] = act.astype(LOW)
                grad = (grad_h[here][piece, :] * slope).astype(LOW)
                grad_s[now, place, :] = grad
                grad = grad.astype(FULL)
                column[0] = column[0] + (grad[0:8] + grad[8:16])
                done[0] += 1

        if here == 0:
            grads[before, 0:512, :] = mm(grad_s[last], z[...], TN).astype(LOW)
        else:
            grads[before, 512:1024, :] = mm(hid[last], df[...], TN).astype(LOW)
        some(2)
        pre[there][...] = mm(z[rows, :], we[after], NT)
        some(3)
        grad_h[there][...] = mm(df[rows, :], wr[after], NT)
        some(4)
        f[rows, :] += mm(hid[ready, rows, :], wr[before if here == 0 else tile])
        some(5)
        dz[rows, :] += mm(grad_s[ready, rows, :], we[before if here == 0 else tile])
        some(6)
        sums[tile] += column[0]

    def one_tile(tile, carry):
        before = jnp.maximum(tile - 1, 0)
        for number in range(2):

            @pl.when(tile == number + 2)
            def _():
                start(leave(number))

        unit(0, tile, before, tile)

        @pl.when(tile < 3)
        def _():
            arrived(tile + 1)

        unit(1, tile, before, jnp.minimum(tile + 1, 3))
        return carry

    lax.fori_loop(0, 4, one_tile, 0)
    start(leave(2))

    def results(number):
        rows = pl.ds(number * half, half)
        return [
            pltpu.make_async_copy(value.at[rows], out.at[rows], sems.at[12 + number])
            for value, out in ((f, f_out), (dz, dz_out))
        ]

    start(results(0))
    rows = HALVES[1]
    f[rows, :] += mm(hid[1, rows, :], wr[3])
    dz[rows, :] += mm(grad_s[1, rows, :], we[3])
    start(results(1))
    grads[3, 0:512, :] = mm(grad_s[1], z[...], TN).astype(LOW)
    grads[3, 512:1024, :] = mm(hid[1], df[...], TN).astype(LOW)
    start(leave(3))
    for tile in range(4):
        gb[8 * tile : 8 * tile + 8, :] = sums[tile]
    dy_leaves.wait()
    for copies in [results(0), results(1)] + [leave(tile) for tile in range(4)]:
        for copy in copies:
            copy.wait()


def feed_forward(z, own_dy, others, perm, vec, expand):
    vmem = pl.BlockSpec(memory_space=pltpu.VMEM)
    anywhere = pl.BlockSpec(memory_space=pl.ANY)
    half = TOKENS // 2
    pair = struct((2, 4096, 128), LOW)
    rows = struct((TOKENS, WIDTH), FULL)
    return call(
        mlp_body,
        (struct((TOKENS, WIDTH), LOW), rows, rows, struct((32, 512), FULL), pair, pair),
        weight=40.0,
        in_specs=[vmem] * 5 + [anywhere] * 6,
        out_specs=(anywhere,) * 3 + (vmem,) + (anywhere,) * 2,
        scratch_shapes=[pltpu.VMEM((TOKENS, WIDTH), LOW)]
        + [pltpu.VMEM((TOKENS, WIDTH), FULL)] * 2
        + [pltpu.VMEM((TOKENS, SHARD), LOW)] * 3
        + [pltpu.VMEM((4, 512, 512), LOW)] * 2
        + [pltpu.VMEM((TOKENS, WIDTH), LOW)]
        + [pltpu.VMEM((half, 512), FULL)] * 4
        + [pltpu.VMEM((2, TOKENS, 512), LOW)] * 2
        + [pltpu.VMEM((4, 1024, 512), LOW)]
        + [pltpu.VMEM((4, 8, 512), FULL)]
        + [pltpu.SemaphoreType.DMA((14,))],
    )(z, own_dy, perm, vec, expand, *others)


def pack_vectors(values, count, source):
    lane = iota((count * 16, 1024), 1)
    keep = (iota((count * 16, 1024), 0) % 16 == lane // 64) & (lane // 16 % 4 == source)
    tall = jnp.broadcast_to(values[:, None, :], (count, 16, 1024)).reshape(count * 16, 1024)
    gather = jnp.where(iota((1024, 128), 0) % 16 == iota((1024, 128), 1), 1.0, 0.0).astype(LOW)
    return mm(jnp.where(keep, tall, 0.0).astype(LOW), gather)


def part_pair(parts, sibling, keep):
    sibling[0] = parts[1]
    sibling[1] = parts[3]
    keep[0] = parts[0]
    keep[1] = parts[2]


def branch_back_body(steps, me_ref, dwv, x, dy, f, dz, vec, w1, w1_back, w2, w3, w_out, perm, gb, *refs):
    (o0, o1, far, g_out, dx_out, sibling, keep) = refs[0:7]
    acc_o, acc_3, acc_2, acc_1, sums, parts = refs[7:]
    step = pl.program_id(0)

    @pl.when(step == 0)
    def _():
        acc_o[...] = jnp.zeros_like(acc_o)
        acc_3[...] = jnp.zeros_like(acc_3)
        acc_2[...] = jnp.zeros_like(acc_2)
        acc_1[...] = jnp.zeros_like(acc_1)
        sums[...] = jnp.zeros_like(sums)

    third = 1.0 / 3.0

    def chain(rows):
        first = dwv[rows, 0:128]
        turned = pltpu.roll(first, GROUP, 1)
        q0 = (first * turned).astype(LOW)
        yield
        t1 = mm(q0, w1[...], NT) + row(vec, V_GB1, 128)
        q1 = (t1 * dwv[rows, 128:256]).astype(LOW)
        yield
        t2 = mm(q1, w2[...], NT) + row(vec, V_GB2, 256)
        q2 = (t2 * dwv[rows, 256:512]).astype(LOW)
        yield
        t3 = mm(q2, w3[...], NT) + row(vec, V_GB3, 512)
        q3 = (t3 * dwv[rows, 512:1024]).astype(LOW)
        yield
        branch = mm(q3, w_out[...], NT) + row(vec, V_OB)
        middle = x[rows, :].astype(FULL) + row(vec, V_LS1) * branch
        yield
        unit, inverse = normed(middle)
        yield
        grad = dz[rows, :]
        top = dy[rows, :].astype(FULL)
        middle_grad = top + norm_back(grad, unit, inverse, row(vec, V_N2G))
        dx_out[rows, :] = middle_grad
        sums[4:5, 0:512] += total(middle_grad * branch)
        sums[5:6, 0:512] += total(grad * unit)
        sums[6:7, 0:512] += total(grad)
        grad_branch = (middle_grad * row(vec, V_LS1)).astype(LOW)
        yield
        back = mm(grad_branch, w_out[...])
        gt3 = (back * dwv[rows, 512:1024]).astype(LOW)
        g_out[rows, 512:1024] = back * t3 * third
        yield
        back = mm(gt3, w3[...])
        acc_o[...] += mm(grad_branch, q3, TN)
        sums[3:4, 0:512] += total(grad_branch.astype(FULL))
        gt2 = (back * dwv[rows, 256:512]).astype(LOW)
        g_out[rows, 256:512] = back * t2 * third
        yield
        back = mm(gt2, w2[...])
        acc_3[...] += mm(gt3, q2, TN)
        sums[2:3, 0:512] += total(gt3.astype(FULL))
        gt1 = (back * dwv[rows, 128:256]).astype(LOW)
        g_out[rows, 128:256] = back * t1 * third
        yield
        back = mm(gt1, w1_back[...])
        acc_2[...] += mm(gt2, q1, TN)
        acc_1[...] += mm(gt1, q0, TN)
        sums[1:2, 0:256] += total(gt2.astype(FULL))
        sums[0:1, 0:128] += total(gt1.astype(FULL))
        g_out[rows, 0:128] = back * turned * third
        yield
        mlp = f[rows, :] + row(vec, V_RB)
        output = (middle + row(vec, V_LS2) * mlp).astype(LOW)
        sums[7:8, 0:512] += total(top) * row(vec, V_LS2)
        sums[8:9, 0:512] += total(top * mlp)
        yield
        blocks = mm(output, perm[...], NT).astype(LOW)
        for k, ref in enumerate((o0, o1, far.at[0], far.at[1])):
            ref[rows, :] = blocks[:, k * SHARD : (k + 1) * SHARD]
        yield

    height = dwv.shape[0]
    stagger(chain, height, 3)

    @pl.when(step == steps - 1)
    def _():
        me = me_ref[0]
        vectors = sums[0:9, :]
        expand_rows = iota((32, 512), 0) == iota((32, 512), 1) // 16
        gather = jnp.where(iota((512, 128), 0) % 16 == iota((512, 128), 1), 1.0, 0.0).astype(LOW)
        for source in range(4):
            k = source ^ me
            for a in range(8):
                rows = slice(a * 64 + source * 16, a * 64 + source * 16 + 16)
                for part in range(4):
                    first = part * 128 + a * 16
                    parts[k, first : first + 16, :] = acc_o[rows, part * 128 : part * 128 + 128].astype(LOW)
                first = E_GATE + a * 16
                parts[k, first : first + 16, :] = acc_3[rows, 0:128].astype(LOW)
                parts[k, first + 128 : first + 144, :] = acc_3[rows, 128:256].astype(LOW)
                if a < 4:
                    parts[k, first + 256 : first + 272, :] = acc_2[rows, :].astype(LOW)
                if a < 2:
                    parts[k, first + 320 : first + 336, :] = acc_1[rows, :].astype(LOW)
            parts[k, E_VEC : E_VEC + 144, :] = pack_vectors(vectors, 9, source).astype(LOW)
        for k in range(4):
            slot = TILE_OF[k]
            line = total(gb[8 * slot : 8 * slot + 8, :])
            tall = jnp.where(expand_rows, jnp.broadcast_to(line, (32, 512)), 0.0)
            parts[k, E_EXPAND : E_EXPAND + 32, :] = mm(tall.astype(LOW), gather).astype(LOW)
            parts[k, E_EXPAND + 32 : E_ROWS, :] = jnp.zeros((E_ROWS - E_EXPAND - 32, 128), LOW)
        part_pair(parts, sibling, keep)


def branch_backward(me, dwv, x, dy, f, dz, vec, w1, w1_back, w2, w3, w_out, perm, biases, tile=784):
    steps = TOKENS // tile
    wide = rows_spec(tile, WIDTH)
    block = rows_spec(tile, SHARD)
    pair = (2, E_ROWS, 128)
    return call(
        partial(branch_back_body, steps),
        (struct((TOKENS, SHARD), LOW),) * 2
        + (
            struct(FAR, LOW),
            struct((TOKENS, 1024), FULL),
            struct((TOKENS, WIDTH), FULL),
            struct(pair, LOW),
            struct(pair, LOW),
        ),
        weight=20.0,
        grid=(steps,),
        in_specs=[
            SMEM_SPEC,
            rows_spec(tile, 1024),
            wide,
            wide,
            wide,
            wide,
            whole((16, 1024)),
            whole((128, 128)),
            whole((128, 128)),
            whole((256, 128)),
            whole((512, 256)),
            whole((512, 512)),
            whole((512, 512)),
        ]
        + [whole((32, 512))],
        out_specs=(block,) * 2 + (far_spec(tile), rows_spec(tile, 1024), wide, whole(pair), whole(pair)),
        scratch_shapes=[
            pltpu.VMEM((512, 512), FULL),
            pltpu.VMEM((512, 256), FULL),
            pltpu.VMEM((256, 128), FULL),
            pltpu.VMEM((128, 128), FULL),
            pltpu.VMEM((16, 1024), FULL),
            pltpu.VMEM((4, E_ROWS, 128), LOW),
        ],
    )(me, dwv, x, dy, f, dz, vec, w1, w1_back, w2, w3, w_out, perm, biases)


def conv_back_body(me_ref, g, u, taps, z_in, du, sibling, keep, weights, grad_taps, parts, z, sem):
    step, steps = pl.program_id(0), pl.num_programs(0)
    coming = pltpu.make_async_copy(z_in, z, sem.at[0])

    @pl.when(step == 0)
    def _():
        coming.start()

    me = me_ref[0]
    wide_taps(taps, weights)
    zero = jnp.zeros((CROPS, 128), FULL)

    def emit(i, sums):
        stacked = jnp.concatenate(list(sums), axis=0).astype(LOW)
        first = i * SIDE * CROPS if isinstance(i, int) else pl.multiple_of(i * SIDE * CROPS, 16)
        du[pl.ds(first, SIDE * CROPS), :] = stacked

    conv_rows(g, weights, emit, True)

    for r in range(7):

        def one_row(i, sums):
            grads = [g[i * SIDE + c] for c in range(SIDE)]
            values = [u[(i + r - 3) * SIDE + c] for c in range(SIDE)]
            sums = list(sums)
            for c in range(SIDE):
                for s in range(7):
                    if 0 <= c + s - 3 < SIDE:
                        sums[s] = sums[s] + grads[c] * values[c + s - 3]
            return tuple(sums)

        sums = lax.fori_loop(max(0, 3 - r), min(SIDE, SIDE + 3 - r), one_row, (zero,) * 7)
        for s in range(7):
            grad_taps[r * 7 + s : r * 7 + s + 1, :] = total(sums[s])
    grad_taps[49:50, :] = total(jnp.sum(g[...], axis=0))
    grad_taps[50:51, :] = total(du[...].astype(FULL))
    grad_taps[51:128, :] = jnp.zeros((77, 128), FULL)

    @pl.when(step == 0)
    def _():
        coming.wait()

    grad_w = mm(du[...], z[...], TN)
    tall = grad_taps[...].T.astype(LOW)
    for a in range(2):
        for source in range(4):
            k = source ^ me
            rows = slice(a * 64 + source * 16, a * 64 + source * 16 + 16)
            for part in range(4):
                place = pl.ds(pl.multiple_of(part * 128 + step * 32 + a * 16, 16), 16)
                parts[k, place, :] = grad_w[rows, part * 128 : part * 128 + 128].astype(LOW)
            place = pl.ds(pl.multiple_of(512 + step * 32 + a * 16, 16), 16)
            parts[k, place, :] = tall[rows, :]

    @pl.when(step == steps - 1)
    def _():
        part_pair(parts, sibling, keep)


C_ROWS = 640


def conv_backward(me, g, u, taps, z, base):
    pixels = pl.BlockSpec((CROP, CROPS, 128), lambda i: (0, 0, i + base))
    pair = (2, C_ROWS, 128)
    return call(
        conv_back_body,
        (struct((TOKENS, 512), LOW), struct(pair, LOW), struct(pair, LOW)),
        weight=24.0,
        grid=(4,),
        in_specs=[
            SMEM_SPEC,
            pixels,
            pixels,
            pl.BlockSpec((64, 128), lambda i: (0, i + base)),
            pl.BlockSpec(memory_space=pl.ANY),
        ],
        out_specs=(lane_block(TOKENS), whole(pair), whole(pair)),
        scratch_shapes=[
            pltpu.VMEM((TAPS, CROPS, 128), FULL),
            pltpu.VMEM((128, 128), FULL),
            pltpu.VMEM((4, C_ROWS, 128), LOW),
            pltpu.VMEM((TOKENS, WIDTH), LOW),
            pltpu.SemaphoreType.DMA((1,)),
        ],
    )(me, g.reshape(CROP, CROPS, 1024), u, taps, z)


def input_back_body(steps, me_ref, du0, du1, x, dx, vec, w_in, perm, *refs):
    (o0, o1, far, e0, e1, e2, e3, sums, parts) = refs
    step = pl.program_id(0)

    @pl.when(step == 0)
    def _():
        sums[...] = jnp.zeros_like(sums)

    def chain(rows):
        grad = mm(jnp.concatenate([du0[rows, :], du1[rows, :]], axis=1), w_in[...])
        yield
        unit, inverse = normed(x[rows, :].astype(FULL))
        sums[0:1, 0:512] += total(grad * unit)
        sums[1:2, 0:512] += total(grad)
        yield
        grad_x = (dx[rows, :] + norm_back(grad, unit, inverse, row(vec, V_N1G))).astype(LOW)
        yield
        blocks = mm(grad_x, perm[...], NT).astype(LOW)
        for k, ref in enumerate((o0, o1, far.at[0], far.at[1])):
            ref[rows, :] = blocks[:, k * SHARD : (k + 1) * SHARD]
        yield

    stagger(chain, x.shape[0], 1)

    @pl.when(step == steps - 1)
    def _():
        me = me_ref[0]
        vectors = sums[0:2, :]
        for source in range(4):
            parts[source ^ me, :, :] = pack_vectors(vectors, 2, source).astype(LOW)
        for k, ref in enumerate((e0, e1, e2, e3)):
            ref[...] = parts[k]


def input_backward(me, dus, x, dx, vec, w_in, perm, tile=784):
    steps = TOKENS // tile
    wide = rows_spec(tile, WIDTH)
    end = (32, 128)
    return call(
        partial(input_back_body, steps),
        (struct((TOKENS, SHARD), LOW),) * 2 + (struct(FAR, LOW),) + (struct(end, LOW),) * 4,
        weight=8.0,
        grid=(steps,),
        in_specs=[
            SMEM_SPEC,
            *[rows_spec(tile, 512)] * 2,
            wide,
            wide,
            whole((16, 1024)),
            whole((1024, 512)),
            whole((512, 512)),
        ],
        out_specs=(rows_spec(tile, SHARD),) * 2 + (far_spec(tile),) + (whole(end),) * 4,
        scratch_shapes=[pltpu.VMEM((16, 1024), FULL), pltpu.VMEM((4, 32, 128), LOW)],
    )(me, *dus, x, dx, vec, w_in, perm)


def unpack_body(middle, final, *refs):
    (g1, g2, g3, conv, w_out, w_in), late_refs, expand = refs[0:6], refs[6:15], refs[15]
    (in_bias, conv_bias, gain, bias), low, full = refs[16:20], refs[20], refs[21]
    size = E_ROWS // middle.shape[0]
    for piece in range(middle.shape[0]):
        full[piece * size : (piece + 1) * size, :] = middle[piece, 0:size, :]
    size = final.shape[1] - 32
    last = jnp.zeros((32, 128), FULL)
    for piece in range(final.shape[0]):
        low[piece * size : (piece + 1) * size, :] = final[piece, 0:size, :]
        last = last + final[piece, size : size + 32, :].astype(FULL)
    gates = full[E_GATE:E_VEC, :].astype(FULL)
    g3[:, 0:128] = gates[0:128]
    g3[:, 128:256] = gates[128:256]
    g2[...] = gates[256:320]
    g1[...] = gates[320:352, 0:GROUP]
    taps = []
    for j, (source, first) in enumerate(((low, 0), (low, C_ROWS))):
        for part in range(4):
            rows = slice(first + part * 128, first + part * 128 + 128)
            w_in[j * 128 : j * 128 + 128, part * 128 : part * 128 + 128] = source[rows, :].astype(FULL)
        taps.append(source[first + 512 : first + 640, :])
    for part in range(4):
        lanes = slice(part * 128, part * 128 + 128)
        w_out[:, lanes] = full[lanes, :].astype(FULL)
    taps = jnp.concatenate(taps, axis=0).astype(FULL)
    conv[...] = taps[16:256, 0:TAPS]
    vectors = full[E_VEC : E_VEC + 144, :].astype(FULL)
    for number, ref in enumerate(late_refs):
        ref[...] = vectors[16 * number : 16 * number + ref.shape[0], 0:16]
    expand[...] = full[E_EXPAND : E_EXPAND + 32, 0:16].astype(FULL).T
    gain[...] = last[0:8, 0:16]
    bias[...] = last[16:24, 0:16]
    own = jnp.where(iota((256, 16), 0) % 16 == iota((256, 16), 1), 1.0, 0.0)
    rows = jnp.where(iota((16, 256), 0) == iota((16, 256), 1) // 16, 1.0, 0.0).astype(LOW)
    conv_bias[...] = mm(rows, (taps[:, 49:50] * own).astype(LOW))[1:16, :]
    in_bias[...] = mm(rows, (taps[:, 50:51] * own).astype(LOW))


VMEM_SPEC = pl.BlockSpec(memory_space=pltpu.VMEM)


def unpack_small(full, final):
    vector = lambda rows: struct((rows, 16), FULL)
    return call(
        unpack_body,
        (struct((32, 64), FULL), struct((64, 128), FULL), struct((128, 256), FULL), struct((240, 49), FULL))
        + (struct((128, 512), FULL), struct((256, 512), FULL))
        + (vector(2), vector(4))
        + (vector(8),) * 7
        + (struct((16, 32), FULL), vector(16), vector(15), vector(8), vector(8)),
        in_specs=[VMEM_SPEC] * 2,
        scratch_shapes=[pltpu.VMEM((2 * C_ROWS, 128), LOW), pltpu.VMEM((E_ROWS, 128), LOW)],
    )(full, final)


def widen_body(values, out_e, out_r):
    size = 4096 // values.shape[0]
    for piece in range(values.shape[0]):
        for first in range(piece * size, (piece + 1) * size, min(size, 512)):
            part, rest = first // 1024, first % 1024
            out = (out_e, out_r)[rest // 512]
            rows = slice(rest % 512, rest % 512 + min(size, 512))
            here = slice(first - piece * size, first - piece * size + min(size, 512))
            out[rows, part * 128 : part * 128 + 128] = values[piece, here, :].astype(FULL)


def widen(values):
    return call(widen_body, (struct((512, 512), FULL),) * 2)(values)


def swap(values, pairs):
    return lax.ppermute(values, "dp", pairs)


def exchange(blocks):
    return (
        blocks[0],
        swap(blocks[1], CORE_SWAP),
        swap(blocks[2], CHIP_SWAP),
        swap(blocks[3], BOTH_SWAP),
    )


def exchange_far(own, near, far):
    across = swap(far, CHIP_SWAP)
    return [own, swap(near, CORE_SWAP), across, swap(across, CORE_SWAP)]


def gather(values):
    across = swap(values, CHIP_SWAP)
    return (values, swap(values, CORE_SWAP), across, swap(across, CORE_SWAP))


def hold(*values):
    return lax.optimization_barrier(values)


def onward(keeps, gots):
    parts = [(k[1].astype(FULL) + g[1].astype(FULL)).astype(LOW) for k, g in zip(keeps, gots)]
    return parts[0] if len(parts) == 1 else jnp.concatenate(parts, axis=0)


def own(keeps, gots, other):
    parts, row = [], 0
    for k, g in zip(keeps, gots):
        value = k[0].astype(FULL) + g[0].astype(FULL) + other[row : row + k.shape[1]].astype(FULL)
        parts.append(value.astype(LOW))
        row += k.shape[1]
    return parts[0] if len(parts) == 1 else jnp.concatenate(parts, axis=0)


def split(values, count):
    return values.reshape(count, -1, values.shape[-1])


def trade(parts):
    return lax.all_to_all(parts, "mp", split_axis=0, concat_axis=0, tiled=True)


def spread_sum(parts):
    value = jnp.sum(parts.astype(FULL), axis=0).astype(LOW)
    return jnp.broadcast_to(value[None], parts.shape)


def flat(parts):
    return parts.reshape(-1, parts.shape[2])


def per_device(
    mp_count,
    block_input,
    norm1_gain,
    norm1_bias,
    input_weight,
    input_bias,
    conv_weight,
    conv_bias,
    gate_weight1,
    gate_bias1,
    gate_weight2,
    gate_bias2,
    gate_weight3,
    gate_bias3,
    output_weight,
    output_bias,
    layer_scale1,
    norm2_gain,
    norm2_bias,
    expand_weight,
    expand_bias,
    reduce_weight,
    reduce_bias,
    layer_scale2,
    cotangent,
):
    me = lax.axis_index("dp").astype(jnp.int32).reshape(1)

    def turned(weight):
        return jnp.transpose(weight, (1, 2, 0)).reshape(-1, weight.shape[0])

    where = lax.axis_index("mp").astype(jnp.int32).reshape(1)
    late_weights = turned(expand_weight), reduce_weight.reshape(-1, WIDTH)
    small, far_small, *x_blocks = first_kernel(
        me,
        where,
        mp_count,
        block_input.reshape(SHARD, -1),
        *late_weights,
        (
            turned(output_weight),
            turned(gate_weight3),
            turned(gate_weight2),
            turned(gate_weight1),
            turned(conv_weight),
            norm1_gain,
            norm1_bias,
            input_bias,
            conv_bias,
            gate_bias1,
            gate_bias2,
            gate_bias3,
            output_bias,
            layer_scale1,
            norm2_gain,
            norm2_bias,
            reduce_bias,
            layer_scale2,
            expand_bias.T,
        ),
    )
    in_weight = turned(input_weight)
    in_across = swap(in_weight, CHIP_SWAP)
    small, far_small, x_blocks, in_across = hold(small, far_small, x_blocks, in_across)
    small_across = swap(far_small, CHIP_SWAP)
    x_blocks = exchange(x_blocks)
    own_dy, near, far = second_kernel(me, cotangent.reshape(SHARD, -1), *late_weights)
    small_across, near, far, in_weight, in_across = hold(small_across, near, far, in_weight, in_across)
    slabs = (small, swap(small, CORE_SWAP), small_across, swap(small_across, CORE_SWAP))
    in_shards = (in_weight, swap(in_weight, CORE_SWAP), in_across, swap(in_across, CORE_SWAP))
    vec, expand, w1, w1_back, w2, w3, w_in, w_out, taps, perm = prepare(me, slabs, in_shards)
    piece = small_across[S_ROWS:]
    vec, near, far, piece = hold(vec, near, far, piece)
    late_across = trade(jnp.broadcast_to(piece[None], (mp_count,) + piece.shape))
    x_blocks, near, far, vec = hold(x_blocks, near, far, vec)
    core, across = swap(near, CORE_SWAP), swap(far, CHIP_SWAP)
    x, z1, u, dwv = front(x_blocks, perm, vec, w_in, taps)
    dwv, core, across, late_across = hold(dwv, core, across, flat(late_across))
    passed, late_passed = swap(across, CORE_SWAP), swap(late_across, CORE_SWAP)
    z2 = branch_forward(dwv, x, vec, w1, w2, w3, w_out)
    others = (near, core, late_across, late_passed, across, passed)
    dy, f, dz, bias_grads, sib_g, keep_g = feed_forward(z2, own_dy, others, perm, vec, expand)


    got_g = swap(sib_g, CORE_SWAP)
    on_g = onward([keep_g], [got_g])
    dz, on_g = hold(dz, on_g)
    other_g = swap(on_g, CHIP_SWAP)
    *outs, g, dx1, sib, keep_late = branch_backward(
        me, dwv, x, dy, f, dz, vec, w1, w1_back, w2, w3, w_out, perm, bias_grads
    )
    got_late = swap(sib, CORE_SWAP)
    g, other_g, outs, got_late = hold(g, other_g, outs, got_late)
    part_g = split(own([keep_g], [got_g], other_g), mp_count)
    on_late = onward([keep_late], [got_late])
    g, part_g, on_late = hold(g, part_g, on_late)
    part_g = trade(part_g)
    other_late = swap(on_late, CHIP_SWAP)
    outs = exchange_far(*outs)

    du1, sib, keep1 = conv_backward(me, g, u, taps, z1, 4)
    got1 = swap(sib, CORE_SWAP)
    du1, part_g, other_late = hold(du1, part_g, other_late)
    part_late = split(own([keep_late], [got_late], other_late), mp_count)
    mixed = jnp.concatenate([spread_sum(part_g), part_late], axis=1)
    g, mixed = hold(g, mixed)
    mixed = trade(mixed)

    du0, sib, keep0 = conv_backward(me, g, u, taps, z1, 0)
    got0 = swap(sib, CORE_SWAP)
    du0, got0, got1, outs = hold(du0, got0, got1, outs)
    on_c = onward([keep0, keep1], [got0, got1])
    du0, on_c = hold(du0, on_c)
    other_c = swap(on_c, CHIP_SWAP)

    *ins, e0, e1, e2, e3 = input_backward(me, (du0, du1), x, dx1, vec, w_in, perm)
    ins, other_c = hold(ins, other_c)
    ins = exchange_far(*ins)
    block_output = from_pixels(me, outs).reshape(block_input.shape)
    ends = exchange((e0, e1, e2, e3))
    ins[1], other_c, mixed = hold(ins[1], other_c, mixed)
    rows = part_g.shape[1]
    part_late = mixed[:, rows:]
    sum_e, sum_r = widen(mixed)
    part_c = split(own([keep0, keep1], [got0, got1], other_c), mp_count)
    mixed = trade(jnp.concatenate([spread_sum(part_late), part_c], axis=1))
    mixed, ins = hold(mixed, ins)
    rows = part_late.shape[1]
    part_c = mixed[:, rows:]
    end = sum(e.astype(FULL) for e in ends).astype(LOW)
    end = jnp.broadcast_to(end[None], (mp_count,) + end.shape)
    full_c = trade(jnp.concatenate([spread_sum(part_c), end], axis=1))

    def back(values, blocks):
        return jnp.transpose(values.reshape(blocks, 16, values.shape[1]), (2, 0, 1))

    (
        g1, g2, g3, gconv, gout, gin, gb1, gb2, gb3, gob, gls1, gn2g, gn2b, grb, gls2, geb, ginb, gcb, gn1g, gn1b,
    ) = unpack_small(mixed, full_c)
    input_grad = from_pixels(me, ins).reshape(block_input.shape)
    return (
        block_output,
        input_grad,
        gn1g,
        gn1b,
        back(gin, 16),
        ginb,
        back(gconv, 15),
        gcb,
        back(g1, 2),
        gb1,
        back(g2, 4),
        gb2,
        back(g3, 8),
        gb3,
        back(gout, 8),
        gob,
        gls1,
        gn2g,
        gn2b,
        back(sum_e, 32),
        geb.T,
        sum_r.reshape(32, 16, WIDTH),
        grb,
        gls2,
    )


def solution(mesh):
    pixels = P(None, "dp", "mp")
    vector = P(None, "dp")
    matrix = P(None, None, "dp")
    params = (
        vector, vector, matrix, vector, matrix, vector, matrix, vector, matrix, vector, matrix, vector,
        matrix, vector, vector, vector, vector, matrix, vector, P(None, "dp", None), vector, vector,
    )
    return jax.shard_map(
        partial(per_device, mesh.shape["mp"]),
        mesh=mesh,
        in_specs=(pixels,) + params + (pixels,),
        out_specs=(pixels, pixels) + params,
        check_vma=False,
    )
```

```python
from functools import partial

import jax
import jax.numpy as jnp
from jax import lax
from jax.experimental import pallas as pl
from jax.experimental.pallas import tpu as pltpu
from jax.sharding import PartitionSpec as P

WIDTH = 512
GROUP = 64
SIDE = 14
CROP = SIDE * SIDE
CROPS = 8
TOKENS = CROP * CROPS
SHARD = 128
TAPS = 49
EPSILON = 1e-06
LOW = jnp.bfloat16
FULL = jnp.float32
VMEM = 58 * 1024 * 1024

NN = (((1,), (0,)), ((), ()))
NT = (((1,), (1,)), ((), ()))
TN = (((0,), (0,)), ((), ()))

CORE_SWAP = [(0, 1), (1, 0), (2, 3), (3, 2)]
CHIP_SWAP = [(0, 2), (2, 0), (1, 3), (3, 1)]
BOTH_SWAP = [(0, 3), (3, 0), (1, 2), (2, 1)]

S_GATE3, S_GATE2, S_GATE1, S_CONV, S_EXPAND, S_OUT, S_ROWS = 0, 256, 320, 352, 560, 592, 1104
S_LANE = 64
(V_N1G, V_N1B, V_INB, V_CB, V_GB1, V_GB2, V_GB3, V_OB, V_LS1, V_N2G, V_N2B, V_RB, V_LS2) = range(13)
VECTORS = 13
E_OUT, E_VEC, E_EXPAND, E_ROWS = 0, 352 + 512, 496 + 512, 640 + 512
E_GATE = 512


def mm(left, right, dims=NN):
    return lax.dot_general(left, right, dims, preferred_element_type=FULL)


def call(body, out, weight=1.0, **kwargs):
    flops, moved = int(weight * 1.15e9 / 4), 1 << 10
    return pl.pallas_call(
        body,
        out_shape=out,
        compiler_params=pltpu.CompilerParams(vmem_limit_bytes=VMEM),
        cost_estimate=pl.CostEstimate(flops=flops, bytes_accessed=moved, transcendentals=0),
        **kwargs,
    )


def struct(shape, dtype):
    return jax.ShapeDtypeStruct(shape, dtype)


SMEM_SPEC = pl.BlockSpec(memory_space=pltpu.SMEM)


def whole(shape):
    return pl.BlockSpec(shape, lambda i: (0,) * len(shape))


def turn_blocks(me, x_ref, outs, wide, blocks):
    lanes = x_ref.shape[1]
    for dest in range(4):
        for crop in range(CROPS):
            start = CROP * (CROPS * dest + crop)
            base = start // 128 * 128
            window = x_ref[:, base : base + min(lanes - base, 384)].astype(FULL)
            wide[pl.ds(crop, CROP, stride=CROPS), :] = window[:, start - base : start - base + CROP].T
        blocks[dest ^ me] = wide[...].astype(LOW)
    for k in range(4):
        outs[k][...] = blocks[k]


PIXEL_SCRATCH = [pltpu.VMEM((TOKENS, SHARD), FULL), pltpu.VMEM((4, TOKENS, SHARD), LOW)]


JOINT = TOKENS + 4 * 1024


def second_body(me_ref, x_ref, expand, reduce, own, near, far, wide, blocks):
    turn_blocks(me_ref[0], x_ref, (own, near.at[0:TOKENS], far.at[0], far.at[1]), wide, blocks)
    for part in range(4):
        lanes = slice(part * 128, part * 128 + 128)
        first = TOKENS + part * 1024
        near[first : first + 512, :] = expand[:, lanes]
        near[first + 512 : first + 1024, :] = reduce[:, lanes]


def second_kernel(me, x, expand, reduce):
    return call(
        second_body,
        (struct((TOKENS, SHARD), LOW), struct((JOINT, SHARD), LOW), struct(FAR, LOW)),
        weight=0.05,
        in_specs=[SMEM_SPEC] + [pl.BlockSpec(memory_space=pltpu.VMEM)] * 3,
        scratch_shapes=PIXEL_SCRATCH,
    )(me, x, expand, reduce)


def first_body(part, me_ref, part_ref, x_ref, expand, reduce, *refs):
    small, far = refs[19], refs[20]
    pack_body(*refs[:19], small, refs[25])
    far[0:S_ROWS, :] = small[...]
    size = 4096 // part
    for number in range(part):
        lanes, rest = number * size // 1024, number * size % 1024
        source = (expand, reduce)[rest // 512]

        @pl.when(part_ref[0] == number)
        def _():
            far[S_ROWS:, :] = source[rest % 512 : rest % 512 + size, lanes * 128 : lanes * 128 + 128]

    turn_blocks(me_ref[0], x_ref, refs[21:25], refs[26], refs[27])


def first_kernel(me, where, parts, x, expand, reduce, small):
    slab = (S_ROWS, 128)
    return call(
        partial(first_body, parts),
        (struct(slab, LOW), struct((S_ROWS + 4096 // parts, 128), LOW)) + (struct((TOKENS, SHARD), LOW),) * 4,
        weight=0.05,
        in_specs=[SMEM_SPEC] * 2 + [pl.BlockSpec(memory_space=pltpu.VMEM)] * 22,
        scratch_shapes=[pltpu.VMEM((S_OUT, 128), FULL)] + PIXEL_SCRATCH,
    )(me, where, x, expand, reduce, *small)


def from_pixels_body(me_ref, own, core, across, passed, out_ref, wide, blocks):
    me = me_ref[0]
    blocks[me] = own[...]
    blocks[1 ^ me] = core[...]
    blocks[2 ^ me] = across[0]
    blocks[3 ^ me] = passed[1]
    for source in range(4):
        wide[...] = blocks[source].astype(FULL)
        for crop in range(CROPS):
            start = CROP * (CROPS * source + crop)
            part = wide[pl.ds(crop, CROP, stride=CROPS), :].T
            out_ref[:, start : start + CROP] = part.astype(LOW)


def from_pixels(me, blocks):
    return call(
        from_pixels_body,
        struct((SHARD, 4 * TOKENS), LOW),
        weight=4.0,
        in_specs=[SMEM_SPEC] + [pl.BlockSpec(memory_space=pltpu.VMEM)] * 4,
        scratch_shapes=[pltpu.VMEM((TOKENS, SHARD), FULL), pltpu.VMEM((4, TOKENS, SHARD), LOW)],
    )(me, *blocks)


FAR = (2, TOKENS, SHARD)


def far_spec(tile):
    return pl.BlockSpec((2, tile, SHARD), lambda i: (0, i, 0))


def pack_body(out_weight, g3, g2, g1, conv, *refs):
    vectors, expand, out_ref, slab = refs[:VECTORS], refs[VECTORS], refs[VECTORS + 1], refs[VECTORS + 2]
    slab[...] = jnp.zeros_like(slab)
    slab[S_GATE3 : S_GATE3 + 128, :] = g3[:, :128].astype(FULL)
    slab[S_GATE3 + 128 : S_GATE3 + 256, :] = g3[:, 128:].astype(FULL)
    slab[S_GATE2 : S_GATE2 + 64, :] = g2[...].astype(FULL)
    slab[S_GATE1 : S_GATE1 + 32, :GROUP] = g1[...].astype(FULL)
    slab[S_CONV : S_CONV + 240, :TAPS] = conv[...].astype(FULL)
    for number, ref in enumerate(vectors):
        first = S_CONV + 16 * number + (1 if number == V_CB else 0)
        slab[first : first + ref.shape[0], S_LANE : S_LANE + 16] = ref[...].astype(FULL)
    slab[S_EXPAND : S_EXPAND + 32, S_LANE : S_LANE + 16] = expand[...].astype(FULL).T
    out_ref[0:S_OUT, :] = slab[...].astype(LOW)
    for part in range(4):
        rows = slice(S_OUT + part * 128, S_OUT + part * 128 + 128)
        out_ref[rows, :] = out_weight[:, part * 128 : part * 128 + 128]


TILE_OF = (2, 0, 3, 1)


def iota(shape, dim):
    return lax.broadcasted_iota(jnp.int32, shape, dim)


def spread(lanes):
    return jnp.where(iota((128, lanes), 1) % 16 + S_LANE == iota((128, lanes), 0), 1.0, 0.0).astype(LOW)


def prepare_body(me_ref, *refs):
    slabs, ins = refs[0:4], refs[4:8]
    vec, expand, w1, w1_back, w2, w3, w_in, w_out, taps, perm, channels = refs[8:]
    me = me_ref[0]
    totals = jnp.zeros((VECTORS, 1024), FULL)
    spread_wide = spread(1024)
    row = iota((VECTORS * 16, 1024), 0) % 16
    lane = iota((VECTORS * 16, 1024), 1)
    in_row = row == lane // 64
    spread_expand = spread(512)
    expand_rows = iota((32, 512), 0) == iota((32, 512), 1) // 16
    w1[...] = jnp.zeros_like(w1)
    channels[0:GROUP, :] = jnp.where(iota((GROUP, 128), 1) == TAPS // 2, 3.0, 0.0)
    for k in range(4):
        source = me ^ k
        slab = slabs[k]
        values = mm(slab[S_CONV : S_CONV + VECTORS * 16, :], spread_wide)
        values = jnp.where(in_row & (lane // 16 % 4 == source), values, 0.0)
        totals = totals + jnp.sum(values.reshape(VECTORS, 16, 1024), axis=1)
        values = mm(slab[S_EXPAND : S_EXPAND + 32, :], spread_expand)
        values = jnp.sum(jnp.where(expand_rows, values, 0.0), axis=0, keepdims=True)
        slot = TILE_OF[k]
        expand[8 * slot : 8 * slot + 8, :] = jnp.broadcast_to(values, (8, 512))
        for a in range(16):
            place = pl.ds(pl.multiple_of(a * 64 + source * 16, 16), 16)
            rows = slice(a * 16, a * 16 + 16)
            w_in[place, :] = ins[k][rows, :]
            if a < 15:
                later = pl.ds(pl.multiple_of((a + 1) * 64 + source * 16, 16), 16)
                channels[later, :] = slab[S_CONV + a * 16 : S_CONV + a * 16 + 16, :].astype(FULL)
            if a < 8:
                for part in range(4):
                    first = S_OUT + part * 128 + a * 16
                    w_out[place, part * 128 : part * 128 + 128] = slab[first : first + 16, :]
                w3[place, 0:128] = slab[S_GATE3 + a * 16 : S_GATE3 + a * 16 + 16, :]
                w3[place, 128:256] = slab[S_GATE3 + 128 + a * 16 : S_GATE3 + 128 + a * 16 + 16, :]
            if a < 4:
                w2[place, :] = slab[S_GATE2 + a * 16 : S_GATE2 + a * 16 + 16, :]
            if a < 2:
                w1[place, :] = slab[S_GATE1 + a * 16 : S_GATE1 + a * 16 + 16, :]
        column = iota((SHARD, WIDTH), 0)
        target = column // 16 * 64 + source * 16 + column % 16
        perm[k * SHARD : (k + 1) * SHARD, :] = jnp.where(iota((SHARD, WIDTH), 1) == target, 1.0, 0.0).astype(LOW)
    vec[0:VECTORS, :] = totals
    vec[VECTORS:16, :] = jnp.zeros((16 - VECTORS, 1024), FULL)
    single = w1[...].astype(FULL)
    w1_back[...] = (single + pltpu.roll(single, GROUP, 1)).astype(LOW)
    taps[...] = channels[...].T[0:64, :]


def prepare(me, slabs, ins):
    return call(
        prepare_body,
        (
            struct((16, 1024), FULL),
            struct((32, 512), FULL),
            struct((128, 128), LOW),
            struct((128, 128), LOW),
            struct((256, 128), LOW),
            struct((512, 256), LOW),
            struct((1024, 512), LOW),
            struct((512, 512), LOW),
            struct((64, 1024), FULL),
            struct((512, 512), LOW),
        ),
        weight=0.05,
        in_specs=[SMEM_SPEC] + [pl.BlockSpec(memory_space=pltpu.VMEM)] * 8,
        scratch_shapes=[pltpu.VMEM((1024, 128), FULL)],
    )(me, *slabs, *ins)


def normed(values):
    center = jnp.sum(values, axis=1, keepdims=True) * (1.0 / WIDTH)
    away = values - center
    spread_sq = jnp.sum(away * away, axis=1, keepdims=True) * (1.0 / WIDTH)
    inverse = lax.rsqrt(spread_sq + EPSILON)
    return away * inverse, inverse


def norm_back(grad, unit, inverse, gain):
    grad_unit = grad * gain
    first = jnp.sum(grad_unit, axis=1, keepdims=True) * (1.0 / WIDTH)
    second = jnp.sum(grad_unit * unit, axis=1, keepdims=True) * (1.0 / WIDTH)
    return inverse * (grad_unit - first - unit * second)


def total(values):
    return jnp.sum(values, axis=0, keepdims=True)


def row(vec, number, lanes=WIDTH):
    return vec[number : number + 1, 0:lanes]


def rows_spec(tile, lanes):
    return pl.BlockSpec((tile, lanes), lambda i: (i, 0))


def chunks(count, size, body):
    def step(i, carry):
        body(pl.ds(pl.multiple_of(i * size, size), size))
        return carry

    lax.fori_loop(0, count // size, step, 0)


NORM_ROWS = 224
HALVES = (slice(0, TOKENS // 2), slice(TOKENS // 2, TOKENS))


def stagger(chain, height, lead):
    cut = height // 32 * 16
    ahead, behind = chain(slice(0, cut)), chain(slice(cut, height))
    for _ in range(lead):
        next(ahead)
    for _ in ahead:
        next(behind)
    for _ in behind:
        pass


def join(blocks, perm, rows):
    return mm(jnp.concatenate([r[rows, :] for r in blocks], axis=1), perm[...])


def conv_rows(source, weights, emit, flip):
    zero = jnp.zeros((CROPS, 128), FULL)

    def tap_row(i, r, sums):
        base = (i + r - 3) * SIDE
        values = [source[base + c] for c in range(SIDE)]
        first = (6 - r) * 7 if flip else r * 7
        taps = [weights[first + (6 - s if flip else s)] for s in range(7)]
        for s in range(7):
            for c in range(SIDE):
                if 0 <= c + s - 3 < SIDE:
                    sums[c] = sums[c] + taps[s] * values[c + s - 3]

    def one_row(i, first, last):
        sums = [zero] * SIDE
        for r in range(first, last):
            tap_row(i, r, sums)
        emit(i, sums)

    def inner_row(i, carry):
        one_row(i, 0, 7)
        return carry

    for i in range(3):
        one_row(i, 3 - i, 7)
    lax.fori_loop(3, SIDE - 3, inner_row, 0)
    for i in range(SIDE - 3, SIDE):
        one_row(i, 0, 17 - i)


def wide_taps(taps, weights):
    for tap in range(TAPS):
        weights[tap] = jnp.broadcast_to(taps[tap : tap + 1, :], (CROPS, 128))


PIXEL_BLOCK = pl.BlockSpec((CROP, CROPS, 128), lambda i: (0, 0, i))


def lane_block(rows):
    return pl.BlockSpec((rows, 128), lambda i: (0, i))


def front_body(r0, r1, r2, r3, perm, vec, w_in, taps, vec_part, x, z, u, dwv, weights):
    @pl.when(pl.program_id(0) == 0)
    def _():
        for rows in HALVES:
            x[rows, :] = join((r0, r1, r2, r3), perm, rows).astype(LOW)

        def norm_rows(rows):
            unit, _ = normed(x[rows, :].astype(FULL))
            z[rows, :] = (unit * row(vec, V_N1G) + row(vec, V_N1B)).astype(LOW)

        chunks(TOKENS, NORM_ROWS, norm_rows)

    wide_taps(taps, weights)
    values = mm(z[...], w_in[...], NT) + vec_part[V_INB : V_INB + 1, :]
    u[...] = values.reshape(CROP, CROPS, 128)
    bias = jnp.broadcast_to(vec_part[V_CB : V_CB + 1, :], (CROPS, 128))

    def emit(i, sums):
        for c in range(SIDE):
            dwv[i * SIDE + c] = (sums[c] + bias) * (1.0 / 3.0)

    conv_rows(u, weights, emit, False)


def front(blocks, perm, vec, w_in, taps):
    pixels = struct((CROP, CROPS, 1024), FULL)
    rows = struct((TOKENS, WIDTH), LOW)
    x, z, u, dwv = call(
        front_body,
        (rows, rows, pixels, pixels),
        weight=28.0,
        grid=(8,),
        in_specs=[whole((TOKENS, SHARD))] * 4
        + [
            whole((512, 512)),
            whole((16, 1024)),
            pl.BlockSpec((128, 512), lambda i: (i, 0)),
            lane_block(64),
            lane_block(16),
        ],
        out_specs=(whole((TOKENS, WIDTH)), whole((TOKENS, WIDTH)), PIXEL_BLOCK, PIXEL_BLOCK),
        scratch_shapes=[pltpu.VMEM((TAPS, CROPS, 128), FULL)],
    )(*blocks, perm, vec, w_in, taps, vec)
    return x, z, u, dwv.reshape(TOKENS, 1024)


def branch_body(dwv, x, vec, w1, w2, w3, w_out, z_out):
    def chain(rows):
        first = dwv[rows, 0:128]
        q = (first * pltpu.roll(first, GROUP, 1)).astype(LOW)
        yield
        t = mm(q, w1[...], NT) + row(vec, V_GB1, 128)
        q = (t * dwv[rows, 128:256]).astype(LOW)
        yield
        t = mm(q, w2[...], NT) + row(vec, V_GB2, 256)
        q = (t * dwv[rows, 256:512]).astype(LOW)
        yield
        t = mm(q, w3[...], NT) + row(vec, V_GB3, 512)
        q = (t * dwv[rows, 512:1024]).astype(LOW)
        yield
        branch = mm(q, w_out[...], NT) + row(vec, V_OB)
        middle = x[rows, :].astype(FULL) + row(vec, V_LS1) * branch
        yield
        unit, _ = normed(middle)
        z_out[rows, :] = (unit * row(vec, V_N2G) + row(vec, V_N2B)).astype(LOW)
        yield

    stagger(chain, dwv.shape[0], 2)


def branch_forward(dwv, x, vec, w1, w2, w3, w_out, tile=784):
    return call(
        branch_body,
        struct((TOKENS, WIDTH), LOW),
        weight=7.0,
        grid=(TOKENS // tile,),
        in_specs=[
            rows_spec(tile, 1024),
            rows_spec(tile, WIDTH),
            whole((16, 1024)),
            whole((128, 128)),
            whole((256, 128)),
            whole((512, 256)),
            whole((512, 512)),
        ],
        out_specs=rows_spec(tile, WIDTH),
    )(dwv, x, vec, w1, w2, w3, w_out)


def gelu_parts(s):
    bell = jnp.exp2((-0.5 * 1.4426950408889634) * (s * s))
    size = jnp.abs(s)
    t = pltpu.reciprocal(1.0 + (0.3275911 * 0.7071067811865476) * size, approx=True)
    poly = 0.5 * 1.061405429
    for coefficient in (-1.453152027, 1.421413741, -0.284496736, 0.254829592):
        poly = poly * t + 0.5 * coefficient
    tail = poly * t * bell
    cdf = jnp.where(s >= 0.0, 1.0 - tail, tail)
    return s * cdf, cdf + s * (bell * 0.3989422804014327)


PIECE = 16


def mlp_body(z, r0, perm, vec, expand, c0, c1, w2, w3, y2, y3, *refs):
    dy_out, f_out, dz_out, gb, sibling, keep = refs[0:6]
    dy, f, dz, r1, r2, r3, we, wr, df, s0, s1, g0, g1, hid, grad_s, grads, sums, sems = refs[6:]
    pre, grad_h = (s0, s1), (g0, g1)
    half = TOKENS // 2
    shards = ((c1, TOKENS), (w3, 0), (c0, TOKENS), (w2, 0))

    def copies(slot):
        for part in range(4):
            for number, matrix in enumerate((we, wr)):
                shard, first = shards[slot]
                rows = pl.ds(first + part * 1024 + number * 512, 512)
                yield pltpu.make_async_copy(
                    shard.at[rows], matrix.at[slot, :, pl.ds(part * 128, 128)], sems.at[slot]
                )

    near = [
        pltpu.make_async_copy(block, r, sems.at[4 + number])
        for number, (block, r) in enumerate(((c1.at[pl.ds(0, TOKENS)], r1), (y2.at[0], r2), (y3.at[1], r3)))
    ]
    for copy in near:
        copy.start()
    for slot in range(4):
        for copy in copies(slot):
            copy.start()

    def arrived(slot):
        for matrix in (we, wr):
            pltpu.make_async_copy(matrix.at[slot], matrix.at[slot], sems.at[slot]).wait()

    def leave(tile):
        out = (sibling, keep)[tile // 2]
        return [
            pltpu.make_async_copy(
                grads.at[tile, :, pl.ds(part * 128, 128)],
                out.at[tile % 2, pl.ds(part * 1024, 1024)],
                sems.at[7 + tile],
            )
            for part in range(4)
        ]

    def start(copies):
        for copy in copies:
            copy.start()

    for copy in near:
        copy.wait()
    for rows in HALVES:
        dy[rows, :] = join((r0, r1, r2, r3), perm, rows).astype(LOW)
    dy_leaves = pltpu.make_async_copy(dy, dy_out, sems.at[11])
    dy_leaves.start()

    def scaled(rows):
        df[rows, :] = (dy[rows, :].astype(FULL) * row(vec, V_LS2)).astype(LOW)
        f[rows, :] = jnp.zeros((112, WIDTH), FULL)
        dz[rows, :] = jnp.zeros((112, WIDTH), FULL)

    chunks(TOKENS, 112, scaled)
    sums[...] = jnp.zeros_like(sums)
    hid[1, HALVES[1], :] = jnp.zeros((half, 512), LOW)
    grad_s[1, HALVES[1], :] = jnp.zeros((half, 512), LOW)
    arrived(0)
    s0[...] = mm(z[HALVES[0], :], we[0], NT)
    g0[...] = mm(df[HALVES[0], :], wr[0], NT)
    pieces = half // PIECE

    def unit(here, tile, before, after):
        there = 1 - here
        rows = HALVES[there]
        now, last = tile & 1, (tile & 1) ^ 1
        ready = last if here == 0 else now
        bias = expand[pl.ds(pl.multiple_of(tile * 8, 8), 1), :]
        done = [0]
        column = [jnp.zeros((8, 512), FULL)]

        def some(part):
            while done[0] < pieces * part // 6:
                first = done[0] * PIECE
                piece = slice(first, first + PIECE)
                place = slice(here * half + first, here * half + first + PIECE)
                act, slope = gelu_parts(pre[here][piece, :] + bias)
                hid[now, place, :] = act.astype(LOW)
                grad = (grad_h[here][piece, :] * slope).astype(LOW)
                grad_s[now, place, :] = grad
                grad = grad.astype(FULL)
                column[0] = column[0] + (grad[0:8] + grad[8:16])
                done[0] += 1

        if here == 0:
            grads[before, 0:512, :] = mm(grad_s[last], z[...], TN).astype(LOW)
        else:
            grads[before, 512:1024, :] = mm(hid[last], df[...], TN).astype(LOW)
        some(2)
        pre[there][...] = mm(z[rows, :], we[after], NT)
        some(3)
        grad_h[there][...] = mm(df[rows, :], wr[after], NT)
        some(4)
        f[rows, :] += mm(hid[ready, rows, :], wr[before if here == 0 else tile])
        some(5)
        dz[rows, :] += mm(grad_s[ready, rows, :], we[before if here == 0 else tile])
        some(6)
        sums[tile] += column[0]

    def one_tile(tile, carry):
        before = jnp.maximum(tile - 1, 0)
        for number in range(2):

            @pl.when(tile == number + 2)
            def _():
                start(leave(number))

        unit(0, tile, before, tile)

        @pl.when(tile < 3)
        def _():
            arrived(tile + 1)

        unit(1, tile, before, jnp.minimum(tile + 1, 3))
        return carry

    lax.fori_loop(0, 4, one_tile, 0)
    start(leave(2))

    def results(number):
        rows = pl.ds(number * half, half)
        return [
            pltpu.make_async_copy(value.at[rows], out.at[rows], sems.at[12 + number])
            for value, out in ((f, f_out), (dz, dz_out))
        ]

    start(results(0))
    rows = HALVES[1]
    f[rows, :] += mm(hid[1, rows, :], wr[3])
    dz[rows, :] += mm(grad_s[1, rows, :], we[3])
    start(results(1))
    grads[3, 0:512, :] = mm(grad_s[1], z[...], TN).astype(LOW)
    grads[3, 512:1024, :] = mm(hid[1], df[...], TN).astype(LOW)
    start(leave(3))
    for tile in range(4):
        gb[8 * tile : 8 * tile + 8, :] = sums[tile]
    dy_leaves.wait()
    for copies in [results(0), results(1)] + [leave(tile) for tile in range(4)]:
        for copy in copies:
            copy.wait()


def feed_forward(z, own_dy, others, perm, vec, expand):
    vmem = pl.BlockSpec(memory_space=pltpu.VMEM)
    anywhere = pl.BlockSpec(memory_space=pl.ANY)
    half = TOKENS // 2
    pair = struct((2, 4096, 128), LOW)
    rows = struct((TOKENS, WIDTH), FULL)
    return call(
        mlp_body,
        (struct((TOKENS, WIDTH), LOW), rows, rows, struct((32, 512), FULL), pair, pair),
        weight=40.0,
        in_specs=[vmem] * 5 + [anywhere] * 6,
        out_specs=(anywhere,) * 3 + (vmem,) + (anywhere,) * 2,
        scratch_shapes=[pltpu.VMEM((TOKENS, WIDTH), LOW)]
        + [pltpu.VMEM((TOKENS, WIDTH), FULL)] * 2
        + [pltpu.VMEM((TOKENS, SHARD), LOW)] * 3
        + [pltpu.VMEM((4, 512, 512), LOW)] * 2
        + [pltpu.VMEM((TOKENS, WIDTH), LOW)]
        + [pltpu.VMEM((half, 512), FULL)] * 4
        + [pltpu.VMEM((2, TOKENS, 512), LOW)] * 2
        + [pltpu.VMEM((4, 1024, 512), LOW)]
        + [pltpu.VMEM((4, 8, 512), FULL)]
        + [pltpu.SemaphoreType.DMA((14,))],
    )(z, own_dy, perm, vec, expand, *others)


def pack_vectors(values, count, source):
    lane = iota((count * 16, 1024), 1)
    keep = (iota((count * 16, 1024), 0) % 16 == lane // 64) & (lane // 16 % 4 == source)
    tall = jnp.broadcast_to(values[:, None, :], (count, 16, 1024)).reshape(count * 16, 1024)
    gather = jnp.where(iota((1024, 128), 0) % 16 == iota((1024, 128), 1), 1.0, 0.0).astype(LOW)
    return mm(jnp.where(keep, tall, 0.0).astype(LOW), gather)


def part_pair(parts, sibling, keep):
    sibling[0] = parts[1]
    sibling[1] = parts[3]
    keep[0] = parts[0]
    keep[1] = parts[2]


def branch_back_body(steps, me_ref, dwv, x, dy, f, dz, vec, w1, w1_back, w2, w3, w_out, perm, gb, *refs):
    (o0, o1, far, g_out, dx_out, sibling, keep) = refs[0:7]
    acc_o, acc_3, acc_2, acc_1, sums, parts = refs[7:]
    step = pl.program_id(0)

    @pl.when(step == 0)
    def _():
        acc_o[...] = jnp.zeros_like(acc_o)
        acc_3[...] = jnp.zeros_like(acc_3)
        acc_2[...] = jnp.zeros_like(acc_2)
        acc_1[...] = jnp.zeros_like(acc_1)
        sums[...] = jnp.zeros_like(sums)

    third = 1.0 / 3.0

    def chain(rows):
        first = dwv[rows, 0:128]
        turned = pltpu.roll(first, GROUP, 1)
        q0 = (first * turned).astype(LOW)
        yield
        t1 = mm(q0, w1[...], NT) + row(vec, V_GB1, 128)
        q1 = (t1 * dwv[rows, 128:256]).astype(LOW)
        yield
        t2 = mm(q1, w2[...], NT) + row(vec, V_GB2, 256)
        q2 = (t2 * dwv[rows, 256:512]).astype(LOW)
        yield
        t3 = mm(q2, w3[...], NT) + row(vec, V_GB3, 512)
        q3 = (t3 * dwv[rows, 512:1024]).astype(LOW)
        yield
        branch = mm(q3, w_out[...], NT) + row(vec, V_OB)
        middle = x[rows, :].astype(FULL) + row(vec, V_LS1) * branch
        yield
        unit, inverse = normed(middle)
        yield
        grad = dz[rows, :]
        top = dy[rows, :].astype(FULL)
        middle_grad = top + norm_back(grad, unit, inverse, row(vec, V_N2G))
        dx_out[rows, :] = middle_grad
        sums[4:5, 0:512] += total(middle_grad * branch)
        sums[5:6, 0:512] += total(grad * unit)
        sums[6:7, 0:512] += total(grad)
        grad_branch = (middle_grad * row(vec, V_LS1)).astype(LOW)
        yield
        back = mm(grad_branch, w_out[...])
        gt3 = (back * dwv[rows, 512:1024]).astype(LOW)
        g_out[rows, 512:1024] = back * t3 * third
        yield
        back = mm(gt3, w3[...])
        acc_o[...] += mm(grad_branch, q3, TN)
        sums[3:4, 0:512] += total(grad_branch.astype(FULL))
        gt2 = (back * dwv[rows, 256:512]).astype(LOW)
        g_out[rows, 256:512] = back * t2 * third
        yield
        back = mm(gt2, w2[...])
        acc_3[...] += mm(gt3, q2, TN)
        sums[2:3, 0:512] += total(gt3.astype(FULL))
        gt1 = (back * dwv[rows, 128:256]).astype(LOW)
        g_out[rows, 128:256] = back * t1 * third
        yield
        back = mm(gt1, w1_back[...])
        acc_2[...] += mm(gt2, q1, TN)
        acc_1[...] += mm(gt1, q0, TN)
        sums[1:2, 0:256] += total(gt2.astype(FULL))
        sums[0:1, 0:128] += total(gt1.astype(FULL))
        g_out[rows, 0:128] = back * turned * third
        yield
        mlp = f[rows, :] + row(vec, V_RB)
        output = (middle + row(vec, V_LS2) * mlp).astype(LOW)
        sums[7:8, 0:512] += total(top) * row(vec, V_LS2)
        sums[8:9, 0:512] += total(top * mlp)
        yield
        blocks = mm(output, perm[...], NT).astype(LOW)
        for k, ref in enumerate((o0, o1, far.at[0], far.at[1])):
            ref[rows, :] = blocks[:, k * SHARD : (k + 1) * SHARD]
        yield

    height = dwv.shape[0]
    stagger(chain, height, 3)

    @pl.when(step == steps - 1)
    def _():
        me = me_ref[0]
        vectors = sums[0:9, :]
        expand_rows = iota((32, 512), 0) == iota((32, 512), 1) // 16
        gather = jnp.where(iota((512, 128), 0) % 16 == iota((512, 128), 1), 1.0, 0.0).astype(LOW)
        for source in range(4):
            k = source ^ me
            for a in range(8):
                rows = slice(a * 64 + source * 16, a * 64 + source * 16 + 16)
                for part in range(4):
                    first = part * 128 + a * 16
                    parts[k, first : first + 16, :] = acc_o[rows, part * 128 : part * 128 + 128].astype(LOW)
                first = E_GATE + a * 16
                parts[k, first : first + 16, :] = acc_3[rows, 0:128].astype(LOW)
                parts[k, first + 128 : first + 144, :] = acc_3[rows, 128:256].astype(LOW)
                if a < 4:
                    parts[k, first + 256 : first + 272, :] = acc_2[rows, :].astype(LOW)
                if a < 2:
                    parts[k, first + 320 : first + 336, :] = acc_1[rows, :].astype(LOW)
            parts[k, E_VEC : E_VEC + 144, :] = pack_vectors(vectors, 9, source).astype(LOW)
        for k in range(4):
            slot = TILE_OF[k]
            line = total(gb[8 * slot : 8 * slot + 8, :])
            tall = jnp.where(expand_rows, jnp.broadcast_to(line, (32, 512)), 0.0)
            parts[k, E_EXPAND : E_EXPAND + 32, :] = mm(tall.astype(LOW), gather).astype(LOW)
            parts[k, E_EXPAND + 32 : E_ROWS, :] = jnp.zeros((E_ROWS - E_EXPAND - 32, 128), LOW)
        part_pair(parts, sibling, keep)


def branch_backward(me, dwv, x, dy, f, dz, vec, w1, w1_back, w2, w3, w_out, perm, biases, tile=784):
    steps = TOKENS // tile
    wide = rows_spec(tile, WIDTH)
    block = rows_spec(tile, SHARD)
    pair = (2, E_ROWS, 128)
    return call(
        partial(branch_back_body, steps),
        (struct((TOKENS, SHARD), LOW),) * 2
        + (
            struct(FAR, LOW),
            struct((TOKENS, 1024), FULL),
            struct((TOKENS, WIDTH), FULL),
            struct(pair, LOW),
            struct(pair, LOW),
        ),
        weight=20.0,
        grid=(steps,),
        in_specs=[
            SMEM_SPEC,
            rows_spec(tile, 1024),
            wide,
            wide,
            wide,
            wide,
            whole((16, 1024)),
            whole((128, 128)),
            whole((128, 128)),
            whole((256, 128)),
            whole((512, 256)),
            whole((512, 512)),
            whole((512, 512)),
        ]
        + [whole((32, 512))],
        out_specs=(block,) * 2 + (far_spec(tile), rows_spec(tile, 1024), wide, whole(pair), whole(pair)),
        scratch_shapes=[
            pltpu.VMEM((512, 512), FULL),
            pltpu.VMEM((512, 256), FULL),
            pltpu.VMEM((256, 128), FULL),
            pltpu.VMEM((128, 128), FULL),
            pltpu.VMEM((16, 1024), FULL),
            pltpu.VMEM((4, E_ROWS, 128), LOW),
        ],
    )(me, dwv, x, dy, f, dz, vec, w1, w1_back, w2, w3, w_out, perm, biases)


def conv_back_body(me_ref, g, u, taps, z_in, du, sibling, keep, weights, grad_taps, parts, z, sem):
    step, steps = pl.program_id(0), pl.num_programs(0)
    coming = pltpu.make_async_copy(z_in, z, sem.at[0])

    @pl.when(step == 0)
    def _():
        coming.start()

    me = me_ref[0]
    wide_taps(taps, weights)
    zero = jnp.zeros((CROPS, 128), FULL)

    def emit(i, sums):
        stacked = jnp.concatenate(list(sums), axis=0).astype(LOW)
        first = i * SIDE * CROPS if isinstance(i, int) else pl.multiple_of(i * SIDE * CROPS, 16)
        du[pl.ds(first, SIDE * CROPS), :] = stacked

    conv_rows(g, weights, emit, True)

    for r in range(7):

        def one_row(i, sums):
            grads = [g[i * SIDE + c] for c in range(SIDE)]
            values = [u[(i + r - 3) * SIDE + c] for c in range(SIDE)]
            sums = list(sums)
            for c in range(SIDE):
                for s in range(7):
                    if 0 <= c + s - 3 < SIDE:
                        sums[s] = sums[s] + grads[c] * values[c + s - 3]
            return tuple(sums)

        sums = lax.fori_loop(max(0, 3 - r), min(SIDE, SIDE + 3 - r), one_row, (zero,) * 7)
        for s in range(7):
            grad_taps[r * 7 + s : r * 7 + s + 1, :] = total(sums[s])
    grad_taps[49:50, :] = total(jnp.sum(g[...], axis=0))
    grad_taps[50:51, :] = total(du[...].astype(FULL))
    grad_taps[51:128, :] = jnp.zeros((77, 128), FULL)

    @pl.when(step == 0)
    def _():
        coming.wait()

    grad_w = mm(du[...], z[...], TN).astype(LOW)
    tall = grad_taps[...].T.astype(LOW)
    for a in range(2):
        for source in range(4):
            k = source ^ me
            rows = slice(a * 64 + source * 16, a * 64 + source * 16 + 16)
            for part in range(4):
                place = pl.ds(pl.multiple_of(part * 128 + step * 32 + a * 16, 16), 16)
                parts[k, place, :] = grad_w[rows, part * 128 : part * 128 + 128]
            place = pl.ds(pl.multiple_of(512 + step * 32 + a * 16, 16), 16)
            parts[k, place, :] = tall[rows, :]

    @pl.when(step == steps - 1)
    def _():
        part_pair(parts, sibling, keep)


C_ROWS = 640


def conv_backward(me, g, u, taps, z, base):
    pixels = pl.BlockSpec((CROP, CROPS, 128), lambda i: (0, 0, i + base))
    pair = (2, C_ROWS, 128)
    return call(
        conv_back_body,
        (struct((TOKENS, 512), LOW), struct(pair, LOW), struct(pair, LOW)),
        weight=24.0,
        grid=(4,),
        in_specs=[
            SMEM_SPEC,
            pixels,
            pixels,
            pl.BlockSpec((64, 128), lambda i: (0, i + base)),
            pl.BlockSpec(memory_space=pl.ANY),
        ],
        out_specs=(lane_block(TOKENS), whole(pair), whole(pair)),
        scratch_shapes=[
            pltpu.VMEM((TAPS, CROPS, 128), FULL),
            pltpu.VMEM((128, 128), FULL),
            pltpu.VMEM((4, C_ROWS, 128), LOW),
            pltpu.VMEM((TOKENS, WIDTH), LOW),
            pltpu.SemaphoreType.DMA((1,)),
        ],
    )(me, g.reshape(CROP, CROPS, 1024), u, taps, z)


def input_back_body(steps, me_ref, du0, du1, x, dx, vec, w_in, perm, *refs):
    (o0, o1, far, e0, e1, e2, e3, sums, parts) = refs
    step = pl.program_id(0)

    @pl.when(step == 0)
    def _():
        sums[...] = jnp.zeros_like(sums)

    def chain(rows):
        grad = mm(jnp.concatenate([du0[rows, :], du1[rows, :]], axis=1), w_in[...])
        yield
        unit, inverse = normed(x[rows, :].astype(FULL))
        sums[0:1, 0:512] += total(grad * unit)
        sums[1:2, 0:512] += total(grad)
        yield
        grad_x = (dx[rows, :] + norm_back(grad, unit, inverse, row(vec, V_N1G))).astype(LOW)
        yield
        blocks = mm(grad_x, perm[...], NT).astype(LOW)
        for k, ref in enumerate((o0, o1, far.at[0], far.at[1])):
            ref[rows, :] = blocks[:, k * SHARD : (k + 1) * SHARD]
        yield

    stagger(chain, x.shape[0], 1)

    @pl.when(step == steps - 1)
    def _():
        me = me_ref[0]
        vectors = sums[0:2, :]
        for source in range(4):
            parts[source ^ me, :, :] = pack_vectors(vectors, 2, source).astype(LOW)
        for k, ref in enumerate((e0, e1, e2, e3)):
            ref[...] = parts[k]


def input_backward(me, dus, x, dx, vec, w_in, perm, tile=784):
    steps = TOKENS // tile
    wide = rows_spec(tile, WIDTH)
    end = (32, 128)
    return call(
        partial(input_back_body, steps),
        (struct((TOKENS, SHARD), LOW),) * 2 + (struct(FAR, LOW),) + (struct(end, LOW),) * 4,
        weight=8.0,
        grid=(steps,),
        in_specs=[
            SMEM_SPEC,
            *[rows_spec(tile, 512)] * 2,
            wide,
            wide,
            whole((16, 1024)),
            whole((1024, 512)),
            whole((512, 512)),
        ],
        out_specs=(rows_spec(tile, SHARD),) * 2 + (far_spec(tile),) + (whole(end),) * 4,
        scratch_shapes=[pltpu.VMEM((16, 1024), FULL), pltpu.VMEM((4, 32, 128), LOW)],
    )(me, *dus, x, dx, vec, w_in, perm)


def unpack_body(middle, final, *refs):
    (g1, g2, g3, conv, w_out, w_in), late_refs, expand = refs[0:6], refs[6:15], refs[15]
    (in_bias, conv_bias, gain, bias), low, full = refs[16:20], refs[20], refs[21]
    size = E_ROWS // middle.shape[0]
    for piece in range(middle.shape[0]):
        full[piece * size : (piece + 1) * size, :] = middle[piece, 0:size, :]
    size = final.shape[1] - 32
    last = jnp.zeros((32, 128), FULL)
    for piece in range(final.shape[0]):
        low[piece * size : (piece + 1) * size, :] = final[piece, 0:size, :]
        last = last + final[piece, size : size + 32, :].astype(FULL)
    gates = full[E_GATE:E_VEC, :].astype(FULL)
    g3[:, 0:128] = gates[0:128]
    g3[:, 128:256] = gates[128:256]
    g2[...] = gates[256:320]
    g1[...] = gates[320:352, 0:GROUP]
    taps = []
    for j, (source, first) in enumerate(((low, 0), (low, C_ROWS))):
        for part in range(4):
            rows = slice(first + part * 128, first + part * 128 + 128)
            w_in[j * 128 : j * 128 + 128, part * 128 : part * 128 + 128] = source[rows, :].astype(FULL)
        taps.append(source[first + 512 : first + 640, :])
    for part in range(4):
        lanes = slice(part * 128, part * 128 + 128)
        w_out[:, lanes] = full[lanes, :].astype(FULL)
    taps = jnp.concatenate(taps, axis=0).astype(FULL)
    conv[...] = taps[16:256, 0:TAPS]
    vectors = full[E_VEC : E_VEC + 144, :].astype(FULL)
    for number, ref in enumerate(late_refs):
        ref[...] = vectors[16 * number : 16 * number + ref.shape[0], 0:16]
    expand[...] = full[E_EXPAND : E_EXPAND + 32, 0:16].astype(FULL).T
    gain[...] = last[0:8, 0:16]
    bias[...] = last[16:24, 0:16]
    own = jnp.where(iota((256, 16), 0) % 16 == iota((256, 16), 1), 1.0, 0.0)
    rows = jnp.where(iota((16, 256), 0) == iota((16, 256), 1) // 16, 1.0, 0.0).astype(LOW)
    conv_bias[...] = mm(rows, (taps[:, 49:50] * own).astype(LOW))[1:16, :]
    in_bias[...] = mm(rows, (taps[:, 50:51] * own).astype(LOW))


VMEM_SPEC = pl.BlockSpec(memory_space=pltpu.VMEM)


def unpack_small(full, final):
    vector = lambda rows: struct((rows, 16), FULL)
    return call(
        unpack_body,
        (struct((32, 64), FULL), struct((64, 128), FULL), struct((128, 256), FULL), struct((240, 49), FULL))
        + (struct((128, 512), FULL), struct((256, 512), FULL))
        + (vector(2), vector(4))
        + (vector(8),) * 7
        + (struct((16, 32), FULL), vector(16), vector(15), vector(8), vector(8)),
        in_specs=[VMEM_SPEC] * 2,
        scratch_shapes=[pltpu.VMEM((2 * C_ROWS, 128), LOW), pltpu.VMEM((E_ROWS, 128), LOW)],
    )(full, final)


def widen_body(values, out_e, out_r):
    size = 4096 // values.shape[0]
    for piece in range(values.shape[0]):
        for first in range(piece * size, (piece + 1) * size, min(size, 512)):
            part, rest = first // 1024, first % 1024
            out = (out_e, out_r)[rest // 512]
            rows = slice(rest % 512, rest % 512 + min(size, 512))
            here = slice(first - piece * size, first - piece * size + min(size, 512))
            out[rows, part * 128 : part * 128 + 128] = values[piece, here, :].astype(FULL)


def widen(values):
    return call(widen_body, (struct((512, 512), FULL),) * 2)(values)


def swap(values, pairs):
    return lax.ppermute(values, "dp", pairs)


def exchange(blocks):
    return (
        blocks[0],
        swap(blocks[1], CORE_SWAP),
        swap(blocks[2], CHIP_SWAP),
        swap(blocks[3], BOTH_SWAP),
    )


def exchange_far(own, near, far):
    across = swap(far, CHIP_SWAP)
    return [own, swap(near, CORE_SWAP), across, swap(across, CORE_SWAP)]


def gather(values):
    across = swap(values, CHIP_SWAP)
    return (values, swap(values, CORE_SWAP), across, swap(across, CORE_SWAP))


def hold(*values):
    return lax.optimization_barrier(values)


def onward(keeps, gots):
    parts = [(k[1].astype(FULL) + g[1].astype(FULL)).astype(LOW) for k, g in zip(keeps, gots)]
    return parts[0] if len(parts) == 1 else jnp.concatenate(parts, axis=0)


def own(keeps, gots, other):
    parts, row = [], 0
    for k, g in zip(keeps, gots):
        value = k[0].astype(FULL) + g[0].astype(FULL) + other[row : row + k.shape[1]].astype(FULL)
        parts.append(value.astype(LOW))
        row += k.shape[1]
    return parts[0] if len(parts) == 1 else jnp.concatenate(parts, axis=0)


def split(values, count):
    return values.reshape(count, -1, values.shape[-1])


def trade(parts):
    return lax.all_to_all(parts, "mp", split_axis=0, concat_axis=0, tiled=True)


def spread_sum(parts):
    value = jnp.sum(parts.astype(FULL), axis=0).astype(LOW)
    return jnp.broadcast_to(value[None], parts.shape)


def flat(parts):
    return parts.reshape(-1, parts.shape[2])


def per_device(
    mp_count,
    block_input,
    norm1_gain,
    norm1_bias,
    input_weight,
    input_bias,
    conv_weight,
    conv_bias,
    gate_weight1,
    gate_bias1,
    gate_weight2,
    gate_bias2,
    gate_weight3,
    gate_bias3,
    output_weight,
    output_bias,
    layer_scale1,
    norm2_gain,
    norm2_bias,
    expand_weight,
    expand_bias,
    reduce_weight,
    reduce_bias,
    layer_scale2,
    cotangent,
):
    me = lax.axis_index("dp").astype(jnp.int32).reshape(1)

    def turned(weight):
        return jnp.transpose(weight, (1, 2, 0)).reshape(-1, weight.shape[0])

    where = lax.axis_index("mp").astype(jnp.int32).reshape(1)
    late_weights = turned(expand_weight), reduce_weight.reshape(-1, WIDTH)
    small, far_small, *x_blocks = first_kernel(
        me,
        where,
        mp_count,
        block_input.reshape(SHARD, -1),
        *late_weights,
        (
            turned(output_weight),
            turned(gate_weight3),
            turned(gate_weight2),
            turned(gate_weight1),
            turned(conv_weight),
            norm1_gain,
            norm1_bias,
            input_bias,
            conv_bias,
            gate_bias1,
            gate_bias2,
            gate_bias3,
            output_bias,
            layer_scale1,
            norm2_gain,
            norm2_bias,
            reduce_bias,
            layer_scale2,
            expand_bias.T,
        ),
    )
    in_weight = turned(input_weight)
    in_across = swap(in_weight, CHIP_SWAP)
    small, far_small, x_blocks, in_across = hold(small, far_small, x_blocks, in_across)
    small_across = swap(far_small, CHIP_SWAP)
    x_blocks = exchange(x_blocks)
    own_dy, near, far = second_kernel(me, cotangent.reshape(SHARD, -1), *late_weights)
    small_across, near, far, in_weight, in_across = hold(small_across, near, far, in_weight, in_across)
    slabs = (small, swap(small, CORE_SWAP), small_across, swap(small_across, CORE_SWAP))
    in_shards = (in_weight, swap(in_weight, CORE_SWAP), in_across, swap(in_across, CORE_SWAP))
    vec, expand, w1, w1_back, w2, w3, w_in, w_out, taps, perm = prepare(me, slabs, in_shards)
    piece = small_across[S_ROWS:]
    vec, near, far, piece = hold(vec, near, far, piece)
    late_across = trade(jnp.broadcast_to(piece[None], (mp_count,) + piece.shape))
    x_blocks, near, far, vec = hold(x_blocks, near, far, vec)
    core, across = swap(near, CORE_SWAP), swap(far, CHIP_SWAP)
    x, z1, u, dwv = front(x_blocks, perm, vec, w_in, taps)
    dwv, core, across, late_across = hold(dwv, core, across, flat(late_across))
    passed, late_passed = swap(across, CORE_SWAP), swap(late_across, CORE_SWAP)
    z2 = branch_forward(dwv, x, vec, w1, w2, w3, w_out)
    others = (near, core, late_across, late_passed, across, passed)
    dy, f, dz, bias_grads, sib_g, keep_g = feed_forward(z2, own_dy, others, perm, vec, expand)


    got_g = swap(sib_g, CORE_SWAP)
    on_g = onward([keep_g], [got_g])
    dz, on_g = hold(dz, on_g)
    other_g = swap(on_g, CHIP_SWAP)
    *outs, g, dx1, sib, keep_late = branch_backward(
        me, dwv, x, dy, f, dz, vec, w1, w1_back, w2, w3, w_out, perm, bias_grads
    )
    got_late = swap(sib, CORE_SWAP)
    g, other_g, outs, got_late = hold(g, other_g, outs, got_late)
    part_g = split(own([keep_g], [got_g], other_g), mp_count)
    on_late = onward([keep_late], [got_late])
    g, part_g, on_late = hold(g, part_g, on_late)
    part_g = trade(part_g)
    other_late = swap(on_late, CHIP_SWAP)
    outs = exchange_far(*outs)

    du1, sib, keep1 = conv_backward(me, g, u, taps, z1, 4)
    got1 = swap(sib, CORE_SWAP)
    du1, part_g, other_late = hold(du1, part_g, other_late)
    part_late = split(own([keep_late], [got_late], other_late), mp_count)
    mixed = jnp.concatenate([spread_sum(part_g), part_late], axis=1)
    g, mixed = hold(g, mixed)
    mixed = trade(mixed)

    du0, sib, keep0 = conv_backward(me, g, u, taps, z1, 0)
    got0 = swap(sib, CORE_SWAP)
    du0, got0, got1, outs = hold(du0, got0, got1, outs)
    on_c = onward([keep0, keep1], [got0, got1])
    du0, on_c = hold(du0, on_c)
    other_c = swap(on_c, CHIP_SWAP)

    *ins, e0, e1, e2, e3 = input_backward(me, (du0, du1), x, dx1, vec, w_in, perm)
    ins, other_c = hold(ins, other_c)
    ins = exchange_far(*ins)
    block_output = from_pixels(me, outs).reshape(block_input.shape)
    ends = exchange((e0, e1, e2, e3))
    ins[1], other_c, mixed = hold(ins[1], other_c, mixed)
    rows = part_g.shape[1]
    part_late = mixed[:, rows:]
    sum_e, sum_r = widen(mixed)
    part_c = split(own([keep0, keep1], [got0, got1], other_c), mp_count)
    mixed = trade(jnp.concatenate([spread_sum(part_late), part_c], axis=1))
    mixed, ins = hold(mixed, ins)
    rows = part_late.shape[1]
    part_c = mixed[:, rows:]
    end = sum(e.astype(FULL) for e in ends).astype(LOW)
    end = jnp.broadcast_to(end[None], (mp_count,) + end.shape)
    full_c = trade(jnp.concatenate([spread_sum(part_c), end], axis=1))

    def back(values, blocks):
        return jnp.transpose(values.reshape(blocks, 16, values.shape[1]), (2, 0, 1))

    (
        g1, g2, g3, gconv, gout, gin, gb1, gb2, gb3, gob, gls1, gn2g, gn2b, grb, gls2, geb, ginb, gcb, gn1g, gn1b,
    ) = unpack_small(mixed, full_c)
    input_grad = from_pixels(me, ins).reshape(block_input.shape)
    return (
        block_output,
        input_grad,
        gn1g,
        gn1b,
        back(gin, 16),
        ginb,
        back(gconv, 15),
        gcb,
        back(g1, 2),
        gb1,
        back(g2, 4),
        gb2,
        back(g3, 8),
        gb3,
        back(gout, 8),
        gob,
        gls1,
        gn2g,
        gn2b,
        back(sum_e, 32),
        geb.T,
        sum_r.reshape(32, 16, WIDTH),
        grb,
        gls2,
    )


def solution(mesh):
    pixels = P(None, "dp", "mp")
    vector = P(None, "dp")
    matrix = P(None, None, "dp")
    params = (
        vector, vector, matrix, vector, matrix, vector, matrix, vector, matrix, vector, matrix, vector,
        matrix, vector, vector, vector, vector, matrix, vector, P(None, "dp", None), vector, vector,
    )
    return jax.shard_map(
        partial(per_device, mesh.shape["mp"]),
        mesh=mesh,
        in_specs=(pixels,) + params + (pixels,),
        out_specs=(pixels, pixels) + params,
        check_vma=False,
    )
```
